32 devices in a mesh: dp: 2 (over x), ctx: 4 (over y, core), expert: 4 (over z).
Axes of the slice: x: 2, y: 2, z: 4, core: 2. Of those that a mesh axis runs over, the one named last changes fastest.
Arguments:
- inputs: bfloat16 [2, 8, 512, 2048], P(None, ('dp', 'expert'), 'ctx'), may hold values from -6 to 6
- cotangent: bfloat16 [2, 8, 512, 2048], P(None, ('dp', 'expert'), 'ctx'), may hold values from -6 to 6
- lengths: int32 [2, 8, 3], P(None, ('dp', 'expert')), may hold values from 1 to 448, 512 in all within a row
- block_order: int32 [2, 8, 4], P(None, ('dp', 'expert')), may hold values from 0 to 3, each once within a row
- routes: int32 [2, 8, 512, 8], P(None, ('dp', 'expert'), 'ctx'), may hold values from 0 to 15, all different within a row; in each aligned block of 128 rows (0 to 127, 128 to 255, ..., all dimensions but the last counted through in order) at most 74 rows name the same one
- query_weight: bfloat16 [2048, 2048], P(('dp', 'ctx', 'expert')), may hold values from -0.125 to 0.125
- key_weight: bfloat16 [2048, 2048], P(('dp', 'ctx', 'expert')), may hold values from -0.125 to 0.125
- value_weight: bfloat16 [2048, 2048], P(('dp', 'ctx', 'expert')), may hold values from -0.125 to 0.125
- output_weight: bfloat16 [2048, 2048], P(('dp', 'ctx', 'expert')), may hold values from -1.5 to 1.5
- attention_gain: bfloat16 [2048], P(('dp', 'ctx', 'expert')), may hold values from 0.099609375 to 1.8984375
- mixture_gain: bfloat16 [2048], P(('dp', 'ctx', 'expert')), may hold values from 0.099609375 to 1.8984375
- query_key_gain: bfloat16 [256], P(('dp', 'ctx', 'expert')), may hold values from 0.099609375 to 1.8984375
- router: bfloat16 [2048, 16], P(('dp', 'ctx', 'expert')), may hold values from -0.0625 to 0.0625
- expert_gate: bfloat16 [16, 2048, 1024], P(('ctx', 'expert'), 'dp'), may hold values from -0.125 to 0.125
- expert_up: bfloat16 [16, 2048, 1024], P(('ctx', 'expert'), 'dp'), may hold values from -0.125 to 0.125
- expert_down: bfloat16 [16, 1024, 2048], P(('ctx', 'expert'), 'dp'), may hold values from -1 to 1
Outputs:
- output: bfloat16 [2, 8, 512, 2048], P(None, ('dp', 'expert'), 'ctx')
- input_grad: float32 [2, 8, 512, 2048], P(None, ('dp', 'expert'), 'ctx')
- query_grad: float32 [2048, 2048], P(('dp', 'ctx', 'expert'))
- key_grad: float32 [2048, 2048], P(('dp', 'ctx', 'expert'))
- value_grad: float32 [2048, 2048], P(('dp', 'ctx', 'expert'))
- output_grad: float32 [2048, 2048], P(('dp', 'ctx', 'expert'))
- attention_gain_grad: float32 [2048], P(('dp', 'ctx', 'expert'))
- mixture_gain_grad: float32 [2048], P(('dp', 'ctx', 'expert'))
- query_key_grad: float32 [256], P(('dp', 'ctx', 'expert'))
- router_grad: float32 [2048, 16], P(('dp', 'ctx', 'expert'))
- gate_grad: float32 [16, 2048, 1024], P(('ctx', 'expert'), 'dp')
- up_grad: float32 [16, 2048, 1024], P(('ctx', 'expert'), 'dp')
- down_grad: float32 [16, 1024, 2048], P(('ctx', 'expert'), 'dp')
The draws below stay inside these ranges and needn't reach their ends.
Inputs may be any that keep to these rules, and one draw needn't show every extreme that they name: The 3 lengths of a group in one micro-batch sum to 512; the longest is 448. `block_order`: in each micro-batch and group a permutation of the 4 blocks. `routes`: each token names 8 different experts; among the tokens of one device in one micro-batch no expert is named more than 74 times, a bound that some block reaches.
All inputs are finite; a program needn't handle non-finite values.
Results may differ from the reference program's by a relative error of at most 0.02.
Values may be sent and summed in bfloat16 or wider, within the bound.
No kernel may reach another device: no remote copies, remote signals or barrier semaphores. Data moves between devices by JAX's collectives and lax.ppermute only.
A program may use at most 320 MiB of HBM per device.

```python
import math
import jax
import jax.numpy as jnp
import numpy as np
from jax import lax

D = 2048
HEADS = 16
DH = 128
FF = 1024
TOP = 8
BLOCK = 128
NSEQ = 3
MICRO = 2
TOK_DEV = 128
HD = 2048
E = 16
GROUPS = 8
GROUP_TOK = 512
NBLK = 4
MOST = 448
CAP = 74
N_CTX = 4


def shard_levels(rng, extent, cuts, smallest, top_value):
    gain = 1.0
    for axis_at, parts in cuts:
        heights = jax.random.uniform(jax.random.fold_in(jax.random.fold_in(rng, 6), axis_at), (parts,), jnp.float32, smallest / len(cuts), top_value / len(cuts))
        gain = gain * jnp.repeat(jnp.exp(heights), extent[axis_at] // parts).reshape((-1,) + (1,) * (len(extent) - 1 - axis_at))
    return gain


def length_profile(amount, total, reach, lean):
    loads = [(1 << 20) // math.isqrt(rank ** lean) + 1 for rank in range(2, amount + 1)]
    surplus, given = total - reach - (amount - 1), [1] * (amount - 1)
    while surplus > 0:
        free = [i for i in range(amount - 1) if given[i] < reach]
        mass, budget = sum([loads[i] for i in free]), surplus
        for i in free:
            more = min(reach - given[i], max(1, budget * loads[i] // mass), surplus)
            given[i] = given[i] + more
            surplus = surplus - more
    return np.array([reach] + given)


def ragged_sizes(rng, number_of, total, reach, skew):
    if number_of == 2:
        one = jax.random.randint(rng, (), max(1, total - reach), min(reach, total - 1) + 1)
        return jnp.stack([one, total - one])
    sizes = jnp.asarray(length_profile(number_of, total, reach, skew), jnp.int32)
    twos = (number_of - 1) // 2
    giver, receiver = sizes[1:1 + 2 * twos:2], sizes[2:2 + 2 * twos:2]
    margin = jnp.minimum(giver - 1, reach - receiver)
    moved = jax.random.randint(jax.random.fold_in(rng, 1), (twos,), 0, 1 << 20) % (margin + 1)
    sizes = sizes.at[1:1 + 2 * twos:2].set(giver - moved).at[2:2 + 2 * twos:2].set(receiver + moved)
    return sizes[jax.random.permutation(jax.random.fold_in(rng, 2), number_of)]


def deal_out(stream_key, own, number, rows, amount, top, limit, skew):
    order = jax.random.permutation(stream_key, amount)
    packed, common = shares(amount, rows * top, limit, skew, True), shares(amount, rows * top, limit, skew, False)
    places = jnp.arange(amount)

    def named(sizes, rotation):
        used = int((sizes > 0).sum())
        fixed = max(1, used // 4)
        passed = fixed + (places - fixed + rotation * (used - fixed)) % max(1, amount - fixed)
        return jnp.zeros((amount,), jnp.int32).at[order[jnp.where(places < fixed, places, passed)]].set(jnp.asarray(sizes, jnp.int32))

    sizes = jnp.where(number % 4 == 0, named(packed, number // 4), named(common, number - number // 4 - 1))
    mixed = jax.random.permutation(jax.random.fold_in(own, 3), amount)
    giver, receiver = mixed[0:amount // 2 * 2:2], mixed[1:amount // 2 * 2:2]
    slack = jnp.minimum(sizes[giver] - 1, limit - sizes[receiver]) // 2
    slack = jnp.where((giver == order[0]) | (receiver == order[0]) | (sizes[receiver] == 0), 0, jnp.maximum(slack, 0))
    passed = jax.random.randint(jax.random.fold_in(own, 4), (amount // 2,), 0, 1 << 20) % (slack + 1)
    sizes = sizes.at[giver].add(-passed).at[receiver].add(passed)
    labels = jnp.searchsorted(jnp.cumsum(sizes), jnp.arange(rows * top), side="right").astype(jnp.int32)
    table = labels.reshape(top, rows).T
    table = table[jax.random.permutation(jax.random.fold_in(own, 1), rows)]
    rotation = jax.random.randint(jax.random.fold_in(own, 2), (rows, 1), 0, top)
    return jnp.take_along_axis(table, (jnp.arange(top)[None, :] + rotation) % top, axis=1)


def shares(number_of, total, most, skew, full):
    weights = [(1 << 20) // math.isqrt(standing ** skew) + 1 for standing in range(1, number_of + 1)]
    largest = most if full else min(most, max(-(-total // number_of), total * weights[0] // sum(weights)))
    least = 1 if total - largest >= number_of - 1 else 0
    holding, rest = [largest] + [least] * (number_of - 1), total - largest - least * (number_of - 1)
    while rest > 0:
        free = [i for i in range(1, number_of) if holding[i] < largest] or [i for i in range(1, number_of) if holding[i] < most]
        whole, left = sum([weights[i] for i in free]), rest
        for i in free:
            more = min(most - holding[i], max(1, left * weights[i] // whole), rest)
            holding[i] = holding[i] + more
            rest = rest - more
    return np.array(holding)


def gaussian(stream_key, extent, width, limit, split=(), kind=jnp.bfloat16):
    drawn = jax.random.normal(stream_key, extent, jnp.float32) * width
    if len(split) > 0:
        drawn = shard_levels(stream_key, extent, split, -0.22, 0.18) * drawn
    return jnp.clip(drawn, min=-limit, max=limit).astype(kind)


def setup_inputs(seed: int = 0) -> dict:
    seeds = jax.random.split(jax.random.key(seed), 17)
    inputs = gaussian(seeds[0], (MICRO, GROUPS, GROUP_TOK, D), 1.0, 6.0, ((1, 8), (2, 4)))
    cotangent = gaussian(seeds[1], (MICRO, GROUPS, GROUP_TOK, D), 1.0, 6.0, ((1, 8), (2, 4)))
    lengths = jax.vmap(lambda own: ragged_sizes(own, NSEQ, GROUP_TOK, MOST, 2))(jax.random.split(seeds[2], MICRO * GROUPS)).reshape((MICRO, GROUPS, NSEQ)).astype(jnp.int32)
    block_order = jax.vmap(lambda own: jax.random.permutation(own, NBLK))(jax.random.split(seeds[3], MICRO * GROUPS)).reshape((MICRO, GROUPS, NBLK)).astype(jnp.int32)
    routes_keys = jax.random.split(jax.random.fold_in(seeds[4], 1), MICRO * GROUPS * GROUP_TOK // TOK_DEV)
    routes_turns = jax.random.permutation(jax.random.fold_in(seeds[4], 3), MICRO * GROUPS * GROUP_TOK // TOK_DEV)
    routes = jax.vmap(lambda own, number: deal_out(jax.random.fold_in(seeds[4], 2), own, number, TOK_DEV, E, TOP, CAP, 1))(routes_keys, routes_turns).reshape((MICRO, GROUPS, GROUP_TOK, TOP))
    query_weight = gaussian(seeds[5], (D, HD), D ** -0.5, 0.125, ((0, 32),))
    key_weight = gaussian(seeds[6], (D, HD), D ** -0.5, 0.125, ((0, 32),))
    value_weight = gaussian(seeds[7], (D, HD), D ** -0.5, 0.125, ((0, 32),))
    output_weight = gaussian(seeds[8], (HD, D), (max(HD * 4 // GROUP_TOK, 1)) ** -0.5, 1.5, ((0, 32),))
    attention_gain = jnp.clip(1.0 + 0.18 * jax.random.normal(seeds[9], (D,), jnp.float32), 0.099609375, 1.8984375).astype(jnp.bfloat16)
    mixture_gain = jnp.clip(1.0 + 0.18 * jax.random.normal(seeds[10], (D,), jnp.float32), 0.099609375, 1.8984375).astype(jnp.bfloat16)
    query_key_gain = jnp.clip(1.0 + 0.18 * jax.random.normal(seeds[11], (2 * DH,), jnp.float32), 0.099609375, 1.8984375).astype(jnp.bfloat16)
    router = gaussian(seeds[12], (D, E), (4 * D) ** -0.5, 0.0625, ((0, 32),))
    expert_gate = gaussian(seeds[13], (E, D, FF), D ** -0.5, 0.125, ((0, 16), (1, 2)))
    expert_up = gaussian(seeds[14], (E, D, FF), D ** -0.5, 0.125, ((0, 16), (1, 2)))
    expert_down = gaussian(seeds[15], (E, FF, D), (max(FF // 32, 1)) ** -0.5, 1.0, ((0, 16), (1, 2)))
    return {"inputs": inputs, "cotangent": cotangent, "lengths": lengths, "block_order": block_order, "routes": routes, "query_weight": query_weight, "key_weight": key_weight, "value_weight": value_weight, "output_weight": output_weight, "attention_gain": attention_gain, "mixture_gain": mixture_gain, "query_key_gain": query_key_gain, "router": router, "expert_gate": expert_gate, "expert_up": expert_up, "expert_down": expert_down}


@jax.custom_vjp
def low(v):
    return lax.optimization_barrier(v.astype(jnp.bfloat16)).astype(jnp.float32)

@jax.custom_vjp
def low_back(v):
    return v

def low_keep(v):
    return (low(v), None)

def low_pass(kept, grad):
    return (grad,)

def back_keep(v):
    return (v, None)

def back_low(kept, grad):
    return (low(grad),)
low.defvjp(low_keep, low_pass)
low_back.defvjp(back_keep, back_low)
EPSILON = 1e-06
NEGATIVE = -1e+30
THETA_BASE = 50000.0
HIGHEST = lax.Precision.HIGHEST

def product(left_side, right_side):
    return jnp.dot(left_side, right_side, precision=HIGHEST)

def places(lengths, block_order, group_tok, block_size):
    stored = jnp.arange(group_tok, dtype=jnp.int32)
    blocks = jnp.arange(block_order.shape[0], dtype=jnp.int32)
    holder = (stored // block_size)[:, None] == blocks[None, :]
    logical = lax.optimization_barrier(jnp.sum(jnp.where(holder, block_order[None, :], 0), axis=1)).astype(jnp.int32) * block_size + stored % block_size
    seq_ends = jnp.cumsum(lengths).astype(jnp.int32)
    segment = lax.optimization_barrier(jnp.sum((logical[:, None] >= seq_ends[None, :]).astype(jnp.int32), axis=1)).astype(jnp.int32)
    starts = seq_ends - lengths.astype(jnp.int32)
    member = segment[:, None] == jnp.arange(lengths.shape[0], dtype=jnp.int32)[None, :]
    seq_first = lax.optimization_barrier(jnp.sum(jnp.where(member, starts[None, :], 0), axis=1)).astype(jnp.int32)
    return (segment, (logical - seq_first).astype(jnp.float32))

def rotary_tables(positions, half_size):
    frequency = THETA_BASE ** (-(jnp.arange(half_size, dtype=jnp.float32) / half_size))
    angles = positions[:, None] * frequency[None, :]
    return (jnp.cos(angles), jnp.sin(angles))

def rotate(values, cosine, sine_table):
    half_size = values.shape[-1] // 2
    first_half = values[..., :half_size]
    second = values[..., half_size:]
    cosine_b = cosine[:, None, :]
    sine_b = sine_table[:, None, :]
    return jnp.concatenate([first_half * cosine_b - second * sine_b, second * cosine_b + first_half * sine_b], axis=-1)

def head_norm(values, scaling):
    return values * lax.rsqrt(lax.optimization_barrier(jnp.mean(values * values, axis=-1, keepdims=True)) + EPSILON) * scaling

def attend(stream, segment, positions, query_weight, key_weight, value_weight, output_weight, attention_gain, query_gain, key_gain):
    tokens_here = stream.shape[0]
    normed = low(stream * lax.rsqrt(lax.optimization_barrier(jnp.mean(stream * stream, axis=-1, keepdims=True)) + EPSILON) * attention_gain)
    query_rows = low_back(product(normed, query_weight)).reshape(tokens_here, HEADS, DH)
    key_rows = low_back(product(normed, key_weight)).reshape(tokens_here, HEADS, DH)
    valued = low_back(low(product(normed, value_weight))).reshape(tokens_here, HEADS, DH)
    cosine, sine_table = rotary_tables(positions, DH // 2)
    query_rot = low_back(low(rotate(head_norm(query_rows, query_gain), cosine, sine_table)))
    key_rot = low_back(low(rotate(head_norm(key_rows, key_gain), cosine, sine_table)))
    scores = low_back(jnp.einsum('qhd,khd->hqk', query_rot, key_rot, precision=HIGHEST) * DH ** (-0.5))
    scores = jnp.where((segment[:, None] == segment[None, :])[None], scores, NEGATIVE)
    row_peak = lax.optimization_barrier(jnp.max(scores, axis=-1, keepdims=True))
    powers = jnp.exp(scores - row_peak)
    attn_probs = low(powers / lax.optimization_barrier(jnp.sum(powers, axis=-1, keepdims=True)))
    mixed = jnp.einsum('hqk,khd->qhd', attn_probs, valued, precision=HIGHEST)
    attended = low_back(low(mixed)).reshape(tokens_here, HEADS * DH)
    return stream + low_back(product(attended, output_weight))

def expert_rows(pieces):
    rows_in, gate_weight, up_weight, down_weight = pieces
    gate_pre = low_back(product(rows_in, gate_weight))
    up_pre = low_back(product(rows_in, up_weight))
    hidden = low(gate_pre * jax.nn.sigmoid(gate_pre) * up_pre)
    return low_back(low(product(hidden, down_weight)))

def dispatch_tables(routes_now):
    sources = GROUPS * N_CTX
    entries = TOK_DEV * TOP
    flat_routes = routes_now.reshape(sources, entries)
    onehot = (flat_routes[:, :, None] == jnp.arange(E, dtype=jnp.int32)[None, None, :]).astype(jnp.int32)
    slot_index = lax.optimization_barrier(jnp.sum((jnp.cumsum(onehot, axis=1).astype(jnp.int32) - 1) * onehot, axis=2)).astype(jnp.int32)
    source_id = jnp.arange(sources, dtype=jnp.int32)[:, None]
    token_id = source_id * TOK_DEV + jnp.arange(entries, dtype=jnp.int32)[None, :] // TOP
    column = source_id * CAP + slot_index
    table = jnp.full((E, sources * CAP), sources * TOK_DEV, jnp.int32).at[flat_routes, column].set(token_id)
    picks = (flat_routes * (sources * CAP) + column).reshape(sources * TOK_DEV, TOP)
    return (table, picks)

def forward(params, inputs, segments, positions, route_hot, tables, picks):
    query_weight, key_weight, value_weight, output_weight, attention_gain, mixture_gain, query_key_gain, router, expert_gate, expert_up, expert_down = params
    query_gain = query_key_gain[:DH]
    key_gain = query_key_gain[DH:]

    def attend_group(pieces):
        return attend(pieces[0], pieces[1], pieces[2], query_weight, key_weight, value_weight, output_weight, attention_gain, query_gain, key_gain)
    results = []
    for micro_step in range(MICRO):
        after = lax.map(jax.checkpoint(attend_group), (inputs[micro_step], segments[micro_step], positions[micro_step]))
        residual = after.reshape(GROUPS * GROUP_TOK, D)
        normed = low(residual * lax.rsqrt(lax.optimization_barrier(jnp.mean(residual * residual, axis=-1, keepdims=True)) + EPSILON) * mixture_gain)
        logits = low_back(product(normed, router))
        chosen = lax.optimization_barrier(jnp.sum(route_hot[micro_step] * logits[:, None, :], axis=2))
        row_peak = lax.optimization_barrier(jnp.max(chosen, axis=1, keepdims=True))
        powers = jnp.exp(chosen - row_peak)
        gate_values = powers / lax.optimization_barrier(jnp.sum(powers, axis=1, keepdims=True))
        padded = jnp.concatenate([normed, jnp.zeros((1, D), jnp.float32)], axis=0)
        expert_in = low_back(padded[tables[micro_step]])
        expert_out = lax.map(jax.checkpoint(expert_rows), (expert_in, expert_gate, expert_up, expert_down))
        routed = expert_out.reshape(-1, D)[picks[micro_step]]
        mixed = residual + lax.optimization_barrier(jnp.sum(gate_values[:, :, None] * routed, axis=1))
        results.append(mixed.reshape(GROUPS, GROUP_TOK, D))
    return jnp.stack(results)

def place_pair(lengths_now, order_now):
    return places(lengths_now, order_now, GROUP_TOK, BLOCK)

def reference(inputs, cotangent, lengths, block_order, routes, query_weight, key_weight, value_weight, output_weight, attention_gain, mixture_gain, query_key_gain, router, expert_gate, expert_up, expert_down):
    segments, positions = jax.vmap(jax.vmap(place_pair))(lengths, block_order)
    tables, picks = jax.vmap(dispatch_tables)(routes)
    route_hot = (routes.reshape(MICRO, GROUPS * GROUP_TOK, TOP)[..., None] == jnp.arange(E, dtype=jnp.int32)).astype(jnp.float32)
    params = (query_weight.astype(jnp.float32), key_weight.astype(jnp.float32), value_weight.astype(jnp.float32), output_weight.astype(jnp.float32), attention_gain.astype(jnp.float32), mixture_gain.astype(jnp.float32), query_key_gain.astype(jnp.float32), router.astype(jnp.float32), expert_gate.astype(jnp.float32), expert_up.astype(jnp.float32), expert_down.astype(jnp.float32))

    def closed(params_now, inputs_now):
        return forward(params_now, inputs_now, segments, positions, route_hot, tables, picks)
    output, pullback = jax.vjp(closed, params, inputs.astype(jnp.float32))
    param_grads, input_grad = pullback(cotangent.astype(jnp.float32))
    return (output.astype(jnp.bfloat16), input_grad, param_grads[0], param_grads[1], param_grads[2], param_grads[3], param_grads[4], param_grads[5], param_grads[6], param_grads[7], param_grads[8], param_grads[9], param_grads[10])
```

```python
import jax
import jax.numpy as jnp
from jax import lax
from jax.sharding import PartitionSpec as P

HEADS = 16
DH = 128
BLOCK = 128
HALVES = 2
SMALL = 128

EPSILON = 1e-06
NEGATIVE = -1e30
THETA_BASE = 50000.0
F32 = jnp.float32
BF16 = jnp.bfloat16


def matmul(left_side, right_side):
    return jnp.dot(left_side, right_side, preferred_element_type=F32)


def matmul_t(left_side, right_side):
    return lax.dot_general(
        left_side, right_side, (((1,), (1,)), ((), ())), preferred_element_type=F32
    )


def inner_rows(left_side, right_side):
    return lax.dot_general(
        left_side, right_side, (((0,), (0,)), ((), ())), preferred_element_type=F32
    )


def swap(value, axis, bit):
    return lax.ppermute(value, axis, [(i, i ^ bit) for i in range(4)])


MIDDLE = [(1, 2), (2, 1)]
OUTWARD = [(1, 0), (2, 3)]
INWARD = [(0, 1), (3, 2)]


def gather_ctx(own):
    across = swap(own, "ctx", 2)
    beside = swap(own, "ctx", 1)
    corner = swap(across, "ctx", 1)
    return [own, beside, across, corner]


def scatter_ctx(slots):
    far = slots[2].astype(F32) + swap(slots[3], "ctx", 1).astype(F32)
    near = slots[0].astype(F32) + swap(slots[1], "ctx", 1).astype(F32)
    return near + swap(far.astype(BF16), "ctx", 2).astype(F32)


def gather_line(own):
    pair = swap(own, "expert", 1)
    third_mid = lax.ppermute(own, "expert", MIDDLE)
    second_mid = lax.ppermute(pair, "expert", MIDDLE)
    second_end = lax.ppermute(third_mid, "expert", OUTWARD)
    third_end = lax.ppermute(second_mid, "expert", OUTWARD)
    place = lax.axis_index("expert")
    middle = (place == 1) | (place == 2)
    return [
        own,
        pair,
        jnp.where(middle, second_mid, second_end),
        jnp.where(middle, third_mid, third_end),
    ]


def scatter_line(slots):
    three = lax.ppermute(slots[3].astype(BF16), "expert", INWARD)
    second = slots[2] + three.astype(F32)
    second_low = second.astype(BF16)
    over = lax.ppermute(second_low, "expert", MIDDLE)
    inward = lax.ppermute(second_low, "expert", INWARD)
    first = slots[1] + over.astype(F32)
    third = slots[3] + inward.astype(F32)
    home = lax.ppermute(third.astype(BF16), "expert", MIDDLE)
    pair = swap(first.astype(BF16), "expert", 1)
    return slots[0] + pair.astype(F32) + home.astype(F32)


def gather_both(own):
    line = gather_line(own)
    here = jnp.stack(line + [swap(piece, "ctx", 2) for piece in line])
    return here, swap(here, "ctx", 1)


def scatter_both(here, there):
    received = [swap(there[s], "ctx", 1) for s in range(8)]
    chip = [here[s].astype(F32) + received[s].astype(F32) for s in range(8)]
    across = [swap(chip[4 + s].astype(BF16), "ctx", 2) for s in range(4)]
    return scatter_line([chip[s] + across[s].astype(F32) for s in range(4)])


def places(index, lengths, block_order):
    blocks = jnp.arange(block_order.shape[0], dtype=jnp.int32)
    holder = (index // BLOCK)[:, None] == blocks[None, :]
    logical = (
        jnp.sum(jnp.where(holder, block_order[None, :], 0), axis=1) * BLOCK + index % BLOCK
    )
    seq_ends = jnp.cumsum(lengths)
    segment = jnp.sum((logical[:, None] >= seq_ends[None, :]).astype(jnp.int32), axis=1)
    starts = seq_ends - lengths
    member = segment[:, None] == jnp.arange(lengths.shape[0], dtype=jnp.int32)[None, :]
    seq_first = jnp.sum(jnp.where(member, starts[None, :], 0), axis=1)
    return (segment, (logical - seq_first).astype(F32))


def rotary_tables(positions, half_size):
    frequency = THETA_BASE ** (-(jnp.arange(half_size, dtype=F32) / half_size))
    angles = positions[:, None] * frequency[None, :]
    return (jnp.cos(angles), jnp.sin(angles))


def rotate(values, cosine, sine_table):
    half_size = values.shape[-1] // 2
    first_half = values[..., :half_size]
    second = values[..., half_size:]
    cosine_b = cosine[:, None, :]
    sine_b = sine_table[:, None, :]
    return jnp.concatenate(
        [first_half * cosine_b - second * sine_b, second * cosine_b + first_half * sine_b], axis=-1
    )


def unrotate(values, cosine, sine_table):
    half_size = values.shape[-1] // 2
    first_half = values[..., :half_size]
    second = values[..., half_size:]
    cosine_b = cosine[:, None, :]
    sine_b = sine_table[:, None, :]
    return jnp.concatenate(
        [first_half * cosine_b + second * sine_b, second * cosine_b - first_half * sine_b], axis=-1
    )


def norm_back(upstream, unit_rows, scaling, gain_vector):
    weighted = upstream * gain_vector
    return scaling * (weighted - unit_rows * jnp.mean(weighted * unit_rows, axis=-1, keepdims=True))


def row_scale(rows):
    return lax.rsqrt(jnp.mean(rows * rows, axis=-1, keepdims=True) + EPSILON)


def gather_weights(query_weight, key_weight, value_weight, output_weight, attention_gain, mixture_gain, query_key_gain, router):
    rows, width = query_weight.shape
    ctx_size = lax.axis_size("ctx")
    share = width // (HALVES * ctx_size)
    stacked = jnp.stack([query_weight, key_weight, value_weight], axis=1)
    stacked = stacked.reshape(rows, 3, HALVES, ctx_size, share).transpose(3, 0, 1, 2, 4)
    stacked = stacked.reshape(ctx_size, rows, 3 * HALVES * share)
    few = query_key_gain.shape[0]
    small = jnp.concatenate(
        [
            attention_gain[:, None],
            mixture_gain[:, None],
            jnp.pad(query_key_gain, (0, rows - few))[:, None],
            router,
        ],
        axis=1,
    )
    small = jnp.pad(small, ((0, 0), (0, SMALL - small.shape[1])))
    payload = jnp.concatenate(
        [stacked, jnp.broadcast_to(small[None], (ctx_size, rows, SMALL))], axis=2
    )
    payload = lax.all_to_all(payload, "ctx", split_axis=0, concat_axis=0, tiled=True)
    whole = lax.all_gather(payload, ("dp", "expert"), axis=0, tiled=False)
    dp_size, line = lax.axis_size("dp"), lax.axis_size("expert")
    whole = whole.reshape(dp_size, line, ctx_size, rows, payload.shape[2])
    whole = whole.transpose(0, 2, 1, 3, 4).reshape(-1, payload.shape[2])
    projections = whole[:, : 3 * HALVES * share]
    small = whole[:, 3 * HALVES * share :].astype(F32)
    pair = small[:, 2].reshape(-1, rows)[:, :few].reshape(-1)
    router_all = whole[:, 3 * HALVES * share + 3 : 3 * HALVES * share + 3 + router.shape[1]]
    if whole_heads(dp_size, rows * line, share):
        out_rows = lax.all_gather(output_weight, ("dp", "expert"), axis=0, tiled=True)
    else:
        out_rows = lax.all_gather(output_weight, ("dp", "ctx", "expert"), axis=0, tiled=True)
        out_rows = out_rows.reshape(HALVES, ctx_size, share, -1)
        out_rows = lax.dynamic_index_in_dim(out_rows, lax.axis_index("ctx"), 1, keepdims=False)
        out_rows = out_rows.reshape(HALVES * share, -1)
    return projections, out_rows, small[:, 0], small[:, 1], pair[:DH], pair[DH:], router_all


def whole_heads(dp_size, line_rows, share):
    return dp_size == HALVES and line_rows == share


def scatter_grads(projections, small_columns, out_rows, rows, few):
    ctx_size, dp_size, line = lax.axis_size("ctx"), lax.axis_size("dp"), lax.axis_size("expert")
    width = projections.shape[0]
    share = out_rows.shape[0] // HALVES
    small = jnp.pad(small_columns, ((0, 0), (0, SMALL - small_columns.shape[1])))
    payload = jnp.concatenate([projections, small], axis=1).astype(BF16)
    columns = payload.shape[1]
    payload = payload.reshape(dp_size, ctx_size, line, rows, columns).transpose(0, 2, 1, 3, 4)
    payload = payload.reshape(dp_size * line * ctx_size, rows, columns)
    payload = lax.psum_scatter(payload, ("dp", "expert"), scatter_dimension=0, tiled=True)
    payload = lax.all_to_all(payload, "ctx", split_axis=0, concat_axis=0, tiled=True)
    parts = payload[:, :, : 3 * HALVES * share].reshape(ctx_size, rows, 3, HALVES, share)
    parts = parts.transpose(2, 1, 3, 0, 4).reshape(3, rows, width).astype(F32)
    small = jnp.sum(payload[:, :, 3 * HALVES * share :].astype(F32), axis=0)
    if whole_heads(dp_size, rows * line, share):
        out_part = lax.psum_scatter(
            out_rows.astype(BF16), ("dp", "expert"), scatter_dimension=0, tiled=True
        )
    else:
        place = lax.axis_index("ctx")
        spread = jnp.zeros((HALVES, ctx_size, share, width), BF16)
        spread = lax.dynamic_update_slice_in_dim(
            spread, out_rows.astype(BF16).reshape(HALVES, 1, share, width), place, 1
        )
        out_part = lax.psum_scatter(
            spread.reshape(-1, width), ("dp", "ctx", "expert"), scatter_dimension=0, tiled=True
        )
    return parts[0], parts[1], parts[2], out_part.astype(F32), small[:, 0], small[:, 1], small[:few, 2], small[:, 3:]


def attention_forward(stream, weights, tables):
    projections, _, attention_gain, _, query_gain, key_gain, _ = weights
    segment, cosine, sine_table = tables
    tokens = stream.shape[0]
    heads = projections.shape[1] // (3 * DH)
    unit = stream * row_scale(stream)
    normed = (unit * attention_gain).astype(BF16)
    joined = matmul(normed, projections).reshape(tokens, 3, heads, DH)
    query_rows, key_rows = joined[:, 0], joined[:, 1]
    valued = joined[:, 2].astype(BF16)
    query_scale = row_scale(query_rows)
    key_scale = row_scale(key_rows)
    query_unit = query_rows * query_scale
    key_unit = key_rows * key_scale
    query_rot = rotate(query_unit * query_gain, cosine, sine_table).astype(BF16)
    key_rot = rotate(key_unit * key_gain, cosine, sine_table).astype(BF16)
    scores = jnp.einsum("qhd,khd->hqk", query_rot, key_rot, preferred_element_type=F32) * DH ** (-0.5)
    scores = jnp.where((segment[:, None] == segment[None, :])[None], scores, NEGATIVE)
    powers = jnp.exp(scores - jnp.max(scores, axis=-1, keepdims=True))
    probs = powers / jnp.sum(powers, axis=-1, keepdims=True)
    attended = jnp.einsum("hqk,khd->qhd", probs.astype(BF16), valued, preferred_element_type=F32)
    attended = attended.reshape(tokens, heads * DH).astype(BF16)
    return attended, (normed, unit, query_scale, query_unit, key_scale, key_unit, query_rot, key_rot, valued, probs)


def attention_backward(branch_grad, saved, weights, tables):
    projections, out_rows, _, _, query_gain, key_gain, _ = weights
    _, cosine, sine_table = tables
    normed, unit, query_scale, query_unit, key_scale, key_unit, query_rot, key_rot, valued, probs = saved
    tokens, heads = query_rot.shape[0], query_rot.shape[1]
    attended_grad = matmul_t(branch_grad, out_rows).astype(BF16).reshape(tokens, heads, DH)
    prob_grad = jnp.einsum("qhd,khd->hqk", attended_grad, valued, preferred_element_type=F32)
    score_grad = (
        probs * (prob_grad - jnp.sum(probs * prob_grad, axis=-1, keepdims=True))
    ).astype(BF16)
    query_rot_grad = jnp.einsum("hqk,khd->qhd", score_grad, key_rot, preferred_element_type=F32)
    key_rot_grad = jnp.einsum("hqk,qhd->khd", score_grad, query_rot, preferred_element_type=F32)
    value_grad = jnp.einsum(
        "hqk,qhd->khd", probs.astype(BF16), attended_grad, preferred_element_type=F32
    ).astype(BF16)
    query_rot_grad = (query_rot_grad * DH ** (-0.5)).astype(BF16).astype(F32)
    key_rot_grad = (key_rot_grad * DH ** (-0.5)).astype(BF16).astype(F32)
    query_norm_grad = unrotate(query_rot_grad, cosine, sine_table)
    key_norm_grad = unrotate(key_rot_grad, cosine, sine_table)
    gain_pair = jnp.concatenate(
        [
            jnp.sum(query_norm_grad * query_unit, axis=(0, 1)),
            jnp.sum(key_norm_grad * key_unit, axis=(0, 1)),
        ]
    )
    query_grad = norm_back(query_norm_grad, query_unit, query_scale, query_gain)
    key_grad = norm_back(key_norm_grad, key_unit, key_scale, key_gain)
    joined = jnp.concatenate(
        [
            query_grad.astype(BF16).reshape(tokens, -1),
            key_grad.astype(BF16).reshape(tokens, -1),
            value_grad.reshape(tokens, -1),
        ],
        axis=1,
    )
    normed_grad = matmul_t(joined, projections)
    attention_gain_grad = jnp.sum(normed_grad * unit, axis=0)
    return joined, normed_grad.astype(BF16), attention_gain_grad, gain_pair


def chosen_gates(normed, router, chosen):
    logits = jnp.where(chosen, matmul(normed, router), NEGATIVE)
    powers = jnp.where(chosen, jnp.exp(logits - jnp.max(logits, axis=1, keepdims=True)), 0.0)
    return powers / jnp.sum(powers, axis=1, keepdims=True)


def pick_rows(onehot, blocks):
    return jnp.einsum("bsj,bjd->bsd", onehot, blocks, preferred_element_type=F32).astype(BF16)


def place_rows(onehot, rows):
    return jnp.einsum("bsj,bsd->bjd", onehot, rows, preferred_element_type=F32).astype(BF16)


def expert_pass(normed, upstream, chosen, router, gate_full, up_full, down_full, expert, capacity):
    blocks, tokens, width = normed.shape
    gates = chosen_gates(
        normed.reshape(-1, width), router, chosen.reshape(blocks * tokens, -1)
    ).reshape(blocks, tokens, -1)
    mine = jnp.arange(gates.shape[2], dtype=jnp.int32) == expert
    gate_here = jnp.sum(jnp.where(mine, gates, 0.0), axis=2)
    here = jnp.any(chosen & mine, axis=2)
    slot = jnp.cumsum(here.astype(jnp.int32), axis=1) - 1
    onehot = (
        slot[:, None, :] == jnp.arange(capacity, dtype=jnp.int32)[None, :, None]
    ) & here[:, None, :]
    gate_rows = jnp.sum(jnp.where(onehot, gate_here[:, None, :], 0.0), axis=2)
    gate_rows = gate_rows.reshape(-1, 1)
    onehot = onehot.astype(BF16)
    rows_in = pick_rows(onehot, normed).reshape(-1, width)
    rows_up = pick_rows(onehot, upstream).reshape(-1, width)
    gate_pre = matmul(rows_in, gate_full)
    up_pre = matmul(rows_in, up_full)
    sigma = jax.nn.sigmoid(gate_pre)
    hidden = (gate_pre * sigma * up_pre).astype(BF16)
    produced = matmul(hidden, down_full).astype(BF16).astype(F32)
    gate_grad = jnp.sum(produced * rows_up.astype(F32), axis=1).reshape(blocks, capacity)
    gate_grad = jnp.einsum("bsj,bs->bj", onehot.astype(F32), gate_grad, precision=lax.Precision.HIGHEST)
    shared = place_rows(onehot, (gate_rows * produced).astype(BF16).reshape(blocks, capacity, width))
    out_grad = (gate_rows * rows_up.astype(F32)).astype(BF16)
    hidden_grad = matmul_t(out_grad, down_full)
    gate_pre_grad = (hidden_grad * up_pre * sigma * (1.0 + gate_pre * (1.0 - sigma))).astype(BF16)
    up_pre_grad = (hidden_grad * gate_pre * sigma).astype(BF16)
    rows_grad = (matmul_t(gate_pre_grad, gate_full) + matmul_t(up_pre_grad, up_full)).astype(BF16)
    back = place_rows(onehot, rows_grad.reshape(blocks, capacity, width))
    return shared, back, gate_grad, (rows_in, hidden, out_grad, gate_pre_grad, up_pre_grad)


def body(
    inputs,
    cotangent,
    lengths,
    block_order,
    routes,
    query_weight,
    key_weight,
    value_weight,
    output_weight,
    attention_gain,
    mixture_gain,
    query_key_gain,
    router,
    expert_gate,
    expert_up,
    expert_down,
):
    micro_count, _, tokens, width = inputs.shape
    top = routes.shape[3]
    expert_count = router.shape[1]
    most = tokens * top * 9 // (8 * expert_count) + 2
    capacity = -(-most // 16) * 16
    place, line = lax.axis_index("ctx"), lax.axis_index("expert")
    line_size = lax.axis_size("expert")
    ctx_size = lax.axis_size("ctx")
    few = query_key_gain.shape[0]
    weights = gather_weights(
        query_weight, key_weight, value_weight, output_weight, attention_gain, mixture_gain, query_key_gain, router
    )
    projections, out_rows, _, mixture_all, _, _, router_all = weights
    gate_full = lax.all_gather(expert_gate[0], "dp", axis=0, tiled=True)
    up_full = lax.all_gather(expert_up[0], "dp", axis=0, tiled=True)
    down_full = lax.all_gather(expert_down[0], "dp", axis=0, tiled=True)

    routes_all = lax.all_gather(routes[:, 0], ("ctx", "expert"), axis=0, tiled=False)
    routes_all = routes_all.reshape(ctx_size, line_size, micro_count, tokens, top)
    ctx_order = [place ^ s for s in (0, 2, 1, 3)]
    line_order = [line ^ s for s in range(4)]
    ordered = jnp.stack([routes_all[a, b] for a in ctx_order for b in line_order])
    chosen_all = jnp.any(
        ordered[..., None] == jnp.arange(expert_count, dtype=jnp.int32), axis=3
    )
    chosen_own = jnp.any(
        routes[:, 0][..., None] == jnp.arange(expert_count, dtype=jnp.int32), axis=2
    )

    index = jnp.concatenate(
        [(place ^ s) * tokens + jnp.arange(tokens, dtype=jnp.int32) for s in range(4)]
    )
    stream_all = jnp.concatenate(gather_ctx(inputs[:, 0]), axis=1).astype(F32)
    upstream_all = [gather_both(cotangent[m, 0]) for m in range(micro_count)]

    outputs, residual_grads, attention_saved, expert_saved = [], [], [], []
    out_terms = jnp.zeros_like(out_rows, F32)
    mixture_gain_grad = jnp.zeros((width,), F32)
    router_grad = jnp.zeros((width, expert_count), F32)
    tables_list = []
    for m in range(micro_count):
        segment, position = places(index, lengths[m, 0], block_order[m, 0])
        tables = (segment,) + rotary_tables(position, DH // 2)
        tables_list.append(tables)
        attended, saved = attention_forward(stream_all[m], weights, tables)
        attention_saved.append((attended, saved))
        terms = matmul(attended, out_rows).astype(BF16).reshape(4, tokens, width)
        residual = inputs[m, 0].astype(F32) + scatter_ctx([terms[s] for s in range(4)])
        scale_two = row_scale(residual)
        unit_two = residual * scale_two
        normed_two = (unit_two * mixture_all).astype(BF16)
        here, there = gather_both(normed_two)
        normed_all = jnp.concatenate([here, there])
        shared, back, gate_grad, kept = expert_pass(
            normed_all,
            jnp.concatenate(upstream_all[m]),
            chosen_all[:, m],
            router_all,
            gate_full,
            up_full,
            down_full,
            place * line_size + line,
            capacity,
        )
        expert_saved.append(kept)
        half = shared.shape[0] // 2
        outputs.append((residual + scatter_both(shared[:half], shared[half:])).astype(BF16))
        ordered_grad = gate_grad.reshape(ctx_size, line_size, tokens)
        ordered_grad = jnp.stack(
            [ordered_grad[((a ^ place) >> 1) + 2 * ((a ^ place) & 1)] for a in range(4)]
        )
        ordered_grad = jnp.stack([ordered_grad[:, b ^ line] for b in range(4)], axis=1)
        gate_value_grad = lax.all_to_all(
            ordered_grad.reshape(-1, tokens), ("ctx", "expert"), split_axis=0, concat_axis=0, tiled=True
        ).T
        gates = chosen_gates(normed_two, router_all, chosen_own[m])
        select_grad = gates * (
            gate_value_grad - jnp.sum(gates * gate_value_grad, axis=1, keepdims=True)
        )
        logit_grad = select_grad.astype(BF16)
        router_grad = router_grad + inner_rows(normed_two, logit_grad)
        normed_grad = scatter_both(back[:half], back[half:]) + matmul_t(logit_grad, router_all)
        mixture_gain_grad = mixture_gain_grad + jnp.sum(normed_grad * unit_two, axis=0)
        residual_grads.append(
            cotangent[m, 0].astype(F32) + norm_back(normed_grad, unit_two, scale_two, mixture_all)
        )

    joined_list, normed_list, input_grads = [], [], []
    attention_gain_grad = jnp.zeros((width,), F32)
    gain_pair = jnp.zeros((2 * DH,), F32)
    for m in range(micro_count):
        branch_grad = jnp.concatenate(gather_ctx(residual_grads[m].astype(BF16)))
        attended, saved = attention_saved[m]
        out_terms = out_terms + inner_rows(attended, branch_grad)
        joined, normed_grad, gain_part, pair_part = attention_backward(
            branch_grad, saved, weights, tables_list[m]
        )
        joined_list.append(joined)
        normed_list.append(saved[0])
        attention_gain_grad = attention_gain_grad + gain_part
        gain_pair = gain_pair + pair_part
        terms = normed_grad.reshape(4, tokens, width)
        normed_grad = scatter_ctx([terms[s] for s in range(4)])
        stream = inputs[m, 0].astype(F32)
        scale_one = row_scale(stream)
        input_grads.append(
            residual_grads[m] + norm_back(normed_grad, stream * scale_one, scale_one, weights[2])
        )

    projection_grad = inner_rows(jnp.concatenate(normed_list), jnp.concatenate(joined_list))
    rows = query_weight.shape[0]
    pair_column = jnp.pad(gain_pair.reshape(-1, few), ((0, 0), (0, rows - few))).reshape(-1)
    small_columns = jnp.concatenate(
        [attention_gain_grad[:, None], mixture_gain_grad[:, None], pair_column[:, None], router_grad], axis=1
    )
    reduced = scatter_grads(projection_grad, small_columns, out_terms, rows, few)

    rows_in, hidden, out_grad, gate_pre_grad, up_pre_grad = [
        jnp.concatenate(parts) for parts in zip(*expert_saved)
    ]
    gate_sum, up_sum, down_sum = [
        lax.psum_scatter(
            inner_rows(a, b).astype(BF16), "dp", scatter_dimension=0, tiled=True
        ).astype(F32)[None]
        for a, b in ((rows_in, gate_pre_grad), (rows_in, up_pre_grad), (hidden, out_grad))
    ]
    return (
        jnp.stack(outputs)[:, None],
        jnp.stack(input_grads)[:, None],
        reduced[0],
        reduced[1],
        reduced[2],
        reduced[3],
        reduced[4],
        reduced[5],
        reduced[6],
        reduced[7][:, :expert_count],
        gate_sum,
        up_sum,
        down_sum,
    )


def solution(mesh):
    tokens_4 = P(None, ("dp", "expert"), "ctx", None)
    group = P(None, ("dp", "expert"), None)
    matrix = P(("dp", "ctx", "expert"), None)
    vector = P(("dp", "ctx", "expert"))
    experts = P(("ctx", "expert"), "dp", None)
    return jax.shard_map(
        body,
        mesh=mesh,
        in_specs=(tokens_4, tokens_4, group, group, tokens_4)
        + (matrix,) * 4
        + (vector,) * 3
        + (matrix,)
        + (experts,) * 3,
        out_specs=(tokens_4, tokens_4)
        + (matrix,) * 4
        + (vector,) * 3
        + (matrix,)
        + (experts,) * 3,
        check_vma=False,
    )
```

```python
import functools

import jax
import jax.numpy as jnp
from jax import lax
from jax.experimental import pallas as pl
from jax.experimental.pallas import tpu as pltpu
from jax.sharding import PartitionSpec as P

HEADS = 16
DH = 128
BLOCK = 128
HALVES = 2
SMALL = 128
TAIL = 16

EPSILON = 1e-06
NEGATIVE = -1e30
THETA_BASE = 50000.0
QUICK = pl.CostEstimate(flops=1000, bytes_accessed=1000, transcendentals=0)
F32 = jnp.float32
BF16 = jnp.bfloat16


def dot(a, b):
    return jnp.dot(a, b, preferred_element_type=F32)
def dot_t(a, b):
    return lax.dot_general(a, b, (((1,), (1,)), ((), ())), preferred_element_type=F32)
def dot_l(a, b):
    return lax.dot_general(a, b, (((0,), (0,)), ((), ())), preferred_element_type=F32)

def expert_kernel(
    capacity, tile_f, tile_d, tokens, extra, order_ref, norm_ref, up_ref,
    wg_col, wu_col, wd_row, wd_col, wg_row, wu_row, *refs
):
    shared_ref, back_ref, rows_ref, dy_ref, h_ref, dhg_ref, dhu_ref = refs[extra : extra + 7]
    ru_ref, gate_rows_ref, sums_ref, slot_ref = refs[extra + 7 :]
    group, width = norm_ref.shape[0], norm_ref.shape[2]
    first_steps = h_ref.shape[1] // tile_f
    tiles = width // tile_d
    step = pl.program_id(0)
    expert = order_ref[0]
    tail = pl.ds(tokens, TAIL)

    def chosen(b):
        slots = lax.broadcasted_iota(jnp.int32, (capacity, tokens), 0).astype(F32)
        return slots == slot_ref[b : b + 1, :]

    @pl.when(step == 0)
    def _():
        lanes = pl.ds(pl.multiple_of(expert * tokens, tokens), tokens)
        gates = jnp.concatenate(
            [
                jnp.sum(norm_ref[b, tail, lanes].astype(F32), axis=0, keepdims=True)
                for b in range(group)
            ],
            axis=0,
        )
        here = gates > 0.0
        shape = (tokens, tokens)
        below = lax.broadcasted_iota(jnp.int32, shape, 0) <= lax.broadcasted_iota(jnp.int32, shape, 1)
        ones = jnp.where(here, 1.0, 0.0)
        counts = dot(
            jnp.concatenate([ones, jnp.zeros((16 - group, tokens), F32)], axis=0).astype(BF16),
            jnp.where(below, 1.0, 0.0).astype(BF16),
        )[:group]
        slot_ref[...] = jnp.where(here, counts - 1.0, -1.0)
        for b in range(group):
            mine = chosen(b)
            hot = jnp.where(mine, 1.0, 0.0).astype(BF16)
            gate_rows = jnp.sum(jnp.where(mine, gates[b : b + 1], 0.0), axis=1, keepdims=True)
            at = pl.ds(b * capacity, capacity)
            rows_ref[at, :] = dot(hot, norm_ref[b, :tokens, :]).astype(BF16)
            up = dot(hot, up_ref[b, 0])
            ru_ref[at, :] = up.astype(BF16)
            dy_ref[at, :] = (gate_rows * up).astype(BF16)
            gate_rows_ref[at, :] = gate_rows
        sums_ref[...] = jnp.zeros_like(sums_ref)

    @pl.when(step < first_steps)
    def _():
        at = pl.ds(pl.multiple_of(step * tile_f, tile_f), tile_f)
        hg = dot(rows_ref[...], wg_col[...])
        hu = dot(rows_ref[...], wu_col[...])
        dh = dot_t(dy_ref[...], wd_row[...])
        sig = jax.nn.sigmoid(hg)
        act = hg * sig
        h_ref[:, at] = (act * hu).astype(BF16)
        dhg_ref[:, at] = (dh * hu * sig * (1.0 + hg * (1.0 - sig))).astype(BF16)
        dhu_ref[:, at] = (dh * act).astype(BF16)

    @pl.when(step >= first_steps)
    def _():
        tile = (step - first_steps + order_ref[1] + 1) % tiles
        at = pl.ds(pl.multiple_of(tile * tile_d, tile_d), tile_d)
        y = dot(h_ref[...], wd_col[...]).astype(BF16).astype(F32)
        sums_ref[...] += jnp.sum(y * ru_ref[:, at].astype(F32), axis=1, keepdims=True)
        gy = (gate_rows_ref[...] * y).astype(BF16)
        dx = (dot_t(dhg_ref[...], wg_row[...]) + dot_t(dhu_ref[...], wu_row[...])).astype(BF16)
        for b in range(group):
            hot = jnp.where(chosen(b), 1.0, 0.0).astype(BF16)
            lo = b * capacity
            shared_ref[0, b] = dot_l(hot, gy[lo : lo + capacity]).astype(BF16)
            back_ref[b, :tokens, :] = dot_l(hot, dx[lo : lo + capacity]).astype(BF16)
            back_ref[b, tail, :] = jnp.zeros((TAIL, tile_d), BF16)

    @pl.when(step == pl.num_programs(0) - 1)
    def _():
        start = (expert % (tile_d // tokens)) * tokens
        lanes = pl.ds(pl.multiple_of(start, tokens), tokens)
        row = lax.broadcasted_iota(jnp.int32, (TAIL, tokens), 0)
        for b in range(group):
            part = sums_ref[pl.ds(b * capacity, capacity), :]
            grad = jnp.sum(jnp.where(chosen(b), part, 0.0), axis=0, keepdims=True)
            high = grad.astype(BF16).astype(F32)
            low = (grad - high).astype(BF16).astype(F32)
            rest = grad - high - low
            packed = jnp.where(row == 0, high, jnp.where(row == 1, low, jnp.where(row == 2, rest, 0.0)))
            back_ref[b, tail, lanes] = packed.astype(BF16)


def expert_call(order, norm, up, tokens, weights, kept, part, parts, shared, capacity, deps, tile_f=512, tile_d=512):
    wg, wu, wd = weights
    group, width = norm.shape[0], norm.shape[2]
    hidden = wg.shape[1]
    rows = group * capacity
    first_steps = hidden // tile_f
    tiles = width // tile_d
    anywhere = pl.BlockSpec(memory_space=pl.ANY)

    def early(i, o):
        return jnp.minimum(i, first_steps - 1)

    def late(i, o):
        return (jnp.maximum(i - first_steps, 0) + o[1] + 1) % tiles

    def fixed(shape, index=0):
        return pl.BlockSpec(shape, lambda i, o: (index,) + (0,) * (len(shape) - 1))

    def column(shape, place):
        return pl.BlockSpec(shape, lambda i, o: (0,) * (len(shape) - 1) + (place(i, o),))

    def row(shape, place):
        return pl.BlockSpec(shape, lambda i, o: (place(i, o), 0))

    micro, shared_in = shared
    shared_in = [] if shared_in is None else [shared_in]
    kept_in = [] if kept is None else list(kept)
    extra = len(deps) + len(shared_in) + len(kept_in)
    sizes = (width, width, hidden, hidden, hidden)
    struct = jax.ShapeDtypeStruct
    results = pl.pallas_call(
        functools.partial(expert_kernel, capacity, tile_f, tile_d, tokens, extra),
        grid_spec=pltpu.PrefetchScalarGridSpec(
            num_scalar_prefetch=1,
            grid=(first_steps + tiles,),
            in_specs=[
                fixed(norm.shape),
                pl.BlockSpec((group, 1, tokens, width), lambda i, o: (0, micro, 0, 0)),
                column((width, tile_f), early),
                column((width, tile_f), early),
                row((tile_f, width), early),
                column((hidden, tile_d), late),
                row((tile_d, hidden), late),
                row((tile_d, hidden), late),
            ]
            + [anywhere] * extra,
            out_specs=[
                pl.BlockSpec((1, group, tokens, tile_d), lambda i, o: (micro, 0, 0, late(i, o))),
                column((group, tokens + TAIL, tile_d), late),
            ]
            + [fixed((rows, size), part) for size in sizes],
            scratch_shapes=[
                pltpu.VMEM((rows, width), BF16),
                pltpu.VMEM((rows, 1), F32),
                pltpu.VMEM((rows, 1), F32),
                pltpu.VMEM((group, tokens), F32),
            ],
        ),
        out_shape=[struct((2, group, tokens, width), BF16), struct((group, tokens + TAIL, width), BF16)]
        + [struct((parts * rows, size), BF16) for size in sizes],
        input_output_aliases={9 + len(deps) + i: i for i in range(len(shared_in))}
        | {9 + len(deps) + len(shared_in) + i: 2 + i for i in range(len(kept_in))},
        compiler_params=pltpu.CompilerParams(vmem_limit_bytes=56 * 2**20),
        cost_estimate=QUICK,
    )(order, norm, up, wg, wu, wd, wd, wg, wu, *deps, *shared_in, *kept_in)
    return results[0], results[1], results[2:]


def product_kernel(left_ref, right_ref, *refs):
    refs[-1][...] = dot_l(left_ref[...], right_ref[...]).astype(BF16)


def product_call(left, right, deps, tile=512):
    depth, rows = left.shape
    columns = right.shape[1]
    wide = min(columns, 1024)
    return pl.pallas_call(
        product_kernel,
        grid=(columns // wide, rows // tile),
        in_specs=[
            pl.BlockSpec((depth, tile), lambda j, i: (0, i)),
            pl.BlockSpec((depth, wide), lambda j, i: (0, j)),
        ]
        + [pl.BlockSpec(memory_space=pl.ANY)] * len(deps),
        out_specs=pl.BlockSpec((tile, wide), lambda j, i: (i, j)),
        out_shape=jax.ShapeDtypeStruct((rows, columns), BF16),
        compiler_params=pltpu.CompilerParams(vmem_limit_bytes=56 * 2**20),
        cost_estimate=QUICK,
    )(left, right, *deps)


def pair_product_kernel(_, left_a, right_a, left_b, right_b, small_ref, *refs):
    out_ref = refs[-1]
    columns, few = right_a.shape[1], small_ref.shape[1]
    total = dot_l(left_a[...], right_a[...]) + dot_l(left_b[...], right_b[...])
    out_ref[:, :columns] = total.astype(BF16)
    out_ref[:, columns : columns + few] = small_ref[...]
    if out_ref.shape[1] > columns + few:
        attended_a, branch_a, attended_b, branch_b = refs[:4]
        wide = out_ref.shape[1] - columns - few
        tall = attended_a.shape[1]
        for j in range(out_ref.shape[0] // tall):
            at = slice(j * wide, (j + 1) * wide)
            total = dot_l(attended_a[...], branch_a[:, at]) + dot_l(attended_b[...], branch_b[:, at])
            out_ref[j * tall : (j + 1) * tall, columns + few :] = total.astype(BF16)


def pair_product_call(part, parts, lefts, rights, small, others, deps, tile=512):
    depth, rows = lefts[0].shape
    columns, few = rights[0].shape[1], small.shape[1]
    steps = rows // tile // parts

    def place(i, o):
        return o[0] * steps + i

    left = pl.BlockSpec((depth, tile), lambda i, o: (0, place(i, o)))
    right = pl.BlockSpec((depth, columns), lambda i, o: (0, 0))
    other_specs, wide = [], 0
    if others:
        wide = others[1].shape[1] // 4
        other_specs = [
            pl.BlockSpec((depth, tile // 2), lambda i, o: (0, place(i, o) // 2)),
            pl.BlockSpec((depth, 2 * wide), lambda i, o: (0, place(i, o) % 2)),
        ] * 2
    return pl.pallas_call(
        pair_product_kernel,
        grid_spec=pltpu.PrefetchScalarGridSpec(
            num_scalar_prefetch=1,
            grid=(steps,),
            in_specs=[left, right, left, right]
            + [pl.BlockSpec((tile, few), lambda i, o: (place(i, o), 0))]
            + other_specs
            + [pl.BlockSpec(memory_space=pl.ANY)] * len(deps),
            out_specs=pl.BlockSpec((tile, columns + few + wide), lambda i, o: (i, 0)),
        ),
        out_shape=jax.ShapeDtypeStruct((rows // parts, columns + few + wide), BF16),
        compiler_params=pltpu.CompilerParams(vmem_limit_bytes=48 * 2**20),
        cost_estimate=QUICK,
    )(part.reshape(1), lefts[0], rights[0], lefts[1], rights[1], small, *others, *deps)


def unpack_kernel(payload_ref, out_rows_ref, query_ref, key_ref, value_ref, output_ref, small_ref):
    ctx_size, _, columns = payload_ref.shape
    heads = (columns - SMALL) // (3 * DH)
    half = heads // HALVES
    for c in range(ctx_size):
        for head in range(heads):
            to = ((head // half) * ctx_size + c) * half + head % half
            for t, ref in enumerate((query_ref, key_ref, value_ref)):
                at = (3 * head + t) * DH
                ref[:, to * DH : (to + 1) * DH] = payload_ref[c, :, at : at + DH].astype(F32)
        wide = out_rows_ref.shape[2]
        output_ref[:, c * wide : (c + 1) * wide] = out_rows_ref[c]
    small_ref[...] = sum(
        payload_ref[c, :, columns - SMALL :].astype(F32) for c in range(ctx_size)
    )


def unpack_call(payload, out_rows):
    rows = payload.shape[1]
    width = out_rows.shape[0] * out_rows.shape[2]
    struct = jax.ShapeDtypeStruct
    return pl.pallas_call(
        unpack_kernel,
        out_shape=[struct((rows, width), F32)] * 4 + [struct((rows, SMALL), F32)],
    )(payload, out_rows)


def nothing_kernel(*refs):
    pass


def meet(values, *deps):
    anywhere = pl.BlockSpec(memory_space=pl.ANY)
    return pl.pallas_call(
        nothing_kernel,
        in_specs=[anywhere] * (len(values) + len(deps)),
        out_specs=[anywhere] * len(values),
        out_shape=[jax.ShapeDtypeStruct(value.shape, value.dtype) for value in values],
        input_output_aliases={i: i for i in range(len(values))},
    )(*values, *deps)


class Flow:
    def __init__(self, steps):
        self.steps = steps
        self.going = next(steps)


def idle():
    while True:
        yield []


def turn(flows, *deps, values=()):
    going = [value for flow in flows for value in flow.going] + list(values)
    deps = [value for value in deps if value is not None]
    met = meet(going, *deps) if going else deps
    token = met[0] if met else None
    for flow in flows:
        count = len(flow.going)
        flow.going = flow.steps.send(list(met[:count]))
        met = met[count:]
    return (token, list(met)) if values else token


def copy_kernel(value_ref, *refs):
    refs[-1][...] = value_ref[...]


def copy_after(value, *deps, tile=256):
    deps = [value for value in deps if value is not None]
    block = pl.BlockSpec((tile, value.shape[1]), lambda i: (i, 0))
    return pl.pallas_call(
        copy_kernel,
        grid=(value.shape[0] // tile,),
        in_specs=[block] + [pl.BlockSpec(memory_space=pl.ANY)] * len(deps),
        out_specs=block,
        out_shape=jax.ShapeDtypeStruct(value.shape, value.dtype),
        cost_estimate=QUICK,
    )(value, *deps)


def head_parts(joined, cos, sin, gain_q, gain_k, dh):
    q = joined[:, :dh]; k = joined[:, dh:2 * dh]
    rq = lax.rsqrt(jnp.mean(q * q, axis=-1, keepdims=True) + EPSILON)
    rk = lax.rsqrt(jnp.mean(k * k, axis=-1, keepdims=True) + EPSILON)
    uq = q * rq; uk = k * rk
    def turn(w):
        return (w * cos + pltpu.roll(w, dh // 2, 1) * sin).astype(BF16)
    return rq, uq, rk, uk, turn(uq * gain_q), turn(uk * gain_k), joined[:, 2 * dh:].astype(BF16)

def probabilities(qr, kr, row_ref, col_ref, dh):
    s = dot_t(qr, kr) * dh ** (-0.5)
    s = jnp.where(row_ref[...] == col_ref[...], s, NEGATIVE)
    p = jnp.exp(s - jnp.max(s, axis=-1, keepdims=True))
    return p / jnp.sum(p, axis=-1, keepdims=True)

def forward_kernel(dh, joined_ref, cos_ref, sin_ref, gain_ref, row_ref, col_ref, *refs):
    o_ref = refs[-1]
    _, _, _, _, qr, kr, v = head_parts(joined_ref[...], cos_ref[...], sin_ref[...], gain_ref[0:1, :], gain_ref[1:2, :], dh)
    p = probabilities(qr, kr, row_ref, col_ref, dh)
    o_ref[...] = dot(p.astype(BF16), v).astype(BF16)

def backward_kernel(dh, joined_ref, do_ref, cos_ref, sin_ref, gain_ref, row_ref, col_ref, *refs):
    d_ref, pair_ref = refs[-2:]
    cos = cos_ref[...]; sin = sin_ref[...]
    gq = gain_ref[0:1, :]; gk = gain_ref[1:2, :]
    rq, uq, rk, uk, qr, kr, v = head_parts(joined_ref[...], cos, sin, gq, gk, dh)
    p = probabilities(qr, kr, row_ref, col_ref, dh)
    do = do_ref[...]
    dp = dot_t(do, v)
    ds = (p * (dp - jnp.sum(p * dp, axis=-1, keepdims=True))).astype(BF16)
    scale = dh ** (-0.5)
    dq = (dot(ds, kr) * scale).astype(BF16).astype(F32)
    dk = (dot_l(ds, qr) * scale).astype(BF16).astype(F32)
    dv = dot_l(p.astype(BF16), do).astype(BF16)
    def back(w):
        return w * cos - pltpu.roll(w, dh // 2, 1) * sin
    def norm_back(up, unit, scaling, gain):
        weighted = up * gain
        return scaling * (weighted - unit * jnp.mean(weighted * unit, axis=-1, keepdims=True))
    nq = back(dq); nk = back(dk)
    d_ref[:, :dh] = norm_back(nq, uq, rq, gq).astype(BF16)
    d_ref[:, dh:2 * dh] = norm_back(nk, uk, rk, gk).astype(BF16)
    d_ref[:, 2 * dh:] = dv
    part = jnp.concatenate([jnp.sum(nq * uq, axis=0, keepdims=True), jnp.sum(nk * uk, axis=0, keepdims=True)], axis=0)
    @pl.when(pl.program_id(0) == 0)
    def _():
        pair_ref[...] = part
    @pl.when(pl.program_id(0) > 0)
    def _():
        pair_ref[...] += part

def attention_specs(tokens, heads, dh, deps):
    fixed = lambda shape: pl.BlockSpec(shape, lambda h: (0, 0))
    return (pl.BlockSpec((tokens, 3 * dh), lambda h: (0, h)), pl.BlockSpec((tokens, dh), lambda h: (0, h)),
            [fixed((tokens, dh)), fixed((tokens, dh)), fixed((2, dh)), fixed((tokens, 1)), fixed((1, tokens))] + [pl.BlockSpec(memory_space=pl.ANY)] * len(deps))

def attention_forward_call(joined, cos, sin, gains, segment, deps, dh=128):
    tokens = joined.shape[0]; heads = joined.shape[1] // (3 * dh)
    three, one, rest = attention_specs(tokens, heads, dh, deps)
    return pl.pallas_call(
        functools.partial(forward_kernel, dh), grid=(heads,), in_specs=[three] + rest, out_specs=one,
        out_shape=jax.ShapeDtypeStruct((tokens, heads * dh), BF16),
        compiler_params=pltpu.CompilerParams(vmem_limit_bytes=40 * 2**20),
        cost_estimate=QUICK,
    )(joined, cos, sin, gains, segment[:, None], segment[None, :], *deps)

def attention_backward_call(joined, grad, cos, sin, gains, segment, deps, dh=128):
    tokens = joined.shape[0]; heads = joined.shape[1] // (3 * dh)
    three, one, rest = attention_specs(tokens, heads, dh, deps)
    return pl.pallas_call(
        functools.partial(backward_kernel, dh), grid=(heads,), in_specs=[three, one] + rest,
        out_specs=[three, pl.BlockSpec((2, dh), lambda h: (0, 0))],
        out_shape=[jax.ShapeDtypeStruct(joined.shape, BF16), jax.ShapeDtypeStruct((2, dh), F32)],
        compiler_params=pltpu.CompilerParams(vmem_limit_bytes=40 * 2**20),
        cost_estimate=QUICK,
    )(joined, grad, cos, sin, gains, segment[:, None], segment[None, :], *deps)


def swap(value, axis, bit):
    return lax.ppermute(value, axis, [(i, i ^ bit) for i in range(lax.axis_size(axis))])


MIDDLE = [(1, 2), (2, 1)]
OUTWARD = [(1, 0), (2, 3)]
INWARD = [(0, 1), (3, 2)]


def scatter_ctx_steps(terms, result):
    (beside,) = yield [swap(terms[2:], "ctx", 1)]
    far = (terms[1].astype(F32) + beside[1].astype(F32)).astype(BF16)
    (across,) = yield [swap(far, "ctx", 2)]
    result.append(terms[0].astype(F32) + beside[0].astype(F32) + across.astype(F32))
    yield from idle()


def gather_ctx_steps(own, blocks):
    across, beside = yield [swap(own, "ctx", 2), swap(own, "ctx", 1)]
    (corner,) = yield [swap(across, "ctx", 1)]
    blocks += [own, across, beside, corner]
    yield from idle()


def line_steps(own, slots, across_dp=None, pause=0):
    place = lax.axis_index("expert")
    middle = (place == 1) | (place == 2)

    def over(block):
        return [] if across_dp is None else [swap(block, "dp", 1)]

    pair, third_mid, *x0 = yield [
        swap(own, "expert", 1),
        lax.ppermute(own, "expert", MIDDLE),
    ] + over(own)
    for _ in range(pause):
        yield []
    second_mid, second_end, *x1 = yield [
        lax.ppermute(pair, "expert", MIDDLE),
        lax.ppermute(third_mid, "expert", OUTWARD),
    ] + over(pair)
    second = jnp.where(middle, second_mid, second_end)
    third_end, *x2 = yield [lax.ppermute(second_mid, "expert", OUTWARD)] + over(second)
    third = jnp.where(middle, third_mid, third_end)
    slots += [own, pair, second, third]
    if across_dp is not None:
        (x3,) = yield over(third)
        across_dp += [x0[0], x1[0], x2[0], x3]
    yield from idle()


def unline_steps(slots, result):
    (three,) = yield [lax.ppermute(slots[3], "expert", INWARD)]
    second = (slots[2].astype(F32) + three.astype(F32)).astype(BF16)
    over, inward = yield [
        lax.ppermute(second, "expert", MIDDLE),
        lax.ppermute(second, "expert", INWARD),
    ]
    first = (slots[1].astype(F32) + over.astype(F32)).astype(BF16)
    third = (slots[3].astype(F32) + inward.astype(F32)).astype(BF16)
    home, pair = yield [lax.ppermute(third, "expert", MIDDLE), swap(first, "expert", 1)]
    result.append(slots[0].astype(F32) + pair.astype(F32) + home.astype(F32))
    yield from idle()


def undp_steps(here, there, result):
    moving = [swap(piece, "dp", 1) for piece in there]
    (x3,) = yield [moving[3]]
    sum3 = here[3].astype(F32) + x3.astype(F32)
    x2, three = yield [moving[2], lax.ppermute(sum3.astype(BF16), "expert", INWARD)]
    second = (here[2].astype(F32) + x2.astype(F32) + three.astype(F32)).astype(BF16)
    x1, over, inward = yield [
        moving[1],
        lax.ppermute(second, "expert", MIDDLE),
        lax.ppermute(second, "expert", INWARD),
    ]
    first = (here[1].astype(F32) + x1.astype(F32) + over.astype(F32)).astype(BF16)
    third = (sum3 + inward.astype(F32)).astype(BF16)
    x0, home, pair = yield [
        moving[0],
        lax.ppermute(third, "expert", MIDDLE),
        swap(first, "expert", 1),
    ]
    result.append(
        here[0].astype(F32) + x0.astype(F32) + pair.astype(F32) + home.astype(F32)
    )
    yield from idle()


def gather_steps(own, groups, plan):
    place = lax.axis_index("expert")
    middle = (place == 1) | (place == 2)
    blocks = [own]
    crossed = [None] * 4

    def across(step):
        return {s: swap(blocks[s], "ctx", 2) for s in range(len(blocks)) if plan[s] == step}

    def note(moving, values):
        for s, value in zip(moving, values):
            crossed[s] = value

    moving = across(0)
    pair, third_mid, *rest = yield [
        swap(own, "expert", 1),
        lax.ppermute(own, "expert", MIDDLE),
    ] + list(moving.values())
    note(moving, rest)
    blocks.append(pair)
    moving = across(1)
    second_mid, second_end, *rest = yield [
        lax.ppermute(pair, "expert", MIDDLE),
        lax.ppermute(third_mid, "expert", OUTWARD),
    ] + list(moving.values())
    note(moving, rest)
    blocks.append(jnp.where(middle, second_mid, second_end))
    moving = across(2)
    third_end, *rest = yield [lax.ppermute(second_mid, "expert", OUTWARD)] + list(moving.values())
    note(moving, rest)
    blocks.append(jnp.where(middle, third_mid, third_end))
    groups[0] = jnp.stack(blocks)
    if plan == (3, 3, 3, 3):
        moving = swap(groups[0], "ctx", 2)
        (groups[1],) = yield [swap(groups[0], "ctx", 1)]
        (groups[2],) = yield [moving]
    else:
        moving = across(3)
        groups[1], *rest = yield [swap(groups[0], "ctx", 1)] + list(moving.values())
        note(moving, rest)
        groups[2] = jnp.stack(crossed)
    (groups[3],) = yield [swap(groups[2], "ctx", 1)]
    yield from idle()


def early_gather_steps(own, groups):
    place = lax.axis_index("expert")
    middle = (place == 1) | (place == 2)
    pair, third_mid = yield [swap(own, "expert", 1), lax.ppermute(own, "expert", MIDDLE)]
    (y0,) = yield [swap(own, "ctx", 2)]
    (y1,) = yield [swap(pair, "ctx", 2)]
    second_mid, second_end = yield [
        lax.ppermute(pair, "expert", MIDDLE),
        lax.ppermute(third_mid, "expert", OUTWARD),
    ]
    second = jnp.where(middle, second_mid, second_end)
    third_end, y2 = yield [lax.ppermute(second_mid, "expert", OUTWARD), swap(second, "ctx", 2)]
    third = jnp.where(middle, third_mid, third_end)
    groups[0] = jnp.stack([own, pair, second, third])
    y3, groups[1] = yield [swap(third, "ctx", 2), swap(groups[0], "ctx", 1)]
    groups[2] = jnp.stack([y0, y1, y2, y3])
    (groups[3],) = yield [swap(groups[2], "ctx", 1)]
    yield from idle()


def scatter_steps(groups, result, slow=False):
    def slot(values, s):
        return values[..., s, :, :]

    (far,) = yield [swap(groups[3], "ctx", 1)]
    over_y = (groups[2].astype(F32) + far.astype(F32)).astype(BF16)

    def across(*slots):
        return [swap(slot(over_y, s), "ctx", 2) for s in slots]

    def total(s, moved):
        return slot(groups[0], s).astype(F32) + slot(near, s).astype(F32) + moved.astype(F32)

    def inwards(sum3):
        return lax.ppermute(sum3.astype(BF16), "expert", INWARD)

    if slow:
        (y3,) = yield across(3)
        (y2,) = yield across(2)
        y1, near = yield across(1) + [swap(groups[1], "ctx", 1)]
        sum3 = total(3, y3)
        (three,) = yield [inwards(sum3)]
        moving = across(0)
    else:
        y3, y2 = yield across(3, 2)
        y1, y0, near = yield across(1, 0) + [swap(groups[1], "ctx", 1)]
        sum3 = total(3, y3)
        (three,) = yield [inwards(sum3)]
        moving = []
    second = (total(2, y2) + three.astype(F32)).astype(BF16)
    over, inward, *rest = yield [
        lax.ppermute(second, "expert", MIDDLE),
        lax.ppermute(second, "expert", INWARD),
    ] + moving
    y0 = rest[0] if rest else y0
    first = (total(1, y1) + over.astype(F32)).astype(BF16)
    third = (sum3 + inward.astype(F32)).astype(BF16)
    home, pair = yield [lax.ppermute(third, "expert", MIDDLE), swap(first, "expert", 1)]
    result.append(total(0, y0) + pair.astype(F32) + home.astype(F32))
    yield from idle()


def places(index, lengths, block_order):
    blocks = jnp.arange(block_order.shape[0], dtype=jnp.int32)
    holder = (index // BLOCK)[:, None] == blocks[None, :]
    logical = (
        jnp.sum(jnp.where(holder, block_order[None, :], 0), axis=1) * BLOCK + index % BLOCK
    )
    seq_ends = jnp.cumsum(lengths)
    segment = jnp.sum((logical[:, None] >= seq_ends[None, :]).astype(jnp.int32), axis=1)
    starts = seq_ends - lengths
    member = segment[:, None] == jnp.arange(lengths.shape[0], dtype=jnp.int32)[None, :]
    seq_first = jnp.sum(jnp.where(member, starts[None, :], 0), axis=1)
    return (segment, (logical - seq_first).astype(F32))


def rotary_tables(positions, half_size):
    frequency = THETA_BASE ** (-(jnp.arange(half_size, dtype=F32) / half_size))
    angles = positions[:, None] * frequency[None, :]
    cosine, sine = jnp.cos(angles), jnp.sin(angles)
    return jnp.concatenate([cosine, cosine], axis=1), jnp.concatenate([-sine, sine], axis=1)


def norm_back(upstream, unit_rows, scaling, gain_vector):
    weighted = upstream * gain_vector
    return scaling * (weighted - unit_rows * jnp.mean(weighted * unit_rows, axis=-1, keepdims=True))


def row_scale(rows):
    return lax.rsqrt(jnp.mean(rows * rows, axis=-1, keepdims=True) + EPSILON)


def whole_heads(rows, share):
    return lax.axis_size("dp") == HALVES and rows * lax.axis_size("expert") == share


def assemble(pieces, shape):
    d, z = lax.axis_index("dp"), lax.axis_index("expert")
    whole = jnp.zeros(shape, BF16)
    for dx, line in enumerate(pieces):
        for s, piece in enumerate(line):
            whole = lax.dynamic_update_slice(
                whole, piece[None, :, None], (d ^ dx if shape[0] > 1 else 0, 0, z ^ s) + (0,) * (len(shape) - 3)
            )
    return whole


def piece_of(whole, dx, s):
    first = lax.axis_index("dp") ^ dx if whole.shape[0] > 1 else 0
    start = (first, 0, lax.axis_index("expert") ^ s) + (0,) * (whole.ndim - 3)
    return lax.dynamic_slice(whole, start, (1, whole.shape[1], 1) + whole.shape[3:])[0, :, 0]


def sum_rows(whole):
    return lax.psum_scatter(whole, "dp", scatter_dimension=0, tiled=True)


def pack_weights(query_weight, key_weight, value_weight, attention_gain, mixture_gain, query_key_gain, router):
    rows, width = query_weight.shape
    ctx_size = lax.axis_size("ctx")
    share = width // (HALVES * ctx_size)
    stacked = jnp.stack([query_weight, key_weight, value_weight], axis=1)
    stacked = stacked.reshape(rows, 3, HALVES, ctx_size, share // DH, DH)
    stacked = stacked.transpose(3, 0, 2, 4, 1, 5).reshape(ctx_size, rows, 3 * HALVES * share)
    small = jnp.concatenate(
        [
            attention_gain[:, None],
            mixture_gain[:, None],
            jnp.pad(query_key_gain, (0, rows - query_key_gain.shape[0]))[:, None],
            router,
        ],
        axis=1,
    )
    small = jnp.pad(small, ((0, 0), (0, SMALL - small.shape[1])))
    return jnp.concatenate(
        [stacked, jnp.broadcast_to(small[None], (ctx_size, rows, SMALL))], axis=2
    )


def chosen_gates(normed, router, chosen):
    logits = jnp.where(chosen, dot(normed, router), NEGATIVE)
    powers = jnp.where(chosen, jnp.exp(logits - jnp.max(logits, axis=1, keepdims=True)), 0.0)
    return powers / jnp.sum(powers, axis=1, keepdims=True)


def with_gates(normed, gates):
    flat = gates.T.reshape(1, -1)
    high = flat.astype(BF16).astype(F32)
    low = (flat - high).astype(BF16).astype(F32)
    row = lax.broadcasted_iota(jnp.int32, (TAIL, flat.shape[1]), 0)
    tail = jnp.where(row == 0, high, jnp.where(row == 1, low, jnp.where(row == 2, flat - high - low, 0.0)))
    return jnp.concatenate([normed, tail.astype(BF16)])


def body(
    inputs,
    cotangent,
    lengths,
    block_order,
    routes,
    query_weight,
    key_weight,
    value_weight,
    output_weight,
    attention_gain,
    mixture_gain,
    query_key_gain,
    router,
    expert_gate,
    expert_up,
    expert_down,
):
    micro_count, _, tokens, width = inputs.shape
    top = routes.shape[3]
    expert_count = router.shape[1]
    most = tokens * top * 9 // (8 * expert_count) + 2
    capacity = -(-most // 16) * 16
    place = lax.axis_index("ctx")
    rows, few = query_weight.shape[0], query_key_gain.shape[0]
    micros = range(micro_count)

    line = lax.axis_index("expert")
    dp_size = lax.axis_size("dp")
    two = dp_size == 2
    share = width // (HALVES * 4)
    per_ctx = HALVES * share

    slots, slots_dp, blocks = [], [] if two else None, []
    heads_here = whole_heads(rows, share)
    upstream_groups = [None] * 4
    upstream_flow = Flow(early_gather_steps(cotangent[:, 0], upstream_groups))
    payload = pack_weights(
        query_weight, key_weight, value_weight, attention_gain, mixture_gain, query_key_gain, router
    )
    payload = lax.all_to_all(payload, "ctx", split_axis=0, concat_axis=0, tiled=True)
    if heads_here:
        chunks = output_weight.reshape(rows, 4, width // 4).transpose(1, 0, 2)
        payload = jnp.concatenate([payload, chunks], axis=2)
    spread = Flow(line_steps(payload, slots, slots_dp))
    stream_flow = Flow(
        gather_ctx_steps(copy_after(inputs.reshape(-1, width), payload).reshape(-1, tokens, width), blocks)
    )
    token = turn([spread, upstream_flow])
    token = turn([spread, stream_flow, upstream_flow])
    token = turn([spread, stream_flow, upstream_flow], token)
    copies = [copy_after(own[0], token) for own in (expert_gate, expert_up, expert_down)]
    token = turn([spread, upstream_flow], token, *copies)
    experts = [lax.all_gather(own, "dp", axis=0, tiled=True) for own in copies]
    shape = (dp_size, 4, 4) + payload.shape[1:]
    if two:
        packed = assemble([slots, slots_dp], shape)
    else:
        packed = lax.all_gather(
            assemble([slots], (1,) + shape[1:])[0], "dp", axis=0, tiled=False
        )
    if heads_here:
        out_rows = packed[..., 3 * per_ctx + SMALL :].transpose(0, 2, 3, 1, 4).reshape(per_ctx, width)
    packed = packed.reshape(width, -1)
    projections = packed[:, : 3 * per_ctx]
    small = packed[:, 3 * per_ctx : 3 * per_ctx + SMALL].astype(F32)
    gain_one, gain_two = small[:, 0], small[:, 1]
    gain_pair = small[:, 2].reshape(-1, rows)[:, :few].reshape(2, DH)
    router_all = packed[:, 3 * per_ctx + 3 : 3 * per_ctx + 3 + expert_count]

    index = jnp.concatenate(
        [(place ^ s) * tokens + jnp.arange(tokens, dtype=jnp.int32) for s in (0, 2, 1, 3)]
    )
    tables = []
    for m in micros:
        segment, position = places(index, lengths[m, 0], block_order[m, 0])
        tables.append(rotary_tables(position, DH // 2) + (gain_pair, segment))
    stream_all = jnp.concatenate(blocks, axis=1)

    normed_one, units, joined_list, attended_list = [], [], [], []

    def attention(m, token, flows):
        stream = stream_all[m].astype(F32)
        unit = stream * row_scale(stream)
        normed = (unit * gain_one).astype(BF16)
        joined = dot(normed, projections)
        if flows:
            token, (joined,) = turn(flows, token, values=[joined])
        attended = attention_forward_call(joined, *tables[m], [token])
        normed_one.append(normed)
        units.append(unit)
        joined_list.append(joined)
        attended_list.append(attended)
        return attended

    def out_terms_of(m):
        return dot(attended_list[m], out_rows).astype(BF16).reshape(4, tokens, width)

    done = attention(0, token, [])
    if not heads_here:
        out_rows = lax.all_gather(output_weight, ("dp", "ctx", "expert"), axis=0, tiled=True)
        out_rows = out_rows.reshape(HALVES, 4, share, -1)
        out_rows = lax.dynamic_index_in_dim(out_rows, place, 1, keepdims=False)
        out_rows = out_rows.reshape(per_ctx, -1)
    sum_a, sum_b = [], []
    flow_a = Flow(scatter_ctx_steps(out_terms_of(0), sum_a))
    token = turn([flow_a], experts[0])
    done = attention(1, token, [])
    token = turn([flow_a, upstream_flow], done)
    flow_b = Flow(scatter_ctx_steps(out_terms_of(1), sum_b))

    normed_two, unit_two, scale_two, gates_own, residuals = [], [], [], [], []

    def route(m, attention_sum):
        residual = inputs[m, 0].astype(F32) + attention_sum
        scale = row_scale(residual)
        unit = residual * scale
        normed = (unit * gain_two).astype(BF16)
        chosen = jnp.any(
            routes[m, 0][..., None] == jnp.arange(expert_count, dtype=jnp.int32), axis=1
        )
        gates = chosen_gates(normed, router_all, chosen)
        residuals.append(residual)
        normed_two.append(normed)
        unit_two.append(unit)
        scale_two.append(scale)
        gates_own.append(gates)
        return with_gates(normed, gates)

    groups = [[None] * 4 for _ in micros]
    gather_a = Flow(gather_steps(route(0, sum_a[0]), groups[0], (3, 3, 3, 3)))
    token = turn([flow_b, gather_a], experts[1])
    token = turn([gather_a, upstream_flow])
    token = turn([gather_a, upstream_flow, flow_b], experts[2])
    second_payload = route(1, sum_b[0])
    gather_b = Flow(gather_steps(second_payload, groups[1], (1, 1, 2, 3)))

    shared, kept, calls = [None] * 4, None, 0
    back = [[None] * 4 for _ in micros]
    expert_index = place * 4 + line
    order = jnp.stack([expert_index, expert_index * tokens // 512]).astype(jnp.int32)

    def expert(m, k, token, flows):
        nonlocal kept, calls
        shared[k], back[m][k], kept = expert_call(
            order, groups[m][k], upstream_groups[k], tokens, experts, kept, calls, 8, (m, shared[k]), capacity, [token]
        )
        calls += 1
        token, met = turn(flows, values=[shared[k], back[m][k], *kept])
        shared[k], back[m][k], kept = met[0], met[1], met[2:]
        return token

    token = expert(0, 0, token, [gather_a, gather_b])
    token = expert(0, 1, token, [gather_a, gather_b])
    token = expert(0, 2, token, [gather_a, gather_b])
    token = expert(0, 3, token, [gather_b])
    down_a, down_b, out_sum = [], [], []
    scatter_a = Flow(scatter_steps(back[0], down_a))
    token = expert(1, 2, token, [gather_b, scatter_a])
    token = expert(1, 3, token, [scatter_a])
    scatter_b = Flow(scatter_steps(back[1], down_b))
    token = expert(1, 1, token, [scatter_a, scatter_b])
    token = expert(1, 0, token, [scatter_a, scatter_b])
    rows_in, out_grad, hidden, gate_pre_grad, up_pre_grad = kept
    out_flow = Flow(scatter_steps(shared, out_sum, True))
    down_whole = product_call(hidden, out_grad, [token])
    token, (down_whole,) = turn([scatter_a, scatter_b, out_flow], values=[down_whole])
    down_sum = sum_rows(down_whole)
    gate_whole = product_call(rows_in, gate_pre_grad, [token])
    token, (gate_whole,) = turn([scatter_a, scatter_b, out_flow], values=[gate_whole])

    gate_sum = sum_rows(gate_whole)
    residual_grads, normed_grads, logit_grads = [], [], []

    def residual_back(m, summed):
        gates = gates_own[m]
        gate_value_grad = jnp.sum(summed[tokens:], axis=0).reshape(expert_count, tokens).T
        select_grad = gates * (
            gate_value_grad - jnp.sum(gates * gate_value_grad, axis=1, keepdims=True)
        )
        logit_grad = select_grad.astype(BF16)
        normed_grad = summed[:tokens] + dot_t(logit_grad, router_all)
        residual_grad = cotangent[m, 0].astype(F32) + norm_back(
            normed_grad, unit_two[m], scale_two[m], gain_two
        )
        residual_grads.append(residual_grad)
        normed_grads.append(normed_grad)
        logit_grads.append(logit_grad)
        return residual_grad.astype(BF16)

    branch = [[], []]
    branch_a = Flow(gather_ctx_steps(residual_back(0, down_a[0]), branch[0]))
    up_whole = product_call(rows_in, up_pre_grad, [token])
    token, (up_whole,) = turn([branch_a, scatter_b, out_flow], values=[up_whole])
    up_sum = sum_rows(up_whole)
    token = turn([branch_a])

    joined_grads, normed_one_grads, pair_grads, branch_list = [], [], [], []

    def attention_back(m, token):
        branch_grad = jnp.concatenate(branch[m])
        attended_grad = dot_t(branch_grad, out_rows).astype(BF16)
        joined_grad, pair_part = attention_backward_call(
            joined_list[m], attended_grad, *tables[m], [token]
        )
        branch_list.append(branch_grad)
        joined_grads.append(joined_grad)
        pair_grads.append(pair_part)
        return pair_part

    done = attention_back(0, token)
    token = turn([scatter_b, out_flow], done, down_sum)
    branch_b = Flow(gather_ctx_steps(residual_back(1, down_b[0]), branch[1]))
    normed_one_grads.append(dot_t(joined_grads[0], projections))
    token = turn([branch_b], normed_one_grads[0])
    token = turn([branch_b])
    done = attention_back(1, token)
    token = turn([out_flow], done, gate_sum)
    normed_one_grads.append(dot_t(joined_grads[1], projections))
    attention_gain_grad = sum(
        jnp.sum(grad * unit, axis=0) for grad, unit in zip(normed_one_grads, units)
    )
    mixture_gain_grad = sum(
        jnp.sum(grad * unit, axis=0) for grad, unit in zip(normed_grads, unit_two)
    )
    router_grad = sum(dot_l(left, right) for left, right in zip(normed_two, logit_grads))
    pair_grad = (pair_grads[0] + pair_grads[1]).reshape(-1, few)
    pair_column = jnp.pad(pair_grad, ((0, 0), (0, rows - few))).reshape(-1)
    small_columns = jnp.concatenate(
        [attention_gain_grad[:, None], mixture_gain_grad[:, None], pair_column[:, None], router_grad], axis=1
    )
    small_columns = jnp.pad(small_columns, ((0, 0), (0, SMALL - small_columns.shape[1])))
    terms = jnp.stack(
        [grad.astype(BF16).reshape(4, tokens, width) for grad in normed_one_grads], axis=1
    )

    others = [attended_list[0], branch_list[0], attended_list[1], branch_list[1]] if heads_here else []

    def gradient_rows(part, parts, token):
        product = pair_product_call(
            part, parts, normed_one, joined_grads, small_columns.astype(BF16), others, [token]
        )
        return product.reshape(dp_size // parts, 4, 4, rows, -1)

    packed_sum, back_sum = [], []
    if two:
        d = lax.axis_index("dp").astype(jnp.int32)
        there = gradient_rows(1 - d, 2, token)
        here = gradient_rows(d, 2, there)
        token, (here,) = turn([out_flow], values=[here])
        last = Flow(
            undp_steps(*[[piece_of(part, 0, s) for s in range(4)] for part in (here, there)], packed_sum)
        )
    else:
        whole = gradient_rows(jnp.zeros((), jnp.int32), 1, token)
        whole = lax.psum_scatter(whole, "dp", scatter_dimension=0, tiled=True)
        token = turn([out_flow])
        last = Flow(unline_steps([piece_of(whole, 0, s) for s in range(4)], packed_sum))
    back_flow = Flow(scatter_ctx_steps(terms, back_sum))
    token = turn([last, back_flow, out_flow])
    token = turn([last, back_flow], up_sum)
    token, (gate_sum, up_sum, down_sum) = turn(
        [last], token, values=[value.astype(F32) for value in (gate_sum, up_sum, down_sum)]
    )
    if two:
        token = turn([last])
    summed = packed_sum[0]
    columns = 3 * per_ctx + SMALL
    swapped = lax.all_to_all(
        summed[..., :columns].astype(BF16), "ctx", split_axis=0, concat_axis=0, tiled=True
    )
    if heads_here:
        out_rows_sum = summed[..., columns:]
    else:
        out_grad_rows = sum(
            dot_l(left, right) for left, right in zip(attended_list, branch_list)
        ).astype(BF16)
        spread_rows = jnp.zeros((HALVES, 4, share, width), BF16)
        spread_rows = lax.dynamic_update_slice_in_dim(
            spread_rows, out_grad_rows.reshape(HALVES, 1, share, width), place, 1
        )
        out_rows_sum = lax.psum_scatter(
            spread_rows.reshape(-1, width), ("dp", "ctx", "expert"), scatter_dimension=0, tiled=True
        ).astype(F32)
        out_rows_sum = out_rows_sum.reshape(rows, 4, width // 4).transpose(1, 0, 2)
    *gradients, small_sums = unpack_call(swapped, out_rows_sum)
    outputs = [(residuals[m] + out_sum[0][m]).astype(BF16) for m in micros]
    input_grads = []
    for m in micros:
        stream = inputs[m, 0].astype(F32)
        scale_one = row_scale(stream)
        input_grads.append(
            residual_grads[m] + norm_back(back_sum[0][m], stream * scale_one, scale_one, gain_one)
        )
    return (
        jnp.stack(outputs)[:, None],
        jnp.stack(input_grads)[:, None],
        gradients[0],
        gradients[1],
        gradients[2],
        gradients[3],
        small_sums[:, 0],
        small_sums[:, 1],
        small_sums[:few, 2],
        small_sums[:, 3 : 3 + expert_count],
        gate_sum[None],
        up_sum[None],
        down_sum[None],
    )


def solution(mesh):
    tokens_4 = P(None, ("dp", "expert"), "ctx", None)
    group = P(None, ("dp", "expert"), None)
    matrix = P(("dp", "ctx", "expert"), None)
    vector = P(("dp", "ctx", "expert"))
    experts = P(("ctx", "expert"), "dp", None)
    return jax.shard_map(
        body,
        mesh=mesh,
        in_specs=(tokens_4, tokens_4, group, group, tokens_4)
        + (matrix,) * 4
        + (vector,) * 3
        + (matrix,)
        + (experts,) * 3,
        out_specs=(tokens_4, tokens_4)
        + (matrix,) * 4
        + (vector,) * 3
        + (matrix,)
        + (experts,) * 3,
        check_vma=False,
    )
```

```python
import functools

import jax
import jax.numpy as jnp
from jax import lax
from jax.experimental import pallas as pl
from jax.experimental.pallas import tpu as pltpu
from jax.sharding import PartitionSpec as P

HEADS = 16
DH = 128
BLOCK = 128
HALVES = 2
SMALL = 128
TAIL = 16

EPSILON = 1e-06
NEGATIVE = -1e30
THETA_BASE = 50000.0
QUICK = pl.CostEstimate(flops=1000, bytes_accessed=1000, transcendentals=0)
F32 = jnp.float32
BF16 = jnp.bfloat16


def dot(a, b):
    return jnp.dot(a, b, preferred_element_type=F32)
def dot_t(a, b):
    return lax.dot_general(a, b, (((1,), (1,)), ((), ())), preferred_element_type=F32)
def dot_l(a, b):
    return lax.dot_general(a, b, (((0,), (0,)), ((), ())), preferred_element_type=F32)

def expert_kernel(
    capacity, tile_f, tile_d, tokens, extra, order_ref, norm_ref, up_ref,
    wg_hbm, wu_hbm, wd_hbm, *refs
):
    shared_ref, back_ref, rows_ref, dy_ref, h_ref, dhg_ref, dhu_ref = refs[extra : extra + 7]
    ru_ref, gate_rows_ref, sums_ref, slot_ref, wg_ref, wu_ref, wd_ref, arrived = refs[extra + 7 :]
    group, width = norm_ref.shape[0], norm_ref.shape[2]
    first_steps = h_ref.shape[1] // tile_f
    tiles = width // tile_d
    step = pl.program_id(0)
    expert = order_ref[0]
    tail = pl.ds(tokens, TAIL)

    def copies(j):
        at = pl.ds(j * tile_f, tile_f)
        return [
            pltpu.make_async_copy(wg_hbm.at[:, at], wg_ref.at[:, at], arrived.at[j, 0]),
            pltpu.make_async_copy(wu_hbm.at[:, at], wu_ref.at[:, at], arrived.at[j, 1]),
            pltpu.make_async_copy(wd_hbm.at[at, :], wd_ref.at[at, :], arrived.at[j, 2]),
        ]

    def chosen(b):
        slots = lax.broadcasted_iota(jnp.int32, (capacity, tokens), 0).astype(F32)
        return slots == slot_ref[b : b + 1, :]

    @pl.when(step == 0)
    def _():
        for j in range(first_steps):
            for copy in copies(j):
                copy.start()
        lanes = pl.ds(pl.multiple_of(expert * tokens, tokens), tokens)
        gates = jnp.concatenate(
            [
                jnp.sum(norm_ref[b, tail, lanes].astype(F32), axis=0, keepdims=True)
                for b in range(group)
            ],
            axis=0,
        )
        here = gates > 0.0
        shape = (tokens, tokens)
        below = lax.broadcasted_iota(jnp.int32, shape, 0) <= lax.broadcasted_iota(jnp.int32, shape, 1)
        ones = jnp.where(here, 1.0, 0.0)
        counts = dot(
            jnp.concatenate([ones, jnp.zeros((16 - group, tokens), F32)], axis=0).astype(BF16),
            jnp.where(below, 1.0, 0.0).astype(BF16),
        )[:group]
        slot_ref[...] = jnp.where(here, counts - 1.0, -1.0)
        for b in range(group):
            mine = chosen(b)
            hot = jnp.where(mine, 1.0, 0.0).astype(BF16)
            gate_rows = jnp.sum(jnp.where(mine, gates[b : b + 1], 0.0), axis=1, keepdims=True)
            at = pl.ds(b * capacity, capacity)
            rows_ref[at, :] = dot(hot, norm_ref[b, :tokens, :]).astype(BF16)
            up = dot(hot, up_ref[b, 0])
            ru_ref[at, :] = up.astype(BF16)
            dy_ref[at, :] = (gate_rows * up).astype(BF16)
            gate_rows_ref[at, :] = gate_rows
        sums_ref[...] = jnp.zeros_like(sums_ref)

    for j in range(first_steps):
        @pl.when(step == j)
        def _():
            for copy in copies(j):
                copy.wait()

    @pl.when(step < first_steps)
    def _():
        at = pl.ds(pl.multiple_of(step * tile_f, tile_f), tile_f)
        hg = dot(rows_ref[...], wg_ref[:, at])
        hu = dot(rows_ref[...], wu_ref[:, at])
        dh = dot_t(dy_ref[...], wd_ref[at, :])
        sig = jax.nn.sigmoid(hg)
        act = hg * sig
        h_ref[:, at] = (act * hu).astype(BF16)
        dhg_ref[:, at] = (dh * hu * sig * (1.0 + hg * (1.0 - sig))).astype(BF16)
        dhu_ref[:, at] = (dh * act).astype(BF16)

    @pl.when(step >= first_steps)
    def _():
        tile = (step - first_steps + order_ref[1] + 1) % tiles
        at = pl.ds(pl.multiple_of(tile * tile_d, tile_d), tile_d)
        y = dot(h_ref[...], wd_ref[:, at]).astype(BF16).astype(F32)
        sums_ref[...] += jnp.sum(y * ru_ref[:, at].astype(F32), axis=1, keepdims=True)
        gy = (gate_rows_ref[...] * y).astype(BF16)
        dx = (dot_t(dhg_ref[...], wg_ref[at, :]) + dot_t(dhu_ref[...], wu_ref[at, :])).astype(BF16)
        for b in range(group):
            hot = jnp.where(chosen(b), 1.0, 0.0).astype(BF16)
            lo = b * capacity
            shared_ref[0, b] = dot_l(hot, gy[lo : lo + capacity]).astype(BF16)
            back_ref[b, :tokens, :] = dot_l(hot, dx[lo : lo + capacity]).astype(BF16)
            back_ref[b, tail, :] = jnp.zeros((TAIL, tile_d), BF16)

    @pl.when(step == pl.num_programs(0) - 1)
    def _():
        start = (expert % (tile_d // tokens)) * tokens
        lanes = pl.ds(pl.multiple_of(start, tokens), tokens)
        row = lax.broadcasted_iota(jnp.int32, (TAIL, tokens), 0)
        for b in range(group):
            part = sums_ref[pl.ds(b * capacity, capacity), :]
            grad = jnp.sum(jnp.where(chosen(b), part, 0.0), axis=0, keepdims=True)
            high = grad.astype(BF16).astype(F32)
            low = (grad - high).astype(BF16).astype(F32)
            rest = grad - high - low
            packed = jnp.where(row == 0, high, jnp.where(row == 1, low, jnp.where(row == 2, rest, 0.0)))
            back_ref[b, tail, lanes] = packed.astype(BF16)


def expert_call(order, norm, up, tokens, weights, kept, part, parts, shared, capacity, deps, tile_f=512, tile_d=512):
    wg, wu, wd = weights
    group, width = norm.shape[0], norm.shape[2]
    hidden = wg.shape[1]
    rows = group * capacity
    first_steps = hidden // tile_f
    tiles = width // tile_d
    anywhere = pl.BlockSpec(memory_space=pl.ANY)

    def late(i, o):
        return (jnp.maximum(i - first_steps, 0) + o[1] + 1) % tiles

    def fixed(shape, index=0):
        return pl.BlockSpec(shape, lambda i, o: (index,) + (0,) * (len(shape) - 1))

    def column(shape, place):
        return pl.BlockSpec(shape, lambda i, o: (0,) * (len(shape) - 1) + (place(i, o),))

    micro, shared_in = shared
    shared_in = [] if shared_in is None else [shared_in]
    kept_in = [] if kept is None else list(kept)
    extra = len(deps) + len(shared_in) + len(kept_in)
    sizes = (width, width, hidden, hidden, hidden)
    struct = jax.ShapeDtypeStruct
    results = pl.pallas_call(
        functools.partial(expert_kernel, capacity, tile_f, tile_d, tokens, extra),
        grid_spec=pltpu.PrefetchScalarGridSpec(
            num_scalar_prefetch=1,
            grid=(first_steps + tiles,),
            in_specs=[
                fixed(norm.shape),
                pl.BlockSpec((group, 1, tokens, width), lambda i, o: (0, micro, 0, 0)),
                anywhere,
                anywhere,
                anywhere,
            ]
            + [anywhere] * extra,
            out_specs=[
                pl.BlockSpec((1, group, tokens, tile_d), lambda i, o: (micro, 0, 0, late(i, o))),
                column((group, tokens + TAIL, tile_d), late),
            ]
            + [fixed((rows, size), part) for size in sizes],
            scratch_shapes=[
                pltpu.VMEM((rows, width), BF16),
                pltpu.VMEM((rows, 1), F32),
                pltpu.VMEM((rows, 1), F32),
                pltpu.VMEM((group, tokens), F32),
                pltpu.VMEM(wg.shape, BF16),
                pltpu.VMEM(wu.shape, BF16),
                pltpu.VMEM(wd.shape, BF16),
                pltpu.SemaphoreType.DMA((first_steps, 3)),
            ],
        ),
        out_shape=[struct((2, group, tokens, width), BF16), struct((group, tokens + TAIL, width), BF16)]
        + [struct((parts * rows, size), BF16) for size in sizes],
        input_output_aliases={6 + len(deps) + i: i for i in range(len(shared_in))}
        | {6 + len(deps) + len(shared_in) + i: 2 + i for i in range(len(kept_in))},
        compiler_params=pltpu.CompilerParams(vmem_limit_bytes=58 * 2**20),
        cost_estimate=QUICK,
    )(order, norm, up, wg, wu, wd, *deps, *shared_in, *kept_in)
    return results[0], results[1], results[2:]


def product_kernel(left_ref, right_ref, *refs):
    refs[-1][...] = dot_l(left_ref[...], right_ref[...]).astype(BF16)


def product_call(left, right, deps, tile=512):
    depth, rows = left.shape
    columns = right.shape[1]
    wide = min(columns, 1024)
    return pl.pallas_call(
        product_kernel,
        grid=(columns // wide, rows // tile),
        in_specs=[
            pl.BlockSpec((depth, tile), lambda j, i: (0, i)),
            pl.BlockSpec((depth, wide), lambda j, i: (0, j)),
        ]
        + [pl.BlockSpec(memory_space=pl.ANY)] * len(deps),
        out_specs=pl.BlockSpec((tile, wide), lambda j, i: (i, j)),
        out_shape=jax.ShapeDtypeStruct((rows, columns), BF16),
        compiler_params=pltpu.CompilerParams(vmem_limit_bytes=56 * 2**20),
        cost_estimate=QUICK,
    )(left, right, *deps)


def pair_product_kernel(_, left_a, right_a, left_b, right_b, small_ref, *refs):
    out_ref = refs[-1]
    columns, few = right_a.shape[1], small_ref.shape[1]
    total = dot_l(left_a[...], right_a[...]) + dot_l(left_b[...], right_b[...])
    out_ref[:, :columns] = total.astype(BF16)
    out_ref[:, columns : columns + few] = small_ref[...]
    if out_ref.shape[1] > columns + few:
        attended_a, branch_a, attended_b, branch_b = refs[:4]
        wide = out_ref.shape[1] - columns - few
        tall = attended_a.shape[1]
        for j in range(out_ref.shape[0] // tall):
            at = slice(j * wide, (j + 1) * wide)
            total = dot_l(attended_a[...], branch_a[:, at]) + dot_l(attended_b[...], branch_b[:, at])
            out_ref[j * tall : (j + 1) * tall, columns + few :] = total.astype(BF16)


def pair_product_call(part, parts, lefts, rights, small, others, deps, tile=512):
    depth, rows = lefts[0].shape
    columns, few = rights[0].shape[1], small.shape[1]
    steps = rows // tile // parts

    def place(i, o):
        return o[0] * steps + i

    left = pl.BlockSpec((depth, tile), lambda i, o: (0, place(i, o)))
    right = pl.BlockSpec((depth, columns), lambda i, o: (0, 0))
    other_specs, wide = [], 0
    if others:
        wide = others[1].shape[1] // 4
        other_specs = [
            pl.BlockSpec((depth, tile // 2), lambda i, o: (0, place(i, o) // 2)),
            pl.BlockSpec((depth, 2 * wide), lambda i, o: (0, place(i, o) % 2)),
        ] * 2
    return pl.pallas_call(
        pair_product_kernel,
        grid_spec=pltpu.PrefetchScalarGridSpec(
            num_scalar_prefetch=1,
            grid=(steps,),
            in_specs=[left, right, left, right]
            + [pl.BlockSpec((tile, few), lambda i, o: (place(i, o), 0))]
            + other_specs
            + [pl.BlockSpec(memory_space=pl.ANY)] * len(deps),
            out_specs=pl.BlockSpec((tile, columns + few + wide), lambda i, o: (i, 0)),
        ),
        out_shape=jax.ShapeDtypeStruct((rows // parts, columns + few + wide), BF16),
        compiler_params=pltpu.CompilerParams(vmem_limit_bytes=48 * 2**20),
        cost_estimate=QUICK,
    )(part.reshape(1), lefts[0], rights[0], lefts[1], rights[1], small, *others, *deps)


def unpack_kernel(payload_ref, query_ref, key_ref, value_ref, small_ref):
    ctx_size, _, columns = payload_ref.shape
    heads = (columns - SMALL) // (3 * DH)
    half = heads // HALVES
    for c in range(ctx_size):
        for head in range(heads):
            to = ((head // half) * ctx_size + c) * half + head % half
            for t, ref in enumerate((query_ref, key_ref, value_ref)):
                at = (3 * head + t) * DH
                ref[:, to * DH : (to + 1) * DH] = payload_ref[c, :, at : at + DH].astype(F32)
    small_ref[...] = sum(
        payload_ref[c, :, columns - SMALL :].astype(F32) for c in range(ctx_size)
    )


def unpack_call(payload):
    ctx_size, rows, columns = payload.shape
    width = ctx_size * (columns - SMALL) // 3
    struct = jax.ShapeDtypeStruct
    return pl.pallas_call(
        unpack_kernel,
        out_shape=[struct((rows, width), F32)] * 3 + [struct((rows, SMALL), F32)],
    )(payload)


def nothing_kernel(*refs):
    pass


def meet(values, *deps):
    anywhere = pl.BlockSpec(memory_space=pl.ANY)
    return pl.pallas_call(
        nothing_kernel,
        in_specs=[anywhere] * (len(values) + len(deps)),
        out_specs=[anywhere] * len(values),
        out_shape=[jax.ShapeDtypeStruct(value.shape, value.dtype) for value in values],
        input_output_aliases={i: i for i in range(len(values))},
    )(*values, *deps)


class Flow:
    def __init__(self, steps):
        self.steps = steps
        self.going = next(steps)


def idle():
    while True:
        yield []


def turn(flows, *deps, values=()):
    going = [value for flow in flows for value in flow.going] + list(values)
    deps = [value for value in deps if value is not None]
    met = meet(going, *deps) if going else deps
    token = met[0] if met else None
    for flow in flows:
        count = len(flow.going)
        flow.going = flow.steps.send(list(met[:count]))
        met = met[count:]
    return (token, list(met)) if values else token


def copy_kernel(value_ref, *refs):
    refs[-1][...] = value_ref[...]


def copy_after(value, *deps, tile=256):
    deps = [value for value in deps if value is not None]
    block = pl.BlockSpec((tile, value.shape[1]), lambda i: (i, 0))
    return pl.pallas_call(
        copy_kernel,
        grid=(value.shape[0] // tile,),
        in_specs=[block] + [pl.BlockSpec(memory_space=pl.ANY)] * len(deps),
        out_specs=block,
        out_shape=jax.ShapeDtypeStruct(value.shape, value.dtype),
        compiler_params=pltpu.CompilerParams(vmem_limit_bytes=16 * 2**20),
        cost_estimate=QUICK,
    )(value, *deps)


def head_parts(joined, cos, sin, gain_q, gain_k, dh):
    q = joined[:, :dh]; k = joined[:, dh:2 * dh]
    rq = lax.rsqrt(jnp.mean(q * q, axis=-1, keepdims=True) + EPSILON)
    rk = lax.rsqrt(jnp.mean(k * k, axis=-1, keepdims=True) + EPSILON)
    uq = q * rq; uk = k * rk
    def turn(w):
        return (w * cos + pltpu.roll(w, dh // 2, 1) * sin).astype(BF16)
    return rq, uq, rk, uk, turn(uq * gain_q), turn(uk * gain_k), joined[:, 2 * dh:].astype(BF16)

def probabilities(qr, kr, row_ref, col_ref, dh):
    s = dot_t(qr, kr) * dh ** (-0.5)
    s = jnp.where(row_ref[...] == col_ref[...], s, NEGATIVE)
    p = jnp.exp(s - jnp.max(s, axis=-1, keepdims=True))
    return p / jnp.sum(p, axis=-1, keepdims=True)

def forward_kernel(dh, joined_ref, cos_ref, sin_ref, gain_ref, row_ref, col_ref, *refs):
    o_ref = refs[-1]
    _, _, _, _, qr, kr, v = head_parts(joined_ref[...], cos_ref[...], sin_ref[...], gain_ref[0:1, :], gain_ref[1:2, :], dh)
    p = probabilities(qr, kr, row_ref, col_ref, dh)
    o_ref[...] = dot(p.astype(BF16), v).astype(BF16)

def backward_kernel(dh, joined_ref, do_ref, cos_ref, sin_ref, gain_ref, row_ref, col_ref, *refs):
    d_ref, pair_ref = refs[-2:]
    cos = cos_ref[...]; sin = sin_ref[...]
    gq = gain_ref[0:1, :]; gk = gain_ref[1:2, :]
    rq, uq, rk, uk, qr, kr, v = head_parts(joined_ref[...], cos, sin, gq, gk, dh)
    p = probabilities(qr, kr, row_ref, col_ref, dh)
    do = do_ref[...]
    dp = dot_t(do, v)
    ds = (p * (dp - jnp.sum(p * dp, axis=-1, keepdims=True))).astype(BF16)
    scale = dh ** (-0.5)
    dq = (dot(ds, kr) * scale).astype(BF16).astype(F32)
    dk = (dot_l(ds, qr) * scale).astype(BF16).astype(F32)
    dv = dot_l(p.astype(BF16), do).astype(BF16)
    def back(w):
        return w * cos - pltpu.roll(w, dh // 2, 1) * sin
    def norm_back(up, unit, scaling, gain):
        weighted = up * gain
        return scaling * (weighted - unit * jnp.mean(weighted * unit, axis=-1, keepdims=True))
    nq = back(dq); nk = back(dk)
    d_ref[:, :dh] = norm_back(nq, uq, rq, gq).astype(BF16)
    d_ref[:, dh:2 * dh] = norm_back(nk, uk, rk, gk).astype(BF16)
    d_ref[:, 2 * dh:] = dv
    part = jnp.concatenate([jnp.sum(nq * uq, axis=0, keepdims=True), jnp.sum(nk * uk, axis=0, keepdims=True)], axis=0)
    @pl.when(pl.program_id(0) == 0)
    def _():
        pair_ref[...] = part
    @pl.when(pl.program_id(0) > 0)
    def _():
        pair_ref[...] += part

def attention_specs(tokens, heads, dh, deps):
    fixed = lambda shape: pl.BlockSpec(shape, lambda h: (0, 0))
    return (pl.BlockSpec((tokens, 3 * dh), lambda h: (0, h)), pl.BlockSpec((tokens, dh), lambda h: (0, h)),
            [fixed((tokens, dh)), fixed((tokens, dh)), fixed((2, dh)), fixed((tokens, 1)), fixed((1, tokens))] + [pl.BlockSpec(memory_space=pl.ANY)] * len(deps))

def attention_forward_call(joined, cos, sin, gains, segment, deps, dh=128):
    tokens = joined.shape[0]; heads = joined.shape[1] // (3 * dh)
    three, one, rest = attention_specs(tokens, heads, dh, deps)
    return pl.pallas_call(
        functools.partial(forward_kernel, dh), grid=(heads,), in_specs=[three] + rest, out_specs=one,
        out_shape=jax.ShapeDtypeStruct((tokens, heads * dh), BF16),
        compiler_params=pltpu.CompilerParams(vmem_limit_bytes=40 * 2**20),
        cost_estimate=QUICK,
    )(joined, cos, sin, gains, segment[:, None], segment[None, :], *deps)

def attention_backward_call(joined, grad, cos, sin, gains, segment, deps, dh=128):
    tokens = joined.shape[0]; heads = joined.shape[1] // (3 * dh)
    three, one, rest = attention_specs(tokens, heads, dh, deps)
    return pl.pallas_call(
        functools.partial(backward_kernel, dh), grid=(heads,), in_specs=[three, one] + rest,
        out_specs=[three, pl.BlockSpec((2, dh), lambda h: (0, 0))],
        out_shape=[jax.ShapeDtypeStruct(joined.shape, BF16), jax.ShapeDtypeStruct((2, dh), F32)],
        compiler_params=pltpu.CompilerParams(vmem_limit_bytes=40 * 2**20),
        cost_estimate=QUICK,
    )(joined, grad, cos, sin, gains, segment[:, None], segment[None, :], *deps)


def swap(value, axis, bit):
    return lax.ppermute(value, axis, [(i, i ^ bit) for i in range(lax.axis_size(axis))])


MIDDLE = [(1, 2), (2, 1)]
OUTWARD = [(1, 0), (2, 3)]
INWARD = [(0, 1), (3, 2)]


def scatter_ctx_steps(terms, result):
    (beside,) = yield [swap(terms[2:], "ctx", 1)]
    far = (terms[1].astype(F32) + beside[1].astype(F32)).astype(BF16)
    (across,) = yield [swap(far, "ctx", 2)]
    result.append(terms[0].astype(F32) + beside[0].astype(F32) + across.astype(F32))
    yield from idle()


def gather_ctx_steps(own, blocks):
    across, beside = yield [swap(own, "ctx", 2), swap(own, "ctx", 1)]
    (corner,) = yield [swap(across, "ctx", 1)]
    blocks += [own, across, beside, corner]
    yield from idle()


def line_steps(own, slots, across_dp=None, pause=0):
    place = lax.axis_index("expert")
    middle = (place == 1) | (place == 2)

    def over(block):
        return [] if across_dp is None else [swap(block, "dp", 1)]

    pair, third_mid, *x0 = yield [
        swap(own, "expert", 1),
        lax.ppermute(own, "expert", MIDDLE),
    ] + over(own)
    for _ in range(pause):
        yield []
    second_mid, second_end, *x1 = yield [
        lax.ppermute(pair, "expert", MIDDLE),
        lax.ppermute(third_mid, "expert", OUTWARD),
    ] + over(pair)
    second = jnp.where(middle, second_mid, second_end)
    third_end, *x2 = yield [lax.ppermute(second_mid, "expert", OUTWARD)] + over(second)
    third = jnp.where(middle, third_mid, third_end)
    slots += [own, pair, second, third]
    if across_dp is not None:
        (x3,) = yield over(third)
        across_dp += [x0[0], x1[0], x2[0], x3]
    yield from idle()


def unline_steps(slots, result):
    (three,) = yield [lax.ppermute(slots[3], "expert", INWARD)]
    second = (slots[2].astype(F32) + three.astype(F32)).astype(BF16)
    over, inward = yield [
        lax.ppermute(second, "expert", MIDDLE),
        lax.ppermute(second, "expert", INWARD),
    ]
    first = (slots[1].astype(F32) + over.astype(F32)).astype(BF16)
    third = (slots[3].astype(F32) + inward.astype(F32)).astype(BF16)
    home, pair = yield [lax.ppermute(third, "expert", MIDDLE), swap(first, "expert", 1)]
    result.append(slots[0].astype(F32) + pair.astype(F32) + home.astype(F32))
    yield from idle()


def undp_steps(here, there, result):
    moving = {s: swap(there[s], "dp", 1) for s in (3, 2)}
    (x3,) = yield [moving[3]]
    sum3 = here[3].astype(F32) + x3.astype(F32)
    moving[1] = swap(there[1], "dp", 1)
    x2, three = yield [moving[2], lax.ppermute(sum3.astype(BF16), "expert", INWARD)]
    second = (here[2].astype(F32) + x2.astype(F32) + three.astype(F32)).astype(BF16)
    moving[0] = swap(there[0], "dp", 1)
    x1, over, inward = yield [
        moving[1],
        lax.ppermute(second, "expert", MIDDLE),
        lax.ppermute(second, "expert", INWARD),
    ]
    first = (here[1].astype(F32) + x1.astype(F32) + over.astype(F32)).astype(BF16)
    third = (sum3 + inward.astype(F32)).astype(BF16)
    x0, home, pair = yield [
        moving[0],
        lax.ppermute(third, "expert", MIDDLE),
        swap(first, "expert", 1),
    ]
    result.append(
        here[0].astype(F32) + x0.astype(F32) + pair.astype(F32) + home.astype(F32)
    )
    yield from idle()


def gather_steps(own, groups, plan):
    place = lax.axis_index("expert")
    middle = (place == 1) | (place == 2)
    blocks = [own]
    crossed = [None] * 4

    def across(step):
        return {s: swap(blocks[s], "ctx", 2) for s in range(len(blocks)) if plan[s] == step}

    def note(moving, values):
        for s, value in zip(moving, values):
            crossed[s] = value

    moving = across(0)
    pair, third_mid, *rest = yield [
        swap(own, "expert", 1),
        lax.ppermute(own, "expert", MIDDLE),
    ] + list(moving.values())
    note(moving, rest)
    blocks.append(pair)
    moving = across(1)
    second_mid, second_end, *rest = yield [
        lax.ppermute(pair, "expert", MIDDLE),
        lax.ppermute(third_mid, "expert", OUTWARD),
    ] + list(moving.values())
    note(moving, rest)
    blocks.append(jnp.where(middle, second_mid, second_end))
    moving = across(2)
    third_end, *rest = yield [lax.ppermute(second_mid, "expert", OUTWARD)] + list(moving.values())
    note(moving, rest)
    blocks.append(jnp.where(middle, third_mid, third_end))
    groups[0] = jnp.stack(blocks)
    if plan == (3, 3, 3, 3):
        moving = swap(groups[0], "ctx", 2)
        (groups[1],) = yield [swap(groups[0], "ctx", 1)]
        (groups[2],) = yield [moving]
    else:
        moving = across(3)
        groups[1], *rest = yield [swap(groups[0], "ctx", 1)] + list(moving.values())
        note(moving, rest)
        groups[2] = jnp.stack(crossed)
    (groups[3],) = yield [swap(groups[2], "ctx", 1)]
    yield from idle()


def early_gather_steps(own, groups):
    place = lax.axis_index("expert")
    middle = (place == 1) | (place == 2)
    pair, third_mid, own = yield [
        swap(own, "expert", 1),
        lax.ppermute(own, "expert", MIDDLE),
        own,
    ]
    (y0,) = yield [swap(own, "ctx", 2)]
    (y1,) = yield [swap(pair, "ctx", 2)]
    second_mid, second_end = yield [
        lax.ppermute(pair, "expert", MIDDLE),
        lax.ppermute(third_mid, "expert", OUTWARD),
    ]
    second = jnp.where(middle, second_mid, second_end)
    third_end, y2 = yield [lax.ppermute(second_mid, "expert", OUTWARD), swap(second, "ctx", 2)]
    third = jnp.where(middle, third_mid, third_end)
    groups[0] = jnp.stack([own, pair, second, third])
    y3, groups[1] = yield [swap(third, "ctx", 2), swap(groups[0], "ctx", 1)]
    groups[2] = jnp.stack([y0, y1, y2, y3])
    (groups[3],) = yield [swap(groups[2], "ctx", 1)]
    yield from idle()


def scatter_steps(groups, result, slow=False):
    def slot(values, s):
        return values[..., s, :, :]

    (far,) = yield [swap(groups[3], "ctx", 1)]
    over_y = (groups[2].astype(F32) + far.astype(F32)).astype(BF16)

    def across(s, count=1):
        return [swap(over_y[..., s : s + count, :, :], "ctx", 2)]

    def total(s, moved):
        return slot(groups[0], s).astype(F32) + slot(near, s).astype(F32) + moved.astype(F32)

    def inwards(sum3):
        return lax.ppermute(sum3.astype(BF16), "expert", INWARD)

    if slow:
        y3, near = yield across(3) + [swap(groups[1], "ctx", 1)]
        y3 = slot(y3, 0)
        sum3 = total(3, y3)
        y2, three = yield across(2) + [inwards(sum3)]
        y2 = slot(y2, 0)
        (y1,) = yield across(1)
        y1 = slot(y1, 0)
        moving = across(0)
    else:
        (far_pair,) = yield across(2, 2)
        near_pair, near = yield across(0, 2) + [swap(groups[1], "ctx", 1)]
        y3, y2, y1, y0 = slot(far_pair, 1), slot(far_pair, 0), slot(near_pair, 1), slot(near_pair, 0)
        sum3 = total(3, y3)
        (three,) = yield [inwards(sum3)]
        moving = []
    second = (total(2, y2) + three.astype(F32)).astype(BF16)
    over, inward, *rest = yield [
        lax.ppermute(second, "expert", MIDDLE),
        lax.ppermute(second, "expert", INWARD),
    ] + moving
    y0 = slot(rest[0], 0) if rest else y0
    first = (total(1, y1) + over.astype(F32)).astype(BF16)
    third = (sum3 + inward.astype(F32)).astype(BF16)
    home, pair = yield [lax.ppermute(third, "expert", MIDDLE), swap(first, "expert", 1)]
    result.append(total(0, y0) + pair.astype(F32) + home.astype(F32))
    yield from idle()


def places(index, lengths, block_order):
    blocks = jnp.arange(block_order.shape[0], dtype=jnp.int32)
    holder = (index // BLOCK)[:, None] == blocks[None, :]
    logical = (
        jnp.sum(jnp.where(holder, block_order[None, :], 0), axis=1) * BLOCK + index % BLOCK
    )
    seq_ends = jnp.cumsum(lengths)
    segment = jnp.sum((logical[:, None] >= seq_ends[None, :]).astype(jnp.int32), axis=1)
    starts = seq_ends - lengths
    member = segment[:, None] == jnp.arange(lengths.shape[0], dtype=jnp.int32)[None, :]
    seq_first = jnp.sum(jnp.where(member, starts[None, :], 0), axis=1)
    return (segment, (logical - seq_first).astype(F32))


def rotary_tables(positions, half_size):
    frequency = THETA_BASE ** (-(jnp.arange(half_size, dtype=F32) / half_size))
    angles = positions[:, None] * frequency[None, :]
    cosine, sine = jnp.cos(angles), jnp.sin(angles)
    return jnp.concatenate([cosine, cosine], axis=1), jnp.concatenate([-sine, sine], axis=1)


def norm_back(upstream, unit_rows, scaling, gain_vector):
    weighted = upstream * gain_vector
    return scaling * (weighted - unit_rows * jnp.mean(weighted * unit_rows, axis=-1, keepdims=True))


def row_scale(rows):
    return lax.rsqrt(jnp.mean(rows * rows, axis=-1, keepdims=True) + EPSILON)


def whole_heads(rows, share):
    return lax.axis_size("dp") == HALVES and rows * lax.axis_size("expert") == share


def assemble(pieces, shape):
    d, z = lax.axis_index("dp"), lax.axis_index("expert")
    whole = jnp.zeros(shape, BF16)
    for dx, line in enumerate(pieces):
        for s, piece in enumerate(line):
            whole = lax.dynamic_update_slice(
                whole, piece[None, :, None], (d ^ dx if shape[0] > 1 else 0, 0, z ^ s) + (0,) * (len(shape) - 3)
            )
    return whole


def piece_of(whole, dx, s):
    first = lax.axis_index("dp") ^ dx if whole.shape[0] > 1 else 0
    start = (first, 0, lax.axis_index("expert") ^ s) + (0,) * (whole.ndim - 3)
    return lax.dynamic_slice(whole, start, (1, whole.shape[1], 1) + whole.shape[3:])[0, :, 0]


def join_rows(own, moved):
    first = lax.axis_index("dp") == 0
    return jnp.concatenate([jnp.where(first, own, moved), jnp.where(first, moved, own)])


def sum_rows(whole):
    return lax.psum_scatter(whole, "dp", scatter_dimension=0, tiled=True)


def pack_weights(query_weight, key_weight, value_weight, attention_gain, mixture_gain, query_key_gain, router):
    rows, width = query_weight.shape
    ctx_size = lax.axis_size("ctx")
    share = width // (HALVES * ctx_size)
    stacked = jnp.stack([query_weight, key_weight, value_weight], axis=1)
    stacked = stacked.reshape(rows, 3, HALVES, ctx_size, share // DH, DH)
    stacked = stacked.transpose(3, 0, 2, 4, 1, 5).reshape(ctx_size, rows, 3 * HALVES * share)
    small = jnp.concatenate(
        [
            attention_gain[:, None],
            mixture_gain[:, None],
            jnp.pad(query_key_gain, (0, rows - query_key_gain.shape[0]))[:, None],
            router,
        ],
        axis=1,
    )
    small = jnp.pad(small, ((0, 0), (0, SMALL - small.shape[1])))
    return jnp.concatenate(
        [stacked, jnp.broadcast_to(small[None], (ctx_size, rows, SMALL))], axis=2
    )


def chosen_gates(normed, router, chosen):
    logits = jnp.where(chosen, dot(normed, router), NEGATIVE)
    powers = jnp.where(chosen, jnp.exp(logits - jnp.max(logits, axis=1, keepdims=True)), 0.0)
    return powers / jnp.sum(powers, axis=1, keepdims=True)


def with_gates(normed, gates):
    flat = gates.T.reshape(1, -1)
    high = flat.astype(BF16).astype(F32)
    low = (flat - high).astype(BF16).astype(F32)
    row = lax.broadcasted_iota(jnp.int32, (TAIL, flat.shape[1]), 0)
    tail = jnp.where(row == 0, high, jnp.where(row == 1, low, jnp.where(row == 2, flat - high - low, 0.0)))
    return jnp.concatenate([normed, tail.astype(BF16)])


def body(
    inputs,
    cotangent,
    lengths,
    block_order,
    routes,
    query_weight,
    key_weight,
    value_weight,
    output_weight,
    attention_gain,
    mixture_gain,
    query_key_gain,
    router,
    expert_gate,
    expert_up,
    expert_down,
):
    micro_count, _, tokens, width = inputs.shape
    top = routes.shape[3]
    expert_count = router.shape[1]
    most = tokens * top * 9 // (8 * expert_count) + 2
    capacity = -(-most // 16) * 16
    place = lax.axis_index("ctx")
    rows, few = query_weight.shape[0], query_key_gain.shape[0]
    micros = range(micro_count)

    line = lax.axis_index("expert")
    dp_size = lax.axis_size("dp")
    two = dp_size == 2
    share = width // (HALVES * 4)
    per_ctx = HALVES * share

    slots, slots_dp, blocks = [], [] if two else None, []
    heads_here = whole_heads(rows, share)
    upstream_groups = [None] * 4
    upstream_flow = Flow(early_gather_steps(
            copy_after(cotangent.reshape(-1, width)).reshape(-1, tokens, width), upstream_groups
        ))
    payload = pack_weights(
        query_weight, key_weight, value_weight, attention_gain, mixture_gain, query_key_gain, router
    )
    payload = lax.all_to_all(payload, "ctx", split_axis=0, concat_axis=0, tiled=True)
    if heads_here:
        chunks = output_weight.reshape(rows, 4, width // 4).transpose(1, 0, 2)
        payload = jnp.concatenate([payload, chunks], axis=2)
    spread = Flow(line_steps(payload, slots, slots_dp))
    stream_flow = Flow(
        gather_ctx_steps(copy_after(inputs.reshape(-1, width), payload).reshape(-1, tokens, width), blocks)
    )
    token = turn([spread, upstream_flow])
    token = turn([spread, stream_flow, upstream_flow])
    token = turn([spread, stream_flow, upstream_flow], token)
    copies = [copy_after(own[0], token) for own in (expert_gate, expert_up, expert_down)]
    token = turn([spread, upstream_flow], token, *copies)
    up_moved = [swap(copies[1], "dp", 1)] if two else []
    experts = [
        lax.all_gather(own, "dp", axis=0, tiled=True) for own in copies[: 1 if two else 3]
    ]
    shape = (dp_size, 4, 4) + payload.shape[1:]
    if two:
        packed = assemble([slots, slots_dp], shape)
    else:
        packed = lax.all_gather(
            assemble([slots], (1,) + shape[1:])[0], "dp", axis=0, tiled=False
        )
    if heads_here:
        out_rows = packed[..., 3 * per_ctx + SMALL :].transpose(0, 2, 3, 1, 4).reshape(per_ctx, width)
    packed = packed.reshape(width, -1)
    projections = packed[:, : 3 * per_ctx]
    small = packed[:, 3 * per_ctx : 3 * per_ctx + SMALL].astype(F32)
    gain_one, gain_two = small[:, 0], small[:, 1]
    gain_pair = small[:, 2].reshape(-1, rows)[:, :few].reshape(2, DH)
    router_all = packed[:, 3 * per_ctx + 3 : 3 * per_ctx + 3 + expert_count]

    index = jnp.concatenate(
        [(place ^ s) * tokens + jnp.arange(tokens, dtype=jnp.int32) for s in (0, 2, 1, 3)]
    )
    tables = []
    for m in micros:
        segment, position = places(index, lengths[m, 0], block_order[m, 0])
        tables.append(rotary_tables(position, DH // 2) + (gain_pair, segment))
    stream_all = jnp.concatenate(blocks, axis=1)

    normed_one, units, joined_list, attended_list = [], [], [], []

    def attention(m, token, flows):
        stream = stream_all[m].astype(F32)
        unit = stream * row_scale(stream)
        normed = (unit * gain_one).astype(BF16)
        joined = dot(normed, projections)
        if flows:
            token, (joined,) = turn(flows, token, values=[joined])
        attended = attention_forward_call(joined, *tables[m], [token])
        normed_one.append(normed)
        units.append(unit)
        joined_list.append(joined)
        attended_list.append(attended)
        return attended

    def out_terms_of(m):
        return dot(attended_list[m], out_rows).astype(BF16).reshape(4, tokens, width)

    done = attention(0, token, [])
    if not heads_here:
        out_rows = lax.all_gather(output_weight, ("dp", "ctx", "expert"), axis=0, tiled=True)
        out_rows = out_rows.reshape(HALVES, 4, share, -1)
        out_rows = lax.dynamic_index_in_dim(out_rows, place, 1, keepdims=False)
        out_rows = out_rows.reshape(per_ctx, -1)
    sum_a, sum_b = [], []
    flow_a = Flow(scatter_ctx_steps(out_terms_of(0), sum_a))
    token = turn([flow_a], experts[0])
    done = attention(1, token, [])
    token = turn([flow_a], done)
    flow_b = Flow(scatter_ctx_steps(out_terms_of(1), sum_b))

    normed_two, unit_two, scale_two, gates_own, residuals = [], [], [], [], []

    def route(m, attention_sum):
        residual = inputs[m, 0].astype(F32) + attention_sum
        scale = row_scale(residual)
        unit = residual * scale
        normed = (unit * gain_two).astype(BF16)
        chosen = jnp.any(
            routes[m, 0][..., None] == jnp.arange(expert_count, dtype=jnp.int32), axis=1
        )
        gates = chosen_gates(normed, router_all, chosen)
        residuals.append(residual)
        normed_two.append(normed)
        unit_two.append(unit)
        scale_two.append(scale)
        gates_own.append(gates)
        return with_gates(normed, gates)

    groups = [[None] * 4 for _ in micros]
    gather_a = Flow(gather_steps(route(0, sum_a[0]), groups[0], (3, 3, 3, 3)))
    token, up_moved = turn([flow_b, gather_a, upstream_flow], values=up_moved + [token])
    if two:
        last_moved = [swap(meet([copies[2]], token)[0], "dp", 1)]
        experts.append(join_rows(expert_up[0], up_moved[0]))
    token = turn([gather_a])
    token = turn([gather_a, upstream_flow, flow_b], experts[0], experts[1])
    if two:
        experts.append(join_rows(expert_down[0], last_moved[0]))
    second_payload = route(1, sum_b[0])
    gather_b = Flow(gather_steps(second_payload, groups[1], (1, 1, 2, 3)))

    shared, kept, calls = [None] * 4, None, 0
    back = [[None] * 4 for _ in micros]
    expert_index = place * 4 + line
    order = jnp.stack([expert_index, expert_index * tokens // 512]).astype(jnp.int32)

    def expert(m, k, token, flows):
        nonlocal kept, calls
        shared[k], back[m][k], kept = expert_call(
            order, groups[m][k], upstream_groups[k], tokens, experts, kept, calls, 8, (m, shared[k]), capacity, [token]
        )
        calls += 1
        token, met = turn(flows, values=[shared[k], back[m][k], *kept])
        shared[k], back[m][k], kept = met[0], met[1], met[2:]
        return token

    token = expert(0, 0, token, [gather_a, upstream_flow, gather_b])
    token = expert(0, 1, token, [gather_a, gather_b])
    token = expert(0, 2, token, [gather_a, gather_b])
    token = expert(0, 3, token, [gather_b])
    down_a, down_b, out_sum = [], [], []
    scatter_a = Flow(scatter_steps(back[0], down_a))
    token = expert(1, 2, token, [gather_b, scatter_a])
    token = expert(1, 3, token, [scatter_a])
    scatter_b = Flow(scatter_steps(back[1], down_b))
    token = expert(1, 1, token, [scatter_a, scatter_b])
    token = expert(1, 0, token, [scatter_a, scatter_b])
    rows_in, out_grad, hidden, gate_pre_grad, up_pre_grad = kept
    out_flow = Flow(scatter_steps(shared, out_sum, True))
    down_whole = product_call(hidden, out_grad, [token])
    token, (down_whole,) = turn([scatter_a, scatter_b, out_flow], values=[down_whole])
    down_sum = sum_rows(down_whole)
    gate_whole = product_call(rows_in, gate_pre_grad, [token])
    token, (gate_whole,) = turn([scatter_a, scatter_b, out_flow], values=[gate_whole])

    gate_sum = sum_rows(gate_whole)
    residual_grads, normed_grads, logit_grads = [], [], []

    def residual_back(m, summed):
        gates = gates_own[m]
        gate_value_grad = jnp.sum(summed[tokens:], axis=0).reshape(expert_count, tokens).T
        select_grad = gates * (
            gate_value_grad - jnp.sum(gates * gate_value_grad, axis=1, keepdims=True)
        )
        logit_grad = select_grad.astype(BF16)
        normed_grad = summed[:tokens] + dot_t(logit_grad, router_all)
        residual_grad = cotangent[m, 0].astype(F32) + norm_back(
            normed_grad, unit_two[m], scale_two[m], gain_two
        )
        residual_grads.append(residual_grad)
        normed_grads.append(normed_grad)
        logit_grads.append(logit_grad)
        return residual_grad.astype(BF16)

    branch = [[], []]
    branch_a = Flow(gather_ctx_steps(residual_back(0, down_a[0]), branch[0]))
    up_whole = product_call(rows_in, up_pre_grad, [token])
    token, (up_whole,) = turn([branch_a, scatter_b, out_flow], values=[up_whole])
    up_sum = sum_rows(up_whole)
    token = turn([branch_a])

    joined_grads, normed_one_grads, pair_grads, branch_list = [], [], [], []

    def attention_back(m, token):
        branch_grad = jnp.concatenate(branch[m])
        attended_grad = dot_t(branch_grad, out_rows).astype(BF16)
        joined_grad, pair_part = attention_backward_call(
            joined_list[m], attended_grad, *tables[m], [token]
        )
        branch_list.append(branch_grad)
        joined_grads.append(joined_grad)
        pair_grads.append(pair_part)
        return pair_part

    done = attention_back(0, token)
    token = turn([scatter_b, out_flow], done, down_sum)
    branch_b = Flow(gather_ctx_steps(residual_back(1, down_b[0]), branch[1]))
    normed_one_grads.append(dot_t(joined_grads[0], projections))
    token = turn([branch_b], normed_one_grads[0])
    token = turn([branch_b])
    out_last_sum = []
    out_last = Flow(idle())
    done = attention_back(1, token)
    if heads_here:
        split = sum(dot_l(left, right) for left, right in zip(attended_list, branch_list))
        split = split.astype(BF16).reshape(2, 1, 4, rows, width)
        out_last = Flow(
            unline_steps(
                [jnp.concatenate([piece_of(split, dx, s) for dx in range(2)]) for s in range(4)],
                out_last_sum,
            )
        )
    token = turn([out_flow, out_last], done, gate_sum)
    normed_one_grads.append(dot_t(joined_grads[1], projections))
    attention_gain_grad = sum(
        jnp.sum(grad * unit, axis=0) for grad, unit in zip(normed_one_grads, units)
    )
    mixture_gain_grad = sum(
        jnp.sum(grad * unit, axis=0) for grad, unit in zip(normed_grads, unit_two)
    )
    router_grad = sum(dot_l(left, right) for left, right in zip(normed_two, logit_grads))
    pair_grad = (pair_grads[0] + pair_grads[1]).reshape(-1, few)
    pair_column = jnp.pad(pair_grad, ((0, 0), (0, rows - few))).reshape(-1)
    small_columns = jnp.concatenate(
        [attention_gain_grad[:, None], mixture_gain_grad[:, None], pair_column[:, None], router_grad], axis=1
    )
    small_columns = jnp.pad(small_columns, ((0, 0), (0, SMALL - small_columns.shape[1])))
    terms = jnp.stack(
        [grad.astype(BF16).reshape(4, tokens, width) for grad in normed_one_grads], axis=1
    )

    def gradient_rows(part, parts, deps):
        product = pair_product_call(
            part, parts, normed_one, joined_grads, small_columns.astype(BF16), [], deps
        )
        return product.reshape(dp_size // parts, 4, 4, rows, -1)

    packed_sum, back_sum = [], []
    if two:
        d = lax.axis_index("dp").astype(jnp.int32)
        there = gradient_rows(1 - d, 2, [token])
        there = [piece_of(there, 0, s) for s in range(4)]
        here = gradient_rows(d, 2, there)
        token, (here,) = turn([out_flow, out_last], values=[here])
        last = Flow(
            undp_steps([piece_of(here, 0, s) for s in range(4)], there, packed_sum)
        )
    else:
        whole = gradient_rows(jnp.zeros((), jnp.int32), 1, [token])
        whole = lax.psum_scatter(whole, "dp", scatter_dimension=0, tiled=True)
        token = turn([out_flow, out_last])
        last = Flow(unline_steps([piece_of(whole, 0, s) for s in range(4)], packed_sum))
    token = turn([last, out_last])
    back_flow = Flow(scatter_ctx_steps(terms, back_sum))
    token = turn([last, back_flow, out_last], up_sum)
    if heads_here:
        own_sum, other_sum = out_last_sum[0]
        out_moved = [swap(other_sum.astype(BF16), "dp", 1)]
    else:
        out_moved = []
    token, (gate_sum, up_sum, down_sum) = turn(
        [last, back_flow], token, values=[value.astype(F32) for value in (gate_sum, up_sum, down_sum)]
    )
    if two:
        token, out_moved = turn([last, back_flow], values=out_moved + [token])
    else:
        token = turn([back_flow], token)
    summed = packed_sum[0]
    columns = 3 * per_ctx + SMALL
    swapped = lax.all_to_all(
        summed[..., :columns].astype(BF16), "ctx", split_axis=0, concat_axis=0, tiled=True
    )
    if heads_here:
        out_rows_sum = own_sum + out_moved[0].astype(F32)
    else:
        out_grad_rows = sum(
            dot_l(left, right) for left, right in zip(attended_list, branch_list)
        ).astype(BF16)
        spread_rows = jnp.zeros((HALVES, 4, share, width), BF16)
        spread_rows = lax.dynamic_update_slice_in_dim(
            spread_rows, out_grad_rows.reshape(HALVES, 1, share, width), place, 1
        )
        out_rows_sum = lax.psum_scatter(
            spread_rows.reshape(-1, width), ("dp", "ctx", "expert"), scatter_dimension=0, tiled=True
        ).astype(F32)
    *gradients, small_sums = unpack_call(swapped)
    outputs = [(residuals[m] + out_sum[0][m]).astype(BF16) for m in micros]
    input_grads = []
    for m in micros:
        stream = inputs[m, 0].astype(F32)
        scale_one = row_scale(stream)
        input_grads.append(
            residual_grads[m] + norm_back(back_sum[0][m], stream * scale_one, scale_one, gain_one)
        )
    return (
        jnp.stack(outputs)[:, None],
        jnp.stack(input_grads)[:, None],
        gradients[0],
        gradients[1],
        gradients[2],
        out_rows_sum,
        small_sums[:, 0],
        small_sums[:, 1],
        small_sums[:few, 2],
        small_sums[:, 3 : 3 + expert_count],
        gate_sum[None],
        up_sum[None],
        down_sum[None],
    )


def solution(mesh):
    tokens_4 = P(None, ("dp", "expert"), "ctx", None)
    group = P(None, ("dp", "expert"), None)
    matrix = P(("dp", "ctx", "expert"), None)
    vector = P(("dp", "ctx", "expert"))
    experts = P(("ctx", "expert"), "dp", None)
    return jax.shard_map(
        body,
        mesh=mesh,
        in_specs=(tokens_4, tokens_4, group, group, tokens_4)
        + (matrix,) * 4
        + (vector,) * 3
        + (matrix,)
        + (experts,) * 3,
        out_specs=(tokens_4, tokens_4)
        + (matrix,) * 4
        + (vector,) * 3
        + (matrix,)
        + (experts,) * 3,
        check_vma=False,
    )
```

```python
import functools

import jax
import jax.numpy as jnp
from jax import lax
from jax.experimental import pallas as pl
from jax.experimental.pallas import tpu as pltpu
from jax.sharding import PartitionSpec as P

HEADS = 16
DH = 128
BLOCK = 128
HALVES = 2
SMALL = 128
TAIL = 16

EPSILON = 1e-06
NEGATIVE = -1e30
THETA_BASE = 50000.0
QUICK = pl.CostEstimate(flops=1000, bytes_accessed=1000, transcendentals=0)
F32 = jnp.float32
BF16 = jnp.bfloat16


def dot(a, b):
    return jnp.dot(a, b, preferred_element_type=F32)
def dot_t(a, b):
    return lax.dot_general(a, b, (((1,), (1,)), ((), ())), preferred_element_type=F32)
def dot_l(a, b):
    return lax.dot_general(a, b, (((0,), (0,)), ((), ())), preferred_element_type=F32)

def expert_kernel(
    capacity, tile_f, tile_d, tokens, extra, order_ref, norm_ref, up_ref,
    *refs
):
    counts, extra = extra
    sources = [refs[sum(counts[:i]) : sum(counts[: i + 1])] for i in range(3)]
    refs = refs[sum(counts) :]
    shared_ref, back_ref, rows_ref, dy_ref, h_ref, dhg_ref, dhu_ref = refs[extra : extra + 7]
    ru_ref, gate_rows_ref, sums_ref, slot_ref, wg_ref, wu_ref, wd_ref, arrived = refs[extra + 7 :]
    group, width = norm_ref.shape[0], norm_ref.shape[2]
    first_steps = h_ref.shape[1] // tile_f
    tiles = width // tile_d
    step = pl.program_id(0)
    expert = order_ref[0]
    tail = pl.ds(tokens, TAIL)

    def copies(j):
        at = pl.ds(j * tile_f, tile_f)
        found = []
        for i, whole in enumerate((wg_ref, wu_ref)):
            for half, source in enumerate(sources[i]):
                size = source.shape[0]
                first = ((order_ref[2] + half) % 2) * size if len(sources[i]) > 1 else 0
                to = whole.at[pl.ds(pl.multiple_of(first, size), size), at]
                found.append((source.at[:, at], to, arrived.at[j, 2 * i + half]))
        for half, source in enumerate(sources[2] if j == 0 else ()):
            size = source.shape[0]
            first = ((order_ref[2] + half) % 2) * size if len(sources[2]) > 1 else 0
            to = wd_ref.at[pl.ds(pl.multiple_of(first, size), size), :]
            found.append((source, to, arrived.at[j, 4 + half]))
        return [pltpu.make_async_copy(*each) for each in found]

    def chosen(b):
        slots = lax.broadcasted_iota(jnp.int32, (capacity, tokens), 0).astype(F32)
        return slots == slot_ref[b : b + 1, :]

    @pl.when(step == 0)
    def _():
        for j in range(first_steps):
            for copy in copies(j):
                copy.start()
        lanes = pl.ds(pl.multiple_of(expert * tokens, tokens), tokens)
        gates = jnp.concatenate(
            [
                jnp.sum(norm_ref[b, tail, lanes].astype(F32), axis=0, keepdims=True)
                for b in range(group)
            ],
            axis=0,
        )
        here = gates > 0.0
        shape = (tokens, tokens)
        below = lax.broadcasted_iota(jnp.int32, shape, 0) <= lax.broadcasted_iota(jnp.int32, shape, 1)
        ones = jnp.where(here, 1.0, 0.0)
        counts = dot(
            jnp.concatenate([ones, jnp.zeros((16 - group, tokens), F32)], axis=0).astype(BF16),
            jnp.where(below, 1.0, 0.0).astype(BF16),
        )[:group]
        slot_ref[...] = jnp.where(here, counts - 1.0, -1.0)
        for b in range(group):
            mine = chosen(b)
            hot = jnp.where(mine, 1.0, 0.0).astype(BF16)
            gate_rows = jnp.sum(jnp.where(mine, gates[b : b + 1], 0.0), axis=1, keepdims=True)
            at = pl.ds(b * capacity, capacity)
            rows_ref[at, :] = dot(hot, norm_ref[b, :tokens, :]).astype(BF16)
            up = dot(hot, up_ref[b, 0])
            ru_ref[at, :] = up.astype(BF16)
            dy_ref[at, :] = (gate_rows * up).astype(BF16)
            gate_rows_ref[at, :] = gate_rows
        sums_ref[...] = jnp.zeros_like(sums_ref)

    for j in range(first_steps):
        @pl.when(step == j)
        def _():
            for copy in copies(j):
                copy.wait()

    @pl.when(step < first_steps)
    def _():
        at = pl.ds(pl.multiple_of(step * tile_f, tile_f), tile_f)
        hg = dot(rows_ref[...], wg_ref[:, at])
        hu = dot(rows_ref[...], wu_ref[:, at])
        dh = dot_t(dy_ref[...], wd_ref[at, :])
        sig = jax.nn.sigmoid(hg)
        act = hg * sig
        h_ref[:, at] = (act * hu).astype(BF16)
        dhg_ref[:, at] = (dh * hu * sig * (1.0 + hg * (1.0 - sig))).astype(BF16)
        dhu_ref[:, at] = (dh * act).astype(BF16)

    @pl.when(step >= first_steps)
    def _():
        tile = (step - first_steps + order_ref[1] + 1) % tiles
        at = pl.ds(pl.multiple_of(tile * tile_d, tile_d), tile_d)
        y = dot(h_ref[...], wd_ref[:, at]).astype(BF16).astype(F32)
        sums_ref[...] += jnp.sum(y * ru_ref[:, at].astype(F32), axis=1, keepdims=True)
        gy = (gate_rows_ref[...] * y).astype(BF16)
        dx = (dot_t(dhg_ref[...], wg_ref[at, :]) + dot_t(dhu_ref[...], wu_ref[at, :])).astype(BF16)
        for b in range(group):
            hot = jnp.where(chosen(b), 1.0, 0.0).astype(BF16)
            lo = b * capacity
            shared_ref[0, b] = dot_l(hot, gy[lo : lo + capacity]).astype(BF16)
            back_ref[b, :tokens, :] = dot_l(hot, dx[lo : lo + capacity]).astype(BF16)
            back_ref[b, tail, :] = jnp.zeros((TAIL, tile_d), BF16)

    @pl.when(step == pl.num_programs(0) - 1)
    def _():
        start = (expert % (tile_d // tokens)) * tokens
        lanes = pl.ds(pl.multiple_of(start, tokens), tokens)
        row = lax.broadcasted_iota(jnp.int32, (TAIL, tokens), 0)
        for b in range(group):
            part = sums_ref[pl.ds(b * capacity, capacity), :]
            grad = jnp.sum(jnp.where(chosen(b), part, 0.0), axis=0, keepdims=True)
            high = grad.astype(BF16).astype(F32)
            low = (grad - high).astype(BF16).astype(F32)
            rest = grad - high - low
            packed = jnp.where(row == 0, high, jnp.where(row == 1, low, jnp.where(row == 2, rest, 0.0)))
            back_ref[b, tail, lanes] = packed.astype(BF16)


def expert_call(order, norm, up, tokens, weights, kept, part, parts, shared, capacity, deps, tile_f=512, tile_d=512):
    group, width = norm.shape[0], norm.shape[2]
    hidden = weights[0][0].shape[1]
    counts = [len(parts) for parts in weights]
    flat = [part for parts in weights for part in parts]
    rows = group * capacity
    first_steps = hidden // tile_f
    tiles = width // tile_d
    anywhere = pl.BlockSpec(memory_space=pl.ANY)

    def late(i, o):
        return (jnp.maximum(i - first_steps, 0) + o[1] + 1) % tiles

    def fixed(shape, index=0):
        return pl.BlockSpec(shape, lambda i, o: (index,) + (0,) * (len(shape) - 1))

    def column(shape, place):
        return pl.BlockSpec(shape, lambda i, o: (0,) * (len(shape) - 1) + (place(i, o),))

    micro, shared_in = shared
    shared_in = [] if shared_in is None else [shared_in]
    kept_in = [] if kept is None else list(kept)
    extra = len(deps) + len(shared_in) + len(kept_in)
    sizes = (width, width, hidden, hidden, hidden)
    struct = jax.ShapeDtypeStruct
    results = pl.pallas_call(
        functools.partial(expert_kernel, capacity, tile_f, tile_d, tokens, (counts, extra)),
        grid_spec=pltpu.PrefetchScalarGridSpec(
            num_scalar_prefetch=1,
            grid=(first_steps + tiles,),
            in_specs=[
                fixed(norm.shape),
                pl.BlockSpec((group, 1, tokens, width), lambda i, o: (0, micro, 0, 0)),
            ]
            + [anywhere] * len(flat)
            + [anywhere] * extra,
            out_specs=[
                pl.BlockSpec((1, group, tokens, tile_d), lambda i, o: (micro, 0, 0, late(i, o))),
                column((group, tokens + TAIL, tile_d), late),
            ]
            + [fixed((rows, size), part) for size in sizes],
            scratch_shapes=[
                pltpu.VMEM((rows, width), BF16),
                pltpu.VMEM((rows, 1), F32),
                pltpu.VMEM((rows, 1), F32),
                pltpu.VMEM((group, tokens), F32),
                pltpu.VMEM((width, hidden), BF16),
                pltpu.VMEM((width, hidden), BF16),
                pltpu.VMEM((hidden, width), BF16),
                pltpu.SemaphoreType.DMA((first_steps, 6)),
            ],
        ),
        out_shape=[struct((2, group, tokens, width), BF16), struct((group, tokens + TAIL, width), BF16)]
        + [struct((parts * rows, size), BF16) for size in sizes],
        input_output_aliases={3 + len(flat) + len(deps) + i: i for i in range(len(shared_in))}
        | {3 + len(flat) + len(deps) + len(shared_in) + i: 2 + i for i in range(len(kept_in))},
        compiler_params=pltpu.CompilerParams(vmem_limit_bytes=58 * 2**20),
        cost_estimate=QUICK,
    )(order, norm, up, *flat, *deps, *shared_in, *kept_in)
    return results[0], results[1], results[2:]


def product_kernel(left_ref, right_ref, *refs):
    refs[-1][...] = dot_l(left_ref[...], right_ref[...]).astype(BF16)


def product_call(left, right, deps, tile=512):
    depth, rows = left.shape
    columns = right.shape[1]
    wide = min(columns, 1024)
    return pl.pallas_call(
        product_kernel,
        grid=(columns // wide, rows // tile),
        in_specs=[
            pl.BlockSpec((depth, tile), lambda j, i: (0, i)),
            pl.BlockSpec((depth, wide), lambda j, i: (0, j)),
        ]
        + [pl.BlockSpec(memory_space=pl.ANY)] * len(deps),
        out_specs=pl.BlockSpec((tile, wide), lambda j, i: (i, j)),
        out_shape=jax.ShapeDtypeStruct((rows, columns), BF16),
        compiler_params=pltpu.CompilerParams(vmem_limit_bytes=56 * 2**20),
        cost_estimate=QUICK,
    )(left, right, *deps)


def pair_product_kernel(_, left_a, right_a, left_b, right_b, small_ref, *refs):
    out_ref = refs[-1]
    columns, few = right_a.shape[1], small_ref.shape[1]
    total = dot_l(left_a[...], right_a[...]) + dot_l(left_b[...], right_b[...])
    out_ref[:, :columns] = total.astype(BF16)
    out_ref[:, columns : columns + few] = small_ref[...]
    if out_ref.shape[1] > columns + few:
        attended_a, branch_a, attended_b, branch_b = refs[:4]
        wide = out_ref.shape[1] - columns - few
        tall = attended_a.shape[1]
        for j in range(out_ref.shape[0] // tall):
            at = slice(j * wide, (j + 1) * wide)
            total = dot_l(attended_a[...], branch_a[:, at]) + dot_l(attended_b[...], branch_b[:, at])
            out_ref[j * tall : (j + 1) * tall, columns + few :] = total.astype(BF16)


def pair_product_call(part, parts, lefts, rights, small, others, deps, tile=512):
    depth, rows = lefts[0].shape
    columns, few = rights[0].shape[1], small.shape[1]
    steps = rows // tile // parts

    def place(i, o):
        return o[0] * steps + i

    left = pl.BlockSpec((depth, tile), lambda i, o: (0, place(i, o)))
    right = pl.BlockSpec((depth, columns), lambda i, o: (0, 0))
    other_specs, wide = [], 0
    if others:
        wide = others[1].shape[1] // 4
        other_specs = [
            pl.BlockSpec((depth, tile // 2), lambda i, o: (0, place(i, o) // 2)),
            pl.BlockSpec((depth, 2 * wide), lambda i, o: (0, place(i, o) % 2)),
        ] * 2
    return pl.pallas_call(
        pair_product_kernel,
        grid_spec=pltpu.PrefetchScalarGridSpec(
            num_scalar_prefetch=1,
            grid=(steps,),
            in_specs=[left, right, left, right]
            + [pl.BlockSpec((tile, few), lambda i, o: (place(i, o), 0))]
            + other_specs
            + [pl.BlockSpec(memory_space=pl.ANY)] * len(deps),
            out_specs=pl.BlockSpec((tile, columns + few + wide), lambda i, o: (i, 0)),
        ),
        out_shape=jax.ShapeDtypeStruct((rows // parts, columns + few + wide), BF16),
        compiler_params=pltpu.CompilerParams(vmem_limit_bytes=48 * 2**20),
        cost_estimate=QUICK,
    )(part.reshape(1), lefts[0], rights[0], lefts[1], rights[1], small, *others, *deps)


def unpack_kernel(payload_ref, query_ref, key_ref, value_ref, small_ref):
    ctx_size, _, columns = payload_ref.shape
    heads = (columns - SMALL) // (3 * DH)
    half = heads // HALVES
    for c in range(ctx_size):
        for head in range(heads):
            to = ((head // half) * ctx_size + c) * half + head % half
            for t, ref in enumerate((query_ref, key_ref, value_ref)):
                at = (3 * head + t) * DH
                ref[:, to * DH : (to + 1) * DH] = payload_ref[c, :, at : at + DH].astype(F32)
    small_ref[...] = sum(
        payload_ref[c, :, columns - SMALL :].astype(F32) for c in range(ctx_size)
    )


def unpack_call(payload):
    ctx_size, rows, columns = payload.shape
    width = ctx_size * (columns - SMALL) // 3
    struct = jax.ShapeDtypeStruct
    return pl.pallas_call(
        unpack_kernel,
        out_shape=[struct((rows, width), F32)] * 3 + [struct((rows, SMALL), F32)],
    )(payload)


def nothing_kernel(*refs):
    pass


def meet(values, *deps):
    anywhere = pl.BlockSpec(memory_space=pl.ANY)
    return pl.pallas_call(
        nothing_kernel,
        in_specs=[anywhere] * (len(values) + len(deps)),
        out_specs=[anywhere] * len(values),
        out_shape=[jax.ShapeDtypeStruct(value.shape, value.dtype) for value in values],
        input_output_aliases={i: i for i in range(len(values))},
    )(*values, *deps)


class Flow:
    def __init__(self, steps):
        self.steps = steps
        self.going = next(steps)


def idle():
    while True:
        yield []


def turn(flows, *deps, values=()):
    going = [value for flow in flows for value in flow.going] + list(values)
    deps = [value for value in deps if value is not None]
    met = meet(going, *deps) if going else deps
    token = met[0] if met else None
    for flow in flows:
        count = len(flow.going)
        flow.going = flow.steps.send(list(met[:count]))
        met = met[count:]
    return (token, list(met)) if values else token


def copy_kernel(value_ref, *refs):
    refs[-1][...] = value_ref[...]


def copy_after(value, *deps, tile=256):
    deps = [value for value in deps if value is not None]
    block = pl.BlockSpec((tile, value.shape[1]), lambda i: (i, 0))
    return pl.pallas_call(
        copy_kernel,
        grid=(value.shape[0] // tile,),
        in_specs=[block] + [pl.BlockSpec(memory_space=pl.ANY)] * len(deps),
        out_specs=block,
        out_shape=jax.ShapeDtypeStruct(value.shape, value.dtype),
        compiler_params=pltpu.CompilerParams(vmem_limit_bytes=16 * 2**20),
        cost_estimate=QUICK,
    )(value, *deps)


def head_parts(joined, cos, sin, gain_q, gain_k, dh):
    q = joined[:, :dh]; k = joined[:, dh:2 * dh]
    rq = lax.rsqrt(jnp.mean(q * q, axis=-1, keepdims=True) + EPSILON)
    rk = lax.rsqrt(jnp.mean(k * k, axis=-1, keepdims=True) + EPSILON)
    uq = q * rq; uk = k * rk
    def turn(w):
        return (w * cos + pltpu.roll(w, dh // 2, 1) * sin).astype(BF16)
    return rq, uq, rk, uk, turn(uq * gain_q), turn(uk * gain_k), joined[:, 2 * dh:].astype(BF16)

def probabilities(qr, kr, row_ref, col_ref, dh):
    s = dot_t(qr, kr) * dh ** (-0.5)
    s = jnp.where(row_ref[...] == col_ref[...], s, NEGATIVE)
    p = jnp.exp(s - jnp.max(s, axis=-1, keepdims=True))
    return p / jnp.sum(p, axis=-1, keepdims=True)

def forward_kernel(dh, joined_ref, cos_ref, sin_ref, gain_ref, row_ref, col_ref, *refs):
    o_ref = refs[-1]
    _, _, _, _, qr, kr, v = head_parts(joined_ref[...], cos_ref[...], sin_ref[...], gain_ref[0:1, :], gain_ref[1:2, :], dh)
    p = probabilities(qr, kr, row_ref, col_ref, dh)
    o_ref[...] = dot(p.astype(BF16), v).astype(BF16)

def backward_kernel(dh, joined_ref, do_ref, cos_ref, sin_ref, gain_ref, row_ref, col_ref, *refs):
    d_ref, pair_ref = refs[-2:]
    cos = cos_ref[...]; sin = sin_ref[...]
    gq = gain_ref[0:1, :]; gk = gain_ref[1:2, :]
    rq, uq, rk, uk, qr, kr, v = head_parts(joined_ref[...], cos, sin, gq, gk, dh)
    p = probabilities(qr, kr, row_ref, col_ref, dh)
    do = do_ref[...]
    dp = dot_t(do, v)
    ds = (p * (dp - jnp.sum(p * dp, axis=-1, keepdims=True))).astype(BF16)
    scale = dh ** (-0.5)
    dq = (dot(ds, kr) * scale).astype(BF16).astype(F32)
    dk = (dot_l(ds, qr) * scale).astype(BF16).astype(F32)
    dv = dot_l(p.astype(BF16), do).astype(BF16)
    def back(w):
        return w * cos - pltpu.roll(w, dh // 2, 1) * sin
    def norm_back(up, unit, scaling, gain):
        weighted = up * gain
        return scaling * (weighted - unit * jnp.mean(weighted * unit, axis=-1, keepdims=True))
    nq = back(dq); nk = back(dk)
    d_ref[:, :dh] = norm_back(nq, uq, rq, gq).astype(BF16)
    d_ref[:, dh:2 * dh] = norm_back(nk, uk, rk, gk).astype(BF16)
    d_ref[:, 2 * dh:] = dv
    part = jnp.concatenate([jnp.sum(nq * uq, axis=0, keepdims=True), jnp.sum(nk * uk, axis=0, keepdims=True)], axis=0)
    @pl.when(pl.program_id(0) == 0)
    def _():
        pair_ref[...] = part
    @pl.when(pl.program_id(0) > 0)
    def _():
        pair_ref[...] += part

def attention_specs(tokens, heads, dh, deps):
    fixed = lambda shape: pl.BlockSpec(shape, lambda h: (0, 0))
    return (pl.BlockSpec((tokens, 3 * dh), lambda h: (0, h)), pl.BlockSpec((tokens, dh), lambda h: (0, h)),
            [fixed((tokens, dh)), fixed((tokens, dh)), fixed((2, dh)), fixed((tokens, 1)), fixed((1, tokens))] + [pl.BlockSpec(memory_space=pl.ANY)] * len(deps))

def attention_forward_call(joined, cos, sin, gains, segment, deps, dh=128):
    tokens = joined.shape[0]; heads = joined.shape[1] // (3 * dh)
    three, one, rest = attention_specs(tokens, heads, dh, deps)
    return pl.pallas_call(
        functools.partial(forward_kernel, dh), grid=(heads,), in_specs=[three] + rest, out_specs=one,
        out_shape=jax.ShapeDtypeStruct((tokens, heads * dh), BF16),
        compiler_params=pltpu.CompilerParams(vmem_limit_bytes=40 * 2**20),
        cost_estimate=QUICK,
    )(joined, cos, sin, gains, segment[:, None], segment[None, :], *deps)

def attention_backward_call(joined, grad, cos, sin, gains, segment, deps, dh=128):
    tokens = joined.shape[0]; heads = joined.shape[1] // (3 * dh)
    three, one, rest = attention_specs(tokens, heads, dh, deps)
    return pl.pallas_call(
        functools.partial(backward_kernel, dh), grid=(heads,), in_specs=[three, one] + rest,
        out_specs=[three, pl.BlockSpec((2, dh), lambda h: (0, 0))],
        out_shape=[jax.ShapeDtypeStruct(joined.shape, BF16), jax.ShapeDtypeStruct((2, dh), F32)],
        compiler_params=pltpu.CompilerParams(vmem_limit_bytes=40 * 2**20),
        cost_estimate=QUICK,
    )(joined, grad, cos, sin, gains, segment[:, None], segment[None, :], *deps)


def swap(value, axis, bit):
    return lax.ppermute(value, axis, [(i, i ^ bit) for i in range(lax.axis_size(axis))])


MIDDLE = [(1, 2), (2, 1)]
OUTWARD = [(1, 0), (2, 3)]
INWARD = [(0, 1), (3, 2)]


def scatter_ctx_steps(terms, result):
    (beside,) = yield [swap(terms[2:], "ctx", 1)]
    far = (terms[1].astype(F32) + beside[1].astype(F32)).astype(BF16)
    (across,) = yield [swap(far, "ctx", 2)]
    result.append(terms[0].astype(F32) + beside[0].astype(F32) + across.astype(F32))
    yield from idle()


def gather_ctx_steps(own, blocks):
    across, beside = yield [swap(own, "ctx", 2), swap(own, "ctx", 1)]
    (corner,) = yield [swap(across, "ctx", 1)]
    blocks += [own, across, beside, corner]
    yield from idle()


def line_steps(own, slots, across_dp=None, pause=0):
    place = lax.axis_index("expert")
    middle = (place == 1) | (place == 2)

    def over(block):
        return [] if across_dp is None else [swap(block, "dp", 1)]

    pair, third_mid, *x0 = yield [
        swap(own, "expert", 1),
        lax.ppermute(own, "expert", MIDDLE),
    ] + over(own)
    for _ in range(pause):
        yield []
    second_mid, second_end, *x1 = yield [
        lax.ppermute(pair, "expert", MIDDLE),
        lax.ppermute(third_mid, "expert", OUTWARD),
    ] + over(pair)
    second = jnp.where(middle, second_mid, second_end)
    third_end, *x2 = yield [lax.ppermute(second_mid, "expert", OUTWARD)] + over(second)
    third = jnp.where(middle, third_mid, third_end)
    slots += [own, pair, second, third]
    if across_dp is not None:
        (x3,) = yield over(third)
        across_dp += [x0[0], x1[0], x2[0], x3]
    yield from idle()


def unline_steps(slots, result):
    (three,) = yield [lax.ppermute(slots[3], "expert", INWARD)]
    second = (slots[2].astype(F32) + three.astype(F32)).astype(BF16)
    over, inward = yield [
        lax.ppermute(second, "expert", MIDDLE),
        lax.ppermute(second, "expert", INWARD),
    ]
    first = (slots[1].astype(F32) + over.astype(F32)).astype(BF16)
    third = (slots[3].astype(F32) + inward.astype(F32)).astype(BF16)
    home, pair = yield [lax.ppermute(third, "expert", MIDDLE), swap(first, "expert", 1)]
    result.append(slots[0].astype(F32) + pair.astype(F32) + home.astype(F32))
    yield from idle()


def undp_steps(here, there, result):
    moving = {s: swap(there[s], "dp", 1) for s in (3, 2)}
    (x3,) = yield [moving[3]]
    sum3 = here[3].astype(F32) + x3.astype(F32)
    moving[1] = swap(there[1], "dp", 1)
    x2, three = yield [moving[2], lax.ppermute(sum3.astype(BF16), "expert", INWARD)]
    second = (here[2].astype(F32) + x2.astype(F32) + three.astype(F32)).astype(BF16)
    moving[0] = swap(there[0], "dp", 1)
    x1, over, inward = yield [
        moving[1],
        lax.ppermute(second, "expert", MIDDLE),
        lax.ppermute(second, "expert", INWARD),
    ]
    first = (here[1].astype(F32) + x1.astype(F32) + over.astype(F32)).astype(BF16)
    third = (sum3 + inward.astype(F32)).astype(BF16)
    x0, home, pair = yield [
        moving[0],
        lax.ppermute(third, "expert", MIDDLE),
        swap(first, "expert", 1),
    ]
    result.append(
        here[0].astype(F32) + x0.astype(F32) + pair.astype(F32) + home.astype(F32)
    )
    yield from idle()


def gather_steps(own, groups, plan):
    place = lax.axis_index("expert")
    middle = (place == 1) | (place == 2)
    blocks = [own]
    crossed = [None] * 4

    def across(step):
        return {s: swap(blocks[s], "ctx", 2) for s in range(len(blocks)) if plan[s] == step}

    def note(moving, values):
        for s, value in zip(moving, values):
            crossed[s] = value

    moving = across(0)
    pair, third_mid, *rest = yield [
        swap(own, "expert", 1),
        lax.ppermute(own, "expert", MIDDLE),
    ] + list(moving.values())
    note(moving, rest)
    blocks.append(pair)
    moving = across(1)
    second_mid, second_end, *rest = yield [
        lax.ppermute(pair, "expert", MIDDLE),
        lax.ppermute(third_mid, "expert", OUTWARD),
    ] + list(moving.values())
    note(moving, rest)
    blocks.append(jnp.where(middle, second_mid, second_end))
    moving = across(2)
    third_end, *rest = yield [lax.ppermute(second_mid, "expert", OUTWARD)] + list(moving.values())
    note(moving, rest)
    blocks.append(jnp.where(middle, third_mid, third_end))
    groups[0] = jnp.stack(blocks)
    if plan == (3, 3, 3, 3):
        moving = swap(groups[0], "ctx", 2)
        (groups[1],) = yield [swap(groups[0], "ctx", 1)]
        (groups[2],) = yield [moving]
    else:
        moving = across(3)
        groups[1], *rest = yield [swap(groups[0], "ctx", 1)] + list(moving.values())
        note(moving, rest)
        groups[2] = jnp.stack(crossed)
    (groups[3],) = yield [swap(groups[2], "ctx", 1)]
    yield from idle()


def early_gather_steps(own, groups):
    place = lax.axis_index("expert")
    middle = (place == 1) | (place == 2)
    pair, third_mid, own = yield [
        swap(own, "expert", 1),
        lax.ppermute(own, "expert", MIDDLE),
        own,
    ]
    (y0,) = yield [swap(own, "ctx", 2)]
    (y1,) = yield [swap(pair, "ctx", 2)]
    second_mid, second_end = yield [
        lax.ppermute(pair, "expert", MIDDLE),
        lax.ppermute(third_mid, "expert", OUTWARD),
    ]
    second = jnp.where(middle, second_mid, second_end)
    third_end, y2 = yield [lax.ppermute(second_mid, "expert", OUTWARD), swap(second, "ctx", 2)]
    third = jnp.where(middle, third_mid, third_end)
    groups[0] = jnp.stack([own, pair, second, third])
    y3, groups[1] = yield [swap(third, "ctx", 2), swap(groups[0], "ctx", 1)]
    groups[2] = jnp.stack([y0, y1, y2, y3])
    (groups[3],) = yield [swap(groups[2], "ctx", 1)]
    yield from idle()


def scatter_steps(groups, result, slow=False):
    def slot(values, s):
        return values[..., s, :, :]

    (far,) = yield [swap(groups[3], "ctx", 1)]
    over_y = (groups[2].astype(F32) + far.astype(F32)).astype(BF16)

    def across(s, count=1):
        return [swap(over_y[..., s : s + count, :, :], "ctx", 2)]

    def total(s, moved):
        return slot(groups[0], s).astype(F32) + slot(near, s).astype(F32) + moved.astype(F32)

    def inwards(sum3):
        return lax.ppermute(sum3.astype(BF16), "expert", INWARD)

    if slow:
        y3, near = yield across(3) + [swap(groups[1], "ctx", 1)]
        y3 = slot(y3, 0)
        sum3 = total(3, y3)
        y2, three = yield across(2) + [inwards(sum3)]
        y2 = slot(y2, 0)
        (y1,) = yield across(1)
        y1 = slot(y1, 0)
        moving = across(0)
    else:
        (far_pair,) = yield across(2, 2)
        near_pair, near = yield across(0, 2) + [swap(groups[1], "ctx", 1)]
        y3, y2, y1, y0 = slot(far_pair, 1), slot(far_pair, 0), slot(near_pair, 1), slot(near_pair, 0)
        sum3 = total(3, y3)
        (three,) = yield [inwards(sum3)]
        moving = []
    second = (total(2, y2) + three.astype(F32)).astype(BF16)
    over, inward, *rest = yield [
        lax.ppermute(second, "expert", MIDDLE),
        lax.ppermute(second, "expert", INWARD),
    ] + moving
    y0 = slot(rest[0], 0) if rest else y0
    first = (total(1, y1) + over.astype(F32)).astype(BF16)
    third = (sum3 + inward.astype(F32)).astype(BF16)
    home, pair = yield [lax.ppermute(third, "expert", MIDDLE), swap(first, "expert", 1)]
    result.append(total(0, y0) + pair.astype(F32) + home.astype(F32))
    yield from idle()


def places(index, lengths, block_order):
    blocks = jnp.arange(block_order.shape[0], dtype=jnp.int32)
    holder = (index // BLOCK)[:, None] == blocks[None, :]
    logical = (
        jnp.sum(jnp.where(holder, block_order[None, :], 0), axis=1) * BLOCK + index % BLOCK
    )
    seq_ends = jnp.cumsum(lengths)
    segment = jnp.sum((logical[:, None] >= seq_ends[None, :]).astype(jnp.int32), axis=1)
    starts = seq_ends - lengths
    member = segment[:, None] == jnp.arange(lengths.shape[0], dtype=jnp.int32)[None, :]
    seq_first = jnp.sum(jnp.where(member, starts[None, :], 0), axis=1)
    return (segment, (logical - seq_first).astype(F32))


def rotary_tables(positions, half_size):
    frequency = THETA_BASE ** (-(jnp.arange(half_size, dtype=F32) / half_size))
    angles = positions[:, None] * frequency[None, :]
    cosine, sine = jnp.cos(angles), jnp.sin(angles)
    return jnp.concatenate([cosine, cosine], axis=1), jnp.concatenate([-sine, sine], axis=1)


def norm_back(upstream, unit_rows, scaling, gain_vector):
    weighted = upstream * gain_vector
    return scaling * (weighted - unit_rows * jnp.mean(weighted * unit_rows, axis=-1, keepdims=True))


def row_scale(rows):
    return lax.rsqrt(jnp.mean(rows * rows, axis=-1, keepdims=True) + EPSILON)


def whole_heads(rows, share):
    return lax.axis_size("dp") == HALVES and rows * lax.axis_size("expert") == share


def assemble(pieces, shape):
    d, z = lax.axis_index("dp"), lax.axis_index("expert")
    whole = jnp.zeros(shape, BF16)
    for dx, line in enumerate(pieces):
        for s, piece in enumerate(line):
            whole = lax.dynamic_update_slice(
                whole, piece[None, :, None], (d ^ dx if shape[0] > 1 else 0, 0, z ^ s) + (0,) * (len(shape) - 3)
            )
    return whole


def piece_of(whole, dx, s):
    first = lax.axis_index("dp") ^ dx if whole.shape[0] > 1 else 0
    start = (first, 0, lax.axis_index("expert") ^ s) + (0,) * (whole.ndim - 3)
    return lax.dynamic_slice(whole, start, (1, whole.shape[1], 1) + whole.shape[3:])[0, :, 0]


def sum_rows(whole):
    return lax.psum_scatter(whole, "dp", scatter_dimension=0, tiled=True)


def pack_weights(query_weight, key_weight, value_weight, attention_gain, mixture_gain, query_key_gain, router):
    rows, width = query_weight.shape
    ctx_size = lax.axis_size("ctx")
    share = width // (HALVES * ctx_size)
    stacked = jnp.stack([query_weight, key_weight, value_weight], axis=1)
    stacked = stacked.reshape(rows, 3, HALVES, ctx_size, share // DH, DH)
    stacked = stacked.transpose(3, 0, 2, 4, 1, 5).reshape(ctx_size, rows, 3 * HALVES * share)
    small = jnp.concatenate(
        [
            attention_gain[:, None],
            mixture_gain[:, None],
            jnp.pad(query_key_gain, (0, rows - query_key_gain.shape[0]))[:, None],
            router,
        ],
        axis=1,
    )
    small = jnp.pad(small, ((0, 0), (0, SMALL - small.shape[1])))
    return jnp.concatenate(
        [stacked, jnp.broadcast_to(small[None], (ctx_size, rows, SMALL))], axis=2
    )


def chosen_gates(normed, router, chosen):
    logits = jnp.where(chosen, dot(normed, router), NEGATIVE)
    powers = jnp.where(chosen, jnp.exp(logits - jnp.max(logits, axis=1, keepdims=True)), 0.0)
    return powers / jnp.sum(powers, axis=1, keepdims=True)


def with_gates(normed, gates):
    flat = gates.T.reshape(1, -1)
    high = flat.astype(BF16).astype(F32)
    low = (flat - high).astype(BF16).astype(F32)
    row = lax.broadcasted_iota(jnp.int32, (TAIL, flat.shape[1]), 0)
    tail = jnp.where(row == 0, high, jnp.where(row == 1, low, jnp.where(row == 2, flat - high - low, 0.0)))
    return jnp.concatenate([normed, tail.astype(BF16)])


def body(
    inputs,
    cotangent,
    lengths,
    block_order,
    routes,
    query_weight,
    key_weight,
    value_weight,
    output_weight,
    attention_gain,
    mixture_gain,
    query_key_gain,
    router,
    expert_gate,
    expert_up,
    expert_down,
):
    micro_count, _, tokens, width = inputs.shape
    top = routes.shape[3]
    expert_count = router.shape[1]
    most = tokens * top * 9 // (8 * expert_count) + 2
    capacity = -(-most // 16) * 16
    place = lax.axis_index("ctx")
    rows, few = query_weight.shape[0], query_key_gain.shape[0]
    micros = range(micro_count)

    line = lax.axis_index("expert")
    dp_size = lax.axis_size("dp")
    two = dp_size == 2
    share = width // (HALVES * 4)
    per_ctx = HALVES * share

    slots, slots_dp, blocks = [], [] if two else None, []
    heads_here = whole_heads(rows, share)
    upstream_groups = [None] * 4
    upstream_flow = Flow(early_gather_steps(
            copy_after(cotangent.reshape(-1, width)).reshape(-1, tokens, width), upstream_groups
        ))
    payload = pack_weights(
        query_weight, key_weight, value_weight, attention_gain, mixture_gain, query_key_gain, router
    )
    payload = lax.all_to_all(payload, "ctx", split_axis=0, concat_axis=0, tiled=True)
    if heads_here:
        chunks = output_weight.reshape(rows, 4, width // 4).transpose(1, 0, 2)
        payload = jnp.concatenate([payload, chunks], axis=2)
    spread = Flow(line_steps(payload, slots, slots_dp))
    stream_flow = Flow(
        gather_ctx_steps(copy_after(inputs.reshape(-1, width), payload).reshape(-1, tokens, width), blocks)
    )
    token = turn([spread, upstream_flow])
    token = turn([spread, stream_flow, upstream_flow])
    token = turn([spread, stream_flow, upstream_flow], token)
    copies = [copy_after(own[0], token) for own in (expert_gate, expert_up, expert_down)]
    token = turn([spread, upstream_flow], token, *copies)
    up_moved = [swap(copies[1], "dp", 1)] if two else []
    experts = [
        [lax.all_gather(own, "dp", axis=0, tiled=True)] for own in (copies[::2] if two else copies)
    ]
    shape = (dp_size, 4, 4) + payload.shape[1:]
    if two:
        packed = assemble([slots, slots_dp], shape)
    else:
        packed = lax.all_gather(
            assemble([slots], (1,) + shape[1:])[0], "dp", axis=0, tiled=False
        )
    if heads_here:
        out_rows = packed[..., 3 * per_ctx + SMALL :].transpose(0, 2, 3, 1, 4).reshape(per_ctx, width)
    packed = packed.reshape(width, -1)
    projections = packed[:, : 3 * per_ctx]
    small = packed[:, 3 * per_ctx : 3 * per_ctx + SMALL].astype(F32)
    gain_one, gain_two = small[:, 0], small[:, 1]
    gain_pair = small[:, 2].reshape(-1, rows)[:, :few].reshape(2, DH)
    router_all = packed[:, 3 * per_ctx + 3 : 3 * per_ctx + 3 + expert_count]

    index = jnp.concatenate(
        [(place ^ s) * tokens + jnp.arange(tokens, dtype=jnp.int32) for s in (0, 2, 1, 3)]
    )
    tables = []
    for m in micros:
        segment, position = places(index, lengths[m, 0], block_order[m, 0])
        tables.append(rotary_tables(position, DH // 2) + (gain_pair, segment))
    stream_all = jnp.concatenate(blocks, axis=1)

    normed_one, units, joined_list, attended_list = [], [], [], []

    def attention(m, token, flows):
        stream = stream_all[m].astype(F32)
        unit = stream * row_scale(stream)
        normed = (unit * gain_one).astype(BF16)
        joined = dot(normed, projections)
        if flows:
            token, (joined,) = turn(flows, token, values=[joined])
        attended = attention_forward_call(joined, *tables[m], [token])
        normed_one.append(normed)
        units.append(unit)
        joined_list.append(joined)
        attended_list.append(attended)
        return attended

    def out_terms_of(m):
        return dot(attended_list[m], out_rows).astype(BF16).reshape(4, tokens, width)

    done = attention(0, token, [])
    if not heads_here:
        out_rows = lax.all_gather(output_weight, ("dp", "ctx", "expert"), axis=0, tiled=True)
        out_rows = out_rows.reshape(HALVES, 4, share, -1)
        out_rows = lax.dynamic_index_in_dim(out_rows, place, 1, keepdims=False)
        out_rows = out_rows.reshape(per_ctx, -1)
    sum_a, sum_b = [], []
    flow_a = Flow(scatter_ctx_steps(out_terms_of(0), sum_a))
    token = turn([flow_a], experts[0][0])
    done = attention(1, token, [])
    token = turn([flow_a], done)
    flow_b = Flow(scatter_ctx_steps(out_terms_of(1), sum_b))

    normed_two, unit_two, scale_two, gates_own, residuals = [], [], [], [], []

    def route(m, attention_sum):
        residual = inputs[m, 0].astype(F32) + attention_sum
        scale = row_scale(residual)
        unit = residual * scale
        normed = (unit * gain_two).astype(BF16)
        chosen = jnp.any(
            routes[m, 0][..., None] == jnp.arange(expert_count, dtype=jnp.int32), axis=1
        )
        gates = chosen_gates(normed, router_all, chosen)
        residuals.append(residual)
        normed_two.append(normed)
        unit_two.append(unit)
        scale_two.append(scale)
        gates_own.append(gates)
        return with_gates(normed, gates)

    groups = [[None] * 4 for _ in micros]
    gather_a = Flow(gather_steps(route(0, sum_a[0]), groups[0], (3, 3, 3, 3)))
    token, up_moved = turn([flow_b, gather_a, upstream_flow], values=up_moved + [token])
    if two:
        experts.insert(1, [expert_up[0], up_moved[0]])
    token = turn([gather_a])
    token = turn([gather_a, upstream_flow, flow_b], experts[0][0], experts[2][0])
    second_payload = route(1, sum_b[0])
    gather_b = Flow(gather_steps(second_payload, groups[1], (2, 2, 3, 3)))

    shared, kept, calls = [None] * 4, None, 0
    back = [[None] * 4 for _ in micros]
    expert_index = place * 4 + line
    order = jnp.stack([expert_index, expert_index * tokens // 512, lax.axis_index("dp")])
    order = order.astype(jnp.int32)

    def expert(m, k, token, flows):
        nonlocal kept, calls
        shared[k], back[m][k], kept = expert_call(
            order, groups[m][k], upstream_groups[k], tokens, experts, kept, calls, 8, (m, shared[k]), capacity, [token]
        )
        calls += 1
        token, met = turn(flows, values=[shared[k], back[m][k], *kept])
        shared[k], back[m][k], kept = met[0], met[1], met[2:]
        return token

    token = expert(0, 0, token, [gather_a, upstream_flow, gather_b])
    token = expert(0, 1, token, [gather_a, gather_b])
    token = expert(0, 2, token, [gather_a, gather_b])
    token = expert(0, 3, token, [gather_b])
    down_a, down_b, out_sum = [], [], []
    scatter_a = Flow(scatter_steps(back[0], down_a))
    token = expert(1, 2, token, [gather_b, scatter_a])
    token = expert(1, 3, token, [scatter_a])
    scatter_b = Flow(scatter_steps(back[1], down_b))
    token = expert(1, 1, token, [scatter_a, scatter_b])
    token = expert(1, 0, token, [scatter_a, scatter_b])
    rows_in, out_grad, hidden, gate_pre_grad, up_pre_grad = kept
    out_flow = Flow(scatter_steps(shared, out_sum, True))
    down_whole = product_call(hidden, out_grad, [token])
    token, (down_whole,) = turn([scatter_a, scatter_b, out_flow], values=[down_whole])
    down_sum = sum_rows(down_whole)
    gate_whole = product_call(rows_in, gate_pre_grad, [token])
    token, (gate_whole,) = turn([scatter_a, scatter_b, out_flow], values=[gate_whole])

    gate_sum = sum_rows(gate_whole)
    residual_grads, normed_grads, logit_grads = [], [], []

    def residual_back(m, summed):
        gates = gates_own[m]
        gate_value_grad = jnp.sum(summed[tokens:], axis=0).reshape(expert_count, tokens).T
        select_grad = gates * (
            gate_value_grad - jnp.sum(gates * gate_value_grad, axis=1, keepdims=True)
        )
        logit_grad = select_grad.astype(BF16)
        normed_grad = summed[:tokens] + dot_t(logit_grad, router_all)
        residual_grad = cotangent[m, 0].astype(F32) + norm_back(
            normed_grad, unit_two[m], scale_two[m], gain_two
        )
        residual_grads.append(residual_grad)
        normed_grads.append(normed_grad)
        logit_grads.append(logit_grad)
        return residual_grad.astype(BF16)

    branch = [[], []]
    branch_a = Flow(gather_ctx_steps(residual_back(0, down_a[0]), branch[0]))
    up_whole = product_call(rows_in, up_pre_grad, [token])
    token, (up_whole,) = turn([branch_a, scatter_b, out_flow], values=[up_whole])
    up_sum = sum_rows(up_whole)
    token = turn([branch_a])

    joined_grads, normed_one_grads, pair_grads, branch_list = [], [], [], []

    def attention_back(m, token):
        branch_grad = jnp.concatenate(branch[m])
        attended_grad = dot_t(branch_grad, out_rows).astype(BF16)
        joined_grad, pair_part = attention_backward_call(
            joined_list[m], attended_grad, *tables[m], [token]
        )
        branch_list.append(branch_grad)
        joined_grads.append(joined_grad)
        pair_grads.append(pair_part)
        return pair_part

    done = attention_back(0, token)
    token = turn([scatter_b, out_flow], done, down_sum)
    branch_b = Flow(gather_ctx_steps(residual_back(1, down_b[0]), branch[1]))
    normed_one_grads.append(dot_t(joined_grads[0], projections))
    token = turn([branch_b], normed_one_grads[0])
    token = turn([branch_b])
    out_last_sum = []
    out_last = Flow(idle())
    done = attention_back(1, token)
    if heads_here:
        split = sum(dot_l(left, right) for left, right in zip(attended_list, branch_list))
        split = split.astype(BF16).reshape(2, 1, 4, rows, width)
        out_last = Flow(
            unline_steps(
                [jnp.concatenate([piece_of(split, dx, s) for dx in range(2)]) for s in range(4)],
                out_last_sum,
            )
        )
    token = turn([out_flow, out_last], done, gate_sum)
    normed_one_grads.append(dot_t(joined_grads[1], projections))
    attention_gain_grad = sum(
        jnp.sum(grad * unit, axis=0) for grad, unit in zip(normed_one_grads, units)
    )
    mixture_gain_grad = sum(
        jnp.sum(grad * unit, axis=0) for grad, unit in zip(normed_grads, unit_two)
    )
    router_grad = sum(dot_l(left, right) for left, right in zip(normed_two, logit_grads))
    pair_grad = (pair_grads[0] + pair_grads[1]).reshape(-1, few)
    pair_column = jnp.pad(pair_grad, ((0, 0), (0, rows - few))).reshape(-1)
    small_columns = jnp.concatenate(
        [attention_gain_grad[:, None], mixture_gain_grad[:, None], pair_column[:, None], router_grad], axis=1
    )
    small_columns = jnp.pad(small_columns, ((0, 0), (0, SMALL - small_columns.shape[1])))
    terms = jnp.stack(
        [grad.astype(BF16).reshape(4, tokens, width) for grad in normed_one_grads], axis=1
    )

    def gradient_rows(part, parts, deps):
        product = pair_product_call(
            part, parts, normed_one, joined_grads, small_columns.astype(BF16), [], deps
        )
        return product.reshape(dp_size // parts, 4, 4, rows, -1)

    packed_sum, back_sum = [], []
    if two:
        d = lax.axis_index("dp").astype(jnp.int32)
        there = gradient_rows(1 - d, 2, [token])
        there = [piece_of(there, 0, s) for s in range(4)]
        here = gradient_rows(d, 2, there)
        token, (here,) = turn([out_flow, out_last], values=[here])
        last = Flow(
            undp_steps([piece_of(here, 0, s) for s in range(4)], there, packed_sum)
        )
    else:
        whole = gradient_rows(jnp.zeros((), jnp.int32), 1, [token])
        whole = lax.psum_scatter(whole, "dp", scatter_dimension=0, tiled=True)
        token = turn([out_flow, out_last])
        last = Flow(unline_steps([piece_of(whole, 0, s) for s in range(4)], packed_sum))
    token = turn([last, out_last])
    back_flow = Flow(scatter_ctx_steps(terms, back_sum))
    token = turn([last, back_flow, out_last], up_sum)
    if heads_here:
        own_sum, other_sum = out_last_sum[0]
        out_moved = [swap(other_sum.astype(BF16), "dp", 1)]
    else:
        out_moved = []
    token, (gate_sum, up_sum, down_sum) = turn(
        [last, back_flow], token, values=[value.astype(F32) for value in (gate_sum, up_sum, down_sum)]
    )
    if two:
        token, out_moved = turn([last, back_flow], values=out_moved + [token])
    else:
        token = turn([back_flow], token)
    summed = packed_sum[0]
    columns = 3 * per_ctx + SMALL
    swapped = lax.all_to_all(
        summed[..., :columns].astype(BF16), "ctx", split_axis=0, concat_axis=0, tiled=True
    )
    if heads_here:
        out_rows_sum = own_sum + out_moved[0].astype(F32)
    else:
        out_grad_rows = sum(
            dot_l(left, right) for left, right in zip(attended_list, branch_list)
        ).astype(BF16)
        spread_rows = jnp.zeros((HALVES, 4, share, width), BF16)
        spread_rows = lax.dynamic_update_slice_in_dim(
            spread_rows, out_grad_rows.reshape(HALVES, 1, share, width), place, 1
        )
        out_rows_sum = lax.psum_scatter(
            spread_rows.reshape(-1, width), ("dp", "ctx", "expert"), scatter_dimension=0, tiled=True
        ).astype(F32)
    *gradients, small_sums = unpack_call(swapped)
    outputs = [(residuals[m] + out_sum[0][m]).astype(BF16) for m in micros]
    input_grads = []
    for m in micros:
        stream = inputs[m, 0].astype(F32)
        scale_one = row_scale(stream)
        input_grads.append(
            residual_grads[m] + norm_back(back_sum[0][m], stream * scale_one, scale_one, gain_one)
        )
    return (
        jnp.stack(outputs)[:, None],
        jnp.stack(input_grads)[:, None],
        gradients[0],
        gradients[1],
        gradients[2],
        out_rows_sum,
        small_sums[:, 0],
        small_sums[:, 1],
        small_sums[:few, 2],
        small_sums[:, 3 : 3 + expert_count],
        gate_sum[None],
        up_sum[None],
        down_sum[None],
    )


def solution(mesh):
    tokens_4 = P(None, ("dp", "expert"), "ctx", None)
    group = P(None, ("dp", "expert"), None)
    matrix = P(("dp", "ctx", "expert"), None)
    vector = P(("dp", "ctx", "expert"))
    experts = P(("ctx", "expert"), "dp", None)
    return jax.shard_map(
        body,
        mesh=mesh,
        in_specs=(tokens_4, tokens_4, group, group, tokens_4)
        + (matrix,) * 4
        + (vector,) * 3
        + (matrix,)
        + (experts,) * 3,
        out_specs=(tokens_4, tokens_4)
        + (matrix,) * 4
        + (vector,) * 3
        + (matrix,)
        + (experts,) * 3,
        check_vma=False,
    )
```

```python
import functools

import jax
import jax.numpy as jnp
from jax import lax
from jax.experimental import pallas as pl
from jax.experimental.pallas import tpu as pltpu
from jax.sharding import PartitionSpec as P

HEADS = 16
DH = 128
BLOCK = 128
HALVES = 2
SMALL = 128
TAIL = 16

EPSILON = 1e-06
NEGATIVE = -1e30
THETA_BASE = 50000.0
QUICK = pl.CostEstimate(flops=1000, bytes_accessed=1000, transcendentals=0)
F32 = jnp.float32
BF16 = jnp.bfloat16


def dot(a, b):
    return jnp.dot(a, b, preferred_element_type=F32)
def dot_t(a, b):
    return lax.dot_general(a, b, (((1,), (1,)), ((), ())), preferred_element_type=F32)
def dot_l(a, b):
    return lax.dot_general(a, b, (((0,), (0,)), ((), ())), preferred_element_type=F32)

def expert_kernel(
    capacity, tile_f, tile_d, tokens, extra, order_ref, norm_ref, up_ref,
    *refs
):
    counts, extra = extra
    sources = [refs[sum(counts[:i]) : sum(counts[: i + 1])] for i in range(3)]
    refs = refs[sum(counts) :]
    shared_ref, back_ref, rows_ref, dy_ref, h_ref, dhg_ref, dhu_ref = refs[extra : extra + 7]
    ru_ref, gate_rows_ref, sums_ref, slot_ref, wg_ref, wu_ref, wd_ref, arrived = refs[extra + 7 :]
    group, width = norm_ref.shape[0], norm_ref.shape[2]
    first_steps = h_ref.shape[1] // tile_f
    tiles = width // tile_d
    step = pl.program_id(0)
    expert = order_ref[0]
    tail = pl.ds(tokens, TAIL)

    def copies(j):
        at = pl.ds(j * tile_f, tile_f)
        found = []
        for i, whole in enumerate((wg_ref, wu_ref)):
            for half, source in enumerate(sources[i]):
                size = source.shape[0]
                first = ((order_ref[2] + half) % 2) * size if len(sources[i]) > 1 else 0
                to = whole.at[pl.ds(pl.multiple_of(first, size), size), at]
                found.append((source.at[:, at], to, arrived.at[j, 2 * i + half]))
        for half, source in enumerate(sources[2] if j == 0 else ()):
            size = source.shape[0]
            first = ((order_ref[2] + half) % 2) * size if len(sources[2]) > 1 else 0
            to = wd_ref.at[pl.ds(pl.multiple_of(first, size), size), :]
            found.append((source, to, arrived.at[j, 4 + half]))
        return [pltpu.make_async_copy(*each) for each in found]

    def chosen(b):
        slots = lax.broadcasted_iota(jnp.int32, (capacity, tokens), 0).astype(F32)
        return slots == slot_ref[b : b + 1, :]

    @pl.when(step == 0)
    def _():
        for j in range(first_steps):
            for copy in copies(j):
                copy.start()
        lanes = pl.ds(pl.multiple_of(expert * tokens, tokens), tokens)
        gates = jnp.concatenate(
            [
                jnp.sum(norm_ref[b, tail, lanes].astype(F32), axis=0, keepdims=True)
                for b in range(group)
            ],
            axis=0,
        )
        here = gates > 0.0
        shape = (tokens, tokens)
        below = lax.broadcasted_iota(jnp.int32, shape, 0) <= lax.broadcasted_iota(jnp.int32, shape, 1)
        ones = jnp.where(here, 1.0, 0.0)
        counts = dot(
            jnp.concatenate([ones, jnp.zeros((16 - group, tokens), F32)], axis=0).astype(BF16),
            jnp.where(below, 1.0, 0.0).astype(BF16),
        )[:group]
        slot_ref[...] = jnp.where(here, counts - 1.0, -1.0)
        for b in range(group):
            mine = chosen(b)
            hot = jnp.where(mine, 1.0, 0.0).astype(BF16)
            gate_rows = jnp.sum(jnp.where(mine, gates[b : b + 1], 0.0), axis=1, keepdims=True)
            at = pl.ds(b * capacity, capacity)
            rows_ref[at, :] = dot(hot, norm_ref[b, :tokens, :]).astype(BF16)
            up = dot(hot, up_ref[b, 0])
            ru_ref[at, :] = up.astype(BF16)
            dy_ref[at, :] = (gate_rows * up).astype(BF16)
            gate_rows_ref[at, :] = gate_rows
        sums_ref[...] = jnp.zeros_like(sums_ref)

    for j in range(first_steps):
        @pl.when(step == j)
        def _():
            for copy in copies(j):
                copy.wait()

    @pl.when(step < first_steps)
    def _():
        at = pl.ds(pl.multiple_of(step * tile_f, tile_f), tile_f)
        hg = dot(rows_ref[...], wg_ref[:, at])
        hu = dot(rows_ref[...], wu_ref[:, at])
        dh = dot_t(dy_ref[...], wd_ref[at, :])
        sig = jax.nn.sigmoid(hg)
        act = hg * sig
        h_ref[:, at] = (act * hu).astype(BF16)
        dhg_ref[:, at] = (dh * hu * sig * (1.0 + hg * (1.0 - sig))).astype(BF16)
        dhu_ref[:, at] = (dh * act).astype(BF16)

    @pl.when(step >= first_steps)
    def _():
        tile = (step - first_steps + order_ref[1] + 1) % tiles
        at = pl.ds(pl.multiple_of(tile * tile_d, tile_d), tile_d)
        y = dot(h_ref[...], wd_ref[:, at]).astype(BF16).astype(F32)
        sums_ref[...] += jnp.sum(y * ru_ref[:, at].astype(F32), axis=1, keepdims=True)
        gy = (gate_rows_ref[...] * y).astype(BF16)
        dx = (dot_t(dhg_ref[...], wg_ref[at, :]) + dot_t(dhu_ref[...], wu_ref[at, :])).astype(BF16)
        for b in range(group):
            hot = jnp.where(chosen(b), 1.0, 0.0).astype(BF16)
            lo = b * capacity
            shared_ref[0, b] = dot_l(hot, gy[lo : lo + capacity]).astype(BF16)
            back_ref[b, :tokens, :] = dot_l(hot, dx[lo : lo + capacity]).astype(BF16)
            back_ref[b, tail, :] = jnp.zeros((TAIL, tile_d), BF16)

    @pl.when(step == pl.num_programs(0) - 1)
    def _():
        start = (expert % (tile_d // tokens)) * tokens
        lanes = pl.ds(pl.multiple_of(start, tokens), tokens)
        row = lax.broadcasted_iota(jnp.int32, (TAIL, tokens), 0)
        for b in range(group):
            part = sums_ref[pl.ds(b * capacity, capacity), :]
            grad = jnp.sum(jnp.where(chosen(b), part, 0.0), axis=0, keepdims=True)
            high = grad.astype(BF16).astype(F32)
            low = (grad - high).astype(BF16).astype(F32)
            rest = grad - high - low
            packed = jnp.where(row == 0, high, jnp.where(row == 1, low, jnp.where(row == 2, rest, 0.0)))
            back_ref[b, tail, lanes] = packed.astype(BF16)


def expert_call(order, norm, up, tokens, weights, kept, part, parts, shared, capacity, deps, tile_f=512, tile_d=512):
    group, width = norm.shape[0], norm.shape[2]
    hidden = weights[0][0].shape[1]
    counts = [len(parts) for parts in weights]
    flat = [part for parts in weights for part in parts]
    rows = group * capacity
    first_steps = hidden // tile_f
    tiles = width // tile_d
    anywhere = pl.BlockSpec(memory_space=pl.ANY)

    def late(i, o):
        return (jnp.maximum(i - first_steps, 0) + o[1] + 1) % tiles

    def fixed(shape, index=0):
        return pl.BlockSpec(shape, lambda i, o: (index,) + (0,) * (len(shape) - 1))

    def column(shape, place):
        return pl.BlockSpec(shape, lambda i, o: (0,) * (len(shape) - 1) + (place(i, o),))

    micro, shared_in = shared
    shared_in = [] if shared_in is None else [shared_in]
    kept_in = [] if kept is None else list(kept)
    extra = len(deps) + len(shared_in) + len(kept_in)
    sizes = (width, width, hidden, hidden, hidden)
    struct = jax.ShapeDtypeStruct
    results = pl.pallas_call(
        functools.partial(expert_kernel, capacity, tile_f, tile_d, tokens, (counts, extra)),
        grid_spec=pltpu.PrefetchScalarGridSpec(
            num_scalar_prefetch=1,
            grid=(first_steps + tiles,),
            in_specs=[
                fixed(norm.shape),
                pl.BlockSpec((group, 1, tokens, width), lambda i, o: (0, micro, 0, 0)),
            ]
            + [anywhere] * len(flat)
            + [anywhere] * extra,
            out_specs=[
                pl.BlockSpec((1, group, tokens, tile_d), lambda i, o: (micro, 0, 0, late(i, o))),
                column((group, tokens + TAIL, tile_d), late),
            ]
            + [fixed((rows, size), part) for size in sizes],
            scratch_shapes=[
                pltpu.VMEM((rows, width), BF16),
                pltpu.VMEM((rows, 1), F32),
                pltpu.VMEM((rows, 1), F32),
                pltpu.VMEM((group, tokens), F32),
                pltpu.VMEM((width, hidden), BF16),
                pltpu.VMEM((width, hidden), BF16),
                pltpu.VMEM((hidden, width), BF16),
                pltpu.SemaphoreType.DMA((first_steps, 6)),
            ],
        ),
        out_shape=[struct((2, group, tokens, width), BF16), struct((group, tokens + TAIL, width), BF16)]
        + [struct((parts * rows, size), BF16) for size in sizes],
        input_output_aliases={3 + len(flat) + len(deps) + i: i for i in range(len(shared_in))}
        | {3 + len(flat) + len(deps) + len(shared_in) + i: 2 + i for i in range(len(kept_in))},
        compiler_params=pltpu.CompilerParams(vmem_limit_bytes=58 * 2**20),
        cost_estimate=QUICK,
    )(order, norm, up, *flat, *deps, *shared_in, *kept_in)
    return results[0], results[1], results[2:]


def product_kernel(left_ref, right_ref, *refs):
    refs[-1][...] = dot_l(left_ref[...], right_ref[...]).astype(BF16)


def product_call(left, right, deps, tile=512):
    depth, rows = left.shape
    columns = right.shape[1]
    wide = min(columns, 1024)
    return pl.pallas_call(
        product_kernel,
        grid=(columns // wide, rows // tile),
        in_specs=[
            pl.BlockSpec((depth, tile), lambda j, i: (0, i)),
            pl.BlockSpec((depth, wide), lambda j, i: (0, j)),
        ]
        + [pl.BlockSpec(memory_space=pl.ANY)] * len(deps),
        out_specs=pl.BlockSpec((tile, wide), lambda j, i: (i, j)),
        out_shape=jax.ShapeDtypeStruct((rows, columns), BF16),
        compiler_params=pltpu.CompilerParams(vmem_limit_bytes=56 * 2**20),
        cost_estimate=QUICK,
    )(left, right, *deps)


def pair_product_kernel(_, left_a, right_a, left_b, right_b, small_ref, *refs):
    out_ref = refs[-1]
    columns, few = right_a.shape[1], small_ref.shape[1]
    total = dot_l(left_a[...], right_a[...]) + dot_l(left_b[...], right_b[...])
    out_ref[:, :columns] = total.astype(BF16)
    out_ref[:, columns : columns + few] = small_ref[...]
    if out_ref.shape[1] > columns + few:
        attended_a, branch_a, attended_b, branch_b = refs[:4]
        wide = out_ref.shape[1] - columns - few
        tall = attended_a.shape[1]
        for j in range(out_ref.shape[0] // tall):
            at = slice(j * wide, (j + 1) * wide)
            total = dot_l(attended_a[...], branch_a[:, at]) + dot_l(attended_b[...], branch_b[:, at])
            out_ref[j * tall : (j + 1) * tall, columns + few :] = total.astype(BF16)


def pair_product_call(part, parts, lefts, rights, small, others, deps, tile=512):
    depth, rows = lefts[0].shape
    columns, few = rights[0].shape[1], small.shape[1]
    steps = rows // tile // parts

    def place(i, o):
        return o[0] * steps + i

    left = pl.BlockSpec((depth, tile), lambda i, o: (0, place(i, o)))
    right = pl.BlockSpec((depth, columns), lambda i, o: (0, 0))
    other_specs, wide = [], 0
    if others:
        wide = others[1].shape[1] // 4
        other_specs = [
            pl.BlockSpec((depth, tile // 2), lambda i, o: (0, place(i, o) // 2)),
            pl.BlockSpec((depth, 2 * wide), lambda i, o: (0, place(i, o) % 2)),
        ] * 2
    return pl.pallas_call(
        pair_product_kernel,
        grid_spec=pltpu.PrefetchScalarGridSpec(
            num_scalar_prefetch=1,
            grid=(steps,),
            in_specs=[left, right, left, right]
            + [pl.BlockSpec((tile, few), lambda i, o: (place(i, o), 0))]
            + other_specs
            + [pl.BlockSpec(memory_space=pl.ANY)] * len(deps),
            out_specs=pl.BlockSpec((tile, columns + few + wide), lambda i, o: (i, 0)),
        ),
        out_shape=jax.ShapeDtypeStruct((rows // parts, columns + few + wide), BF16),
        compiler_params=pltpu.CompilerParams(vmem_limit_bytes=48 * 2**20),
        cost_estimate=QUICK,
    )(part.reshape(1), lefts[0], rights[0], lefts[1], rights[1], small, *others, *deps)


def unpack_kernel(payload_ref, query_ref, key_ref, value_ref, small_ref):
    ctx_size, _, columns = payload_ref.shape
    heads = (columns - SMALL) // (3 * DH)
    half = heads // HALVES
    for c in range(ctx_size):
        for head in range(heads):
            to = ((head // half) * ctx_size + c) * half + head % half
            for t, ref in enumerate((query_ref, key_ref, value_ref)):
                at = (3 * head + t) * DH
                ref[:, to * DH : (to + 1) * DH] = payload_ref[c, :, at : at + DH].astype(F32)
    small_ref[...] = sum(
        payload_ref[c, :, columns - SMALL :].astype(F32) for c in range(ctx_size)
    )


def unpack_call(payload):
    ctx_size, rows, columns = payload.shape
    width = ctx_size * (columns - SMALL) // 3
    struct = jax.ShapeDtypeStruct
    return pl.pallas_call(
        unpack_kernel,
        out_shape=[struct((rows, width), F32)] * 3 + [struct((rows, SMALL), F32)],
    )(payload)


def nothing_kernel(*refs):
    pass


def meet(values, *deps):
    anywhere = pl.BlockSpec(memory_space=pl.ANY)
    return pl.pallas_call(
        nothing_kernel,
        in_specs=[anywhere] * (len(values) + len(deps)),
        out_specs=[anywhere] * len(values),
        out_shape=[jax.ShapeDtypeStruct(value.shape, value.dtype) for value in values],
        input_output_aliases={i: i for i in range(len(values))},
    )(*values, *deps)


class Flow:
    def __init__(self, steps):
        self.steps = steps
        self.going = next(steps)


def idle():
    while True:
        yield []


def turn(flows, *deps, values=()):
    going = [value for flow in flows for value in flow.going] + list(values)
    deps = [value for value in deps if value is not None]
    met = meet(going, *deps) if going else deps
    token = met[0] if met else None
    for flow in flows:
        count = len(flow.going)
        flow.going = flow.steps.send(list(met[:count]))
        met = met[count:]
    return (token, list(met)) if values else token


def copy_kernel(value_ref, *refs):
    refs[-1][...] = value_ref[...]


def copy_after(value, *deps, tile=256):
    deps = [value for value in deps if value is not None]
    block = pl.BlockSpec((tile, value.shape[1]), lambda i: (i, 0))
    return pl.pallas_call(
        copy_kernel,
        grid=(value.shape[0] // tile,),
        in_specs=[block] + [pl.BlockSpec(memory_space=pl.ANY)] * len(deps),
        out_specs=block,
        out_shape=jax.ShapeDtypeStruct(value.shape, value.dtype),
        compiler_params=pltpu.CompilerParams(vmem_limit_bytes=16 * 2**20),
        cost_estimate=QUICK,
    )(value, *deps)


def head_parts(joined, cos, sin, gain_q, gain_k, dh):
    q = joined[:, :dh]; k = joined[:, dh:2 * dh]
    rq = lax.rsqrt(jnp.mean(q * q, axis=-1, keepdims=True) + EPSILON)
    rk = lax.rsqrt(jnp.mean(k * k, axis=-1, keepdims=True) + EPSILON)
    uq = q * rq; uk = k * rk
    def turn(w):
        return (w * cos + pltpu.roll(w, dh // 2, 1) * sin).astype(BF16)
    return rq, uq, rk, uk, turn(uq * gain_q), turn(uk * gain_k), joined[:, 2 * dh:].astype(BF16)

def probabilities(qr, kr, row_ref, col_ref, dh):
    s = dot_t(qr, kr) * dh ** (-0.5)
    s = jnp.where(row_ref[...] == col_ref[...], s, NEGATIVE)
    p = jnp.exp(s - jnp.max(s, axis=-1, keepdims=True))
    return p / jnp.sum(p, axis=-1, keepdims=True)

def forward_kernel(dh, joined_ref, cos_ref, sin_ref, gain_ref, row_ref, col_ref, *refs):
    o_ref = refs[-1]
    _, _, _, _, qr, kr, v = head_parts(joined_ref[...], cos_ref[...], sin_ref[...], gain_ref[0:1, :], gain_ref[1:2, :], dh)
    p = probabilities(qr, kr, row_ref, col_ref, dh)
    o_ref[...] = dot(p.astype(BF16), v).astype(BF16)

def backward_kernel(dh, joined_ref, do_ref, cos_ref, sin_ref, gain_ref, row_ref, col_ref, *refs):
    d_ref, pair_ref = refs[-2:]
    cos = cos_ref[...]; sin = sin_ref[...]
    gq = gain_ref[0:1, :]; gk = gain_ref[1:2, :]
    rq, uq, rk, uk, qr, kr, v = head_parts(joined_ref[...], cos, sin, gq, gk, dh)
    p = probabilities(qr, kr, row_ref, col_ref, dh)
    do = do_ref[...]
    dp = dot_t(do, v)
    ds = (p * (dp - jnp.sum(p * dp, axis=-1, keepdims=True))).astype(BF16)
    scale = dh ** (-0.5)
    dq = (dot(ds, kr) * scale).astype(BF16).astype(F32)
    dk = (dot_l(ds, qr) * scale).astype(BF16).astype(F32)
    dv = dot_l(p.astype(BF16), do).astype(BF16)
    def back(w):
        return w * cos - pltpu.roll(w, dh // 2, 1) * sin
    def norm_back(up, unit, scaling, gain):
        weighted = up * gain
        return scaling * (weighted - unit * jnp.mean(weighted * unit, axis=-1, keepdims=True))
    nq = back(dq); nk = back(dk)
    d_ref[:, :dh] = norm_back(nq, uq, rq, gq).astype(BF16)
    d_ref[:, dh:2 * dh] = norm_back(nk, uk, rk, gk).astype(BF16)
    d_ref[:, 2 * dh:] = dv
    part = jnp.concatenate([jnp.sum(nq * uq, axis=0, keepdims=True), jnp.sum(nk * uk, axis=0, keepdims=True)], axis=0)
    @pl.when(pl.program_id(0) == 0)
    def _():
        pair_ref[...] = part
    @pl.when(pl.program_id(0) > 0)
    def _():
        pair_ref[...] += part

def attention_specs(tokens, heads, dh, deps):
    fixed = lambda shape: pl.BlockSpec(shape, lambda h: (0, 0))
    return (pl.BlockSpec((tokens, 3 * dh), lambda h: (0, h)), pl.BlockSpec((tokens, dh), lambda h: (0, h)),
            [fixed((tokens, dh)), fixed((tokens, dh)), fixed((2, dh)), fixed((tokens, 1)), fixed((1, tokens))] + [pl.BlockSpec(memory_space=pl.ANY)] * len(deps))

def attention_forward_call(joined, cos, sin, gains, segment, deps, dh=128):
    tokens = joined.shape[0]; heads = joined.shape[1] // (3 * dh)
    three, one, rest = attention_specs(tokens, heads, dh, deps)
    return pl.pallas_call(
        functools.partial(forward_kernel, dh), grid=(heads,), in_specs=[three] + rest, out_specs=one,
        out_shape=jax.ShapeDtypeStruct((tokens, heads * dh), BF16),
        compiler_params=pltpu.CompilerParams(vmem_limit_bytes=40 * 2**20),
        cost_estimate=QUICK,
    )(joined, cos, sin, gains, segment[:, None], segment[None, :], *deps)

def attention_backward_call(joined, grad, cos, sin, gains, segment, deps, dh=128):
    tokens = joined.shape[0]; heads = joined.shape[1] // (3 * dh)
    three, one, rest = attention_specs(tokens, heads, dh, deps)
    return pl.pallas_call(
        functools.partial(backward_kernel, dh), grid=(heads,), in_specs=[three, one] + rest,
        out_specs=[three, pl.BlockSpec((2, dh), lambda h: (0, 0))],
        out_shape=[jax.ShapeDtypeStruct(joined.shape, BF16), jax.ShapeDtypeStruct((2, dh), F32)],
        compiler_params=pltpu.CompilerParams(vmem_limit_bytes=40 * 2**20),
        cost_estimate=QUICK,
    )(joined, grad, cos, sin, gains, segment[:, None], segment[None, :], *deps)


def swap(value, axis, bit):
    return lax.ppermute(value, axis, [(i, i ^ bit) for i in range(lax.axis_size(axis))])


MIDDLE = [(1, 2), (2, 1)]
OUTWARD = [(1, 0), (2, 3)]
INWARD = [(0, 1), (3, 2)]


def scatter_ctx_steps(terms, result):
    (beside,) = yield [swap(terms[2:], "ctx", 1)]
    far = (terms[1].astype(F32) + beside[1].astype(F32)).astype(BF16)
    (across,) = yield [swap(far, "ctx", 2)]
    result.append(terms[0].astype(F32) + beside[0].astype(F32) + across.astype(F32))
    yield from idle()


def gather_ctx_steps(own, blocks):
    across, beside = yield [swap(own, "ctx", 2), swap(own, "ctx", 1)]
    (corner,) = yield [swap(across, "ctx", 1)]
    blocks += [own, across, beside, corner]
    yield from idle()


def line_steps(own, slots, across_dp=None, pause=0):
    place = lax.axis_index("expert")
    middle = (place == 1) | (place == 2)

    def over(block):
        return [] if across_dp is None else [swap(block, "dp", 1)]

    pair, third_mid, *x0 = yield [
        swap(own, "expert", 1),
        lax.ppermute(own, "expert", MIDDLE),
    ] + over(own)
    for _ in range(pause):
        yield []
    second_mid, second_end, *x1 = yield [
        lax.ppermute(pair, "expert", MIDDLE),
        lax.ppermute(third_mid, "expert", OUTWARD),
    ] + over(pair)
    second = jnp.where(middle, second_mid, second_end)
    third_end, *x2 = yield [lax.ppermute(second_mid, "expert", OUTWARD)] + over(second)
    third = jnp.where(middle, third_mid, third_end)
    slots += [own, pair, second, third]
    if across_dp is not None:
        (x3,) = yield over(third)
        across_dp += [x0[0], x1[0], x2[0], x3]
    yield from idle()


def unline_steps(slots, result):
    (three,) = yield [lax.ppermute(slots[3], "expert", INWARD)]
    second = (slots[2].astype(F32) + three.astype(F32)).astype(BF16)
    over, inward = yield [
        lax.ppermute(second, "expert", MIDDLE),
        lax.ppermute(second, "expert", INWARD),
    ]
    first = (slots[1].astype(F32) + over.astype(F32)).astype(BF16)
    third = (slots[3].astype(F32) + inward.astype(F32)).astype(BF16)
    home, pair = yield [lax.ppermute(third, "expert", MIDDLE), swap(first, "expert", 1)]
    result.append(slots[0].astype(F32) + pair.astype(F32) + home.astype(F32))
    yield from idle()


def undp_steps(here, there, result):
    moving = {s: swap(there[s], "dp", 1) for s in (3, 2)}
    (x3,) = yield [moving[3]]
    sum3 = here[3].astype(F32) + x3.astype(F32)
    moving[1] = swap(there[1], "dp", 1)
    x2, three = yield [moving[2], lax.ppermute(sum3.astype(BF16), "expert", INWARD)]
    second = (here[2].astype(F32) + x2.astype(F32) + three.astype(F32)).astype(BF16)
    moving[0] = swap(there[0], "dp", 1)
    x1, over, inward = yield [
        moving[1],
        lax.ppermute(second, "expert", MIDDLE),
        lax.ppermute(second, "expert", INWARD),
    ]
    first = (here[1].astype(F32) + x1.astype(F32) + over.astype(F32)).astype(BF16)
    third = (sum3 + inward.astype(F32)).astype(BF16)
    x0, home, pair = yield [
        moving[0],
        lax.ppermute(third, "expert", MIDDLE),
        swap(first, "expert", 1),
    ]
    result.append(
        here[0].astype(F32) + x0.astype(F32) + pair.astype(F32) + home.astype(F32)
    )
    yield from idle()


def gather_steps(own, groups, plan):
    place = lax.axis_index("expert")
    middle = (place == 1) | (place == 2)
    blocks = [own]
    crossed = [None] * 4

    def across(step):
        return {s: swap(blocks[s], "ctx", 2) for s in range(len(blocks)) if plan[s] == step}

    def note(moving, values):
        for s, value in zip(moving, values):
            crossed[s] = value

    moving = across(0)
    pair, third_mid, *rest = yield [
        swap(own, "expert", 1),
        lax.ppermute(own, "expert", MIDDLE),
    ] + list(moving.values())
    note(moving, rest)
    blocks.append(pair)
    moving = across(1)
    second_mid, second_end, *rest = yield [
        lax.ppermute(pair, "expert", MIDDLE),
        lax.ppermute(third_mid, "expert", OUTWARD),
    ] + list(moving.values())
    note(moving, rest)
    blocks.append(jnp.where(middle, second_mid, second_end))
    moving = across(2)
    third_end, *rest = yield [lax.ppermute(second_mid, "expert", OUTWARD)] + list(moving.values())
    note(moving, rest)
    blocks.append(jnp.where(middle, third_mid, third_end))
    groups[0] = jnp.stack(blocks)
    if plan == (3, 3, 3, 3):
        moving = swap(groups[0], "ctx", 2)
        (groups[1],) = yield [swap(groups[0], "ctx", 1)]
        (groups[2],) = yield [moving]
    else:
        moving = across(3)
        groups[1], *rest = yield [swap(groups[0], "ctx", 1)] + list(moving.values())
        note(moving, rest)
        groups[2] = jnp.stack(crossed)
    (groups[3],) = yield [swap(groups[2], "ctx", 1)]
    yield from idle()


def early_gather_steps(own, groups):
    place = lax.axis_index("expert")
    middle = (place == 1) | (place == 2)
    pair, third_mid, own = yield [
        swap(own, "expert", 1),
        lax.ppermute(own, "expert", MIDDLE),
        own,
    ]
    (y0,) = yield [swap(own, "ctx", 2)]
    (y1,) = yield [swap(pair, "ctx", 2)]
    second_mid, second_end = yield [
        lax.ppermute(pair, "expert", MIDDLE),
        lax.ppermute(third_mid, "expert", OUTWARD),
    ]
    second = jnp.where(middle, second_mid, second_end)
    (third_end,) = yield [lax.ppermute(second_mid, "expert", OUTWARD)]
    (y2,) = yield [swap(second, "ctx", 2)]
    third = jnp.where(middle, third_mid, third_end)
    groups[0] = jnp.stack([own, pair, second, third])
    y3, groups[1] = yield [swap(third, "ctx", 2), swap(groups[0], "ctx", 1)]
    groups[2] = jnp.stack([y0, y1, y2, y3])
    (groups[3],) = yield [swap(groups[2], "ctx", 1)]
    yield from idle()


def scatter_steps(groups, result, slow=False):
    def slot(values, s):
        return values[..., s, :, :]

    (far,) = yield [swap(groups[3], "ctx", 1)]
    over_y = (groups[2].astype(F32) + far.astype(F32)).astype(BF16)

    def across(s, count=1):
        return [swap(over_y[..., s : s + count, :, :], "ctx", 2)]

    def total(s, moved):
        return slot(groups[0], s).astype(F32) + slot(near, s).astype(F32) + moved.astype(F32)

    def inwards(sum3):
        return lax.ppermute(sum3.astype(BF16), "expert", INWARD)

    if slow:
        y3, near = yield across(3) + [swap(groups[1], "ctx", 1)]
        y3 = slot(y3, 0)
        sum3 = total(3, y3)
        y2, three = yield across(2) + [inwards(sum3)]
        y2 = slot(y2, 0)
        (y1,) = yield across(1)
        y1 = slot(y1, 0)
        moving = across(0)
    else:
        (far_pair,) = yield across(2, 2)
        near_pair, near = yield across(0, 2) + [swap(groups[1], "ctx", 1)]
        y3, y2, y1, y0 = slot(far_pair, 1), slot(far_pair, 0), slot(near_pair, 1), slot(near_pair, 0)
        sum3 = total(3, y3)
        (three,) = yield [inwards(sum3)]
        moving = []
    second = (total(2, y2) + three.astype(F32)).astype(BF16)
    over, inward, *rest = yield [
        lax.ppermute(second, "expert", MIDDLE),
        lax.ppermute(second, "expert", INWARD),
    ] + moving
    y0 = slot(rest[0], 0) if rest else y0
    first = (total(1, y1) + over.astype(F32)).astype(BF16)
    third = (sum3 + inward.astype(F32)).astype(BF16)
    home, pair = yield [lax.ppermute(third, "expert", MIDDLE), swap(first, "expert", 1)]
    result.append(total(0, y0) + pair.astype(F32) + home.astype(F32))
    yield from idle()


def places(index, lengths, block_order):
    blocks = jnp.arange(block_order.shape[0], dtype=jnp.int32)
    holder = (index // BLOCK)[:, None] == blocks[None, :]
    logical = (
        jnp.sum(jnp.where(holder, block_order[None, :], 0), axis=1) * BLOCK + index % BLOCK
    )
    seq_ends = jnp.cumsum(lengths)
    segment = jnp.sum((logical[:, None] >= seq_ends[None, :]).astype(jnp.int32), axis=1)
    starts = seq_ends - lengths
    member = segment[:, None] == jnp.arange(lengths.shape[0], dtype=jnp.int32)[None, :]
    seq_first = jnp.sum(jnp.where(member, starts[None, :], 0), axis=1)
    return (segment, (logical - seq_first).astype(F32))


def rotary_tables(positions, half_size):
    frequency = THETA_BASE ** (-(jnp.arange(half_size, dtype=F32) / half_size))
    angles = positions[:, None] * frequency[None, :]
    cosine, sine = jnp.cos(angles), jnp.sin(angles)
    return jnp.concatenate([cosine, cosine], axis=1), jnp.concatenate([-sine, sine], axis=1)


def norm_back(upstream, unit_rows, scaling, gain_vector):
    weighted = upstream * gain_vector
    return scaling * (weighted - unit_rows * jnp.mean(weighted * unit_rows, axis=-1, keepdims=True))


def row_scale(rows):
    return lax.rsqrt(jnp.mean(rows * rows, axis=-1, keepdims=True) + EPSILON)


def whole_heads(rows, share):
    return lax.axis_size("dp") == HALVES and rows * lax.axis_size("expert") == share


def assemble(pieces, shape):
    d, z = lax.axis_index("dp"), lax.axis_index("expert")
    whole = jnp.zeros(shape, BF16)
    for dx, line in enumerate(pieces):
        for s, piece in enumerate(line):
            whole = lax.dynamic_update_slice(
                whole, piece[None, :, None], (d ^ dx if shape[0] > 1 else 0, 0, z ^ s) + (0,) * (len(shape) - 3)
            )
    return whole


def piece_of(whole, dx, s):
    first = lax.axis_index("dp") ^ dx if whole.shape[0] > 1 else 0
    start = (first, 0, lax.axis_index("expert") ^ s) + (0,) * (whole.ndim - 3)
    return lax.dynamic_slice(whole, start, (1, whole.shape[1], 1) + whole.shape[3:])[0, :, 0]


def sum_rows(whole):
    return lax.psum_scatter(whole, "dp", scatter_dimension=0, tiled=True)


def pack_weights(query_weight, key_weight, value_weight, attention_gain, mixture_gain, query_key_gain, router):
    rows, width = query_weight.shape
    ctx_size = lax.axis_size("ctx")
    share = width // (HALVES * ctx_size)
    stacked = jnp.stack([query_weight, key_weight, value_weight], axis=1)
    stacked = stacked.reshape(rows, 3, HALVES, ctx_size, share // DH, DH)
    stacked = stacked.transpose(3, 0, 2, 4, 1, 5).reshape(ctx_size, rows, 3 * HALVES * share)
    small = jnp.concatenate(
        [
            attention_gain[:, None],
            mixture_gain[:, None],
            jnp.pad(query_key_gain, (0, rows - query_key_gain.shape[0]))[:, None],
            router,
        ],
        axis=1,
    )
    small = jnp.pad(small, ((0, 0), (0, SMALL - small.shape[1])))
    return jnp.concatenate(
        [stacked, jnp.broadcast_to(small[None], (ctx_size, rows, SMALL))], axis=2
    )


def chosen_gates(normed, router, chosen):
    logits = jnp.where(chosen, dot(normed, router), NEGATIVE)
    powers = jnp.where(chosen, jnp.exp(logits - jnp.max(logits, axis=1, keepdims=True)), 0.0)
    return powers / jnp.sum(powers, axis=1, keepdims=True)


def with_gates(normed, gates):
    flat = gates.T.reshape(1, -1)
    high = flat.astype(BF16).astype(F32)
    low = (flat - high).astype(BF16).astype(F32)
    row = lax.broadcasted_iota(jnp.int32, (TAIL, flat.shape[1]), 0)
    tail = jnp.where(row == 0, high, jnp.where(row == 1, low, jnp.where(row == 2, flat - high - low, 0.0)))
    return jnp.concatenate([normed, tail.astype(BF16)])


def body(
    inputs,
    cotangent,
    lengths,
    block_order,
    routes,
    query_weight,
    key_weight,
    value_weight,
    output_weight,
    attention_gain,
    mixture_gain,
    query_key_gain,
    router,
    expert_gate,
    expert_up,
    expert_down,
):
    micro_count, _, tokens, width = inputs.shape
    top = routes.shape[3]
    expert_count = router.shape[1]
    most = tokens * top * 9 // (8 * expert_count) + 2
    capacity = -(-most // 16) * 16
    place = lax.axis_index("ctx")
    rows, few = query_weight.shape[0], query_key_gain.shape[0]
    micros = range(micro_count)

    line = lax.axis_index("expert")
    dp_size = lax.axis_size("dp")
    two = dp_size == 2
    share = width // (HALVES * 4)
    per_ctx = HALVES * share

    slots, slots_dp, blocks = [], [] if two else None, []
    heads_here = whole_heads(rows, share)
    upstream_groups = [None] * 4
    upstream_flow = Flow(early_gather_steps(
            copy_after(cotangent.reshape(-1, width)).reshape(-1, tokens, width), upstream_groups
        ))
    payload = pack_weights(
        query_weight, key_weight, value_weight, attention_gain, mixture_gain, query_key_gain, router
    )
    payload = lax.all_to_all(payload, "ctx", split_axis=0, concat_axis=0, tiled=True)
    if heads_here:
        chunks = output_weight.reshape(rows, 4, width // 4).transpose(1, 0, 2)
        payload = jnp.concatenate([payload, chunks], axis=2)
    spread = Flow(line_steps(payload, slots, slots_dp))
    stream_flow = Flow(
        gather_ctx_steps(copy_after(inputs.reshape(-1, width), payload).reshape(-1, tokens, width), blocks)
    )
    token = turn([spread, upstream_flow])
    token = turn([spread, stream_flow, upstream_flow])
    token = turn([spread, stream_flow, upstream_flow], token)
    copies = [copy_after(own[0], token) for own in (expert_gate, expert_up, expert_down)]
    token = turn([spread, upstream_flow], token, *copies)
    up_moved = [swap(copies[1], "dp", 1)] if two else []
    experts = [
        [lax.all_gather(own, "dp", axis=0, tiled=True)] for own in (copies[::2] if two else copies)
    ]
    shape = (dp_size, 4, 4) + payload.shape[1:]
    if two:
        packed = assemble([slots, slots_dp], shape)
    else:
        packed = lax.all_gather(
            assemble([slots], (1,) + shape[1:])[0], "dp", axis=0, tiled=False
        )
    if heads_here:
        out_rows = packed[..., 3 * per_ctx + SMALL :].transpose(0, 2, 3, 1, 4).reshape(per_ctx, width)
    packed = packed.reshape(width, -1)
    projections = packed[:, : 3 * per_ctx]
    small = packed[:, 3 * per_ctx : 3 * per_ctx + SMALL].astype(F32)
    gain_one, gain_two = small[:, 0], small[:, 1]
    gain_pair = small[:, 2].reshape(-1, rows)[:, :few].reshape(2, DH)
    router_all = packed[:, 3 * per_ctx + 3 : 3 * per_ctx + 3 + expert_count]

    index = jnp.concatenate(
        [(place ^ s) * tokens + jnp.arange(tokens, dtype=jnp.int32) for s in (0, 2, 1, 3)]
    )
    tables = []
    for m in micros:
        segment, position = places(index, lengths[m, 0], block_order[m, 0])
        tables.append(rotary_tables(position, DH // 2) + (gain_pair, segment))
    stream_all = jnp.concatenate(blocks, axis=1)

    normed_one, units, joined_list, attended_list = [], [], [], []

    def attention(m, token, flows):
        stream = stream_all[m].astype(F32)
        unit = stream * row_scale(stream)
        normed = (unit * gain_one).astype(BF16)
        joined = dot(normed, projections)
        if flows:
            token, (joined,) = turn(flows, token, values=[joined])
        attended = attention_forward_call(joined, *tables[m], [token])
        normed_one.append(normed)
        units.append(unit)
        joined_list.append(joined)
        attended_list.append(attended)
        return attended

    def out_terms_of(m):
        return dot(attended_list[m], out_rows).astype(BF16).reshape(4, tokens, width)

    done = attention(0, token, [])
    if not heads_here:
        out_rows = lax.all_gather(output_weight, ("dp", "ctx", "expert"), axis=0, tiled=True)
        out_rows = out_rows.reshape(HALVES, 4, share, -1)
        out_rows = lax.dynamic_index_in_dim(out_rows, place, 1, keepdims=False)
        out_rows = out_rows.reshape(per_ctx, -1)
    sum_a, sum_b = [], []
    flow_a = Flow(scatter_ctx_steps(out_terms_of(0), sum_a))
    token = turn([flow_a], experts[0][0])
    done = attention(1, token, [])
    token = turn([flow_a, upstream_flow], done)
    flow_b = Flow(scatter_ctx_steps(out_terms_of(1), sum_b))

    normed_two, unit_two, scale_two, gates_own, residuals = [], [], [], [], []

    def route(m, attention_sum):
        residual = inputs[m, 0].astype(F32) + attention_sum
        scale = row_scale(residual)
        unit = residual * scale
        normed = (unit * gain_two).astype(BF16)
        chosen = jnp.any(
            routes[m, 0][..., None] == jnp.arange(expert_count, dtype=jnp.int32), axis=1
        )
        gates = chosen_gates(normed, router_all, chosen)
        residuals.append(residual)
        normed_two.append(normed)
        unit_two.append(unit)
        scale_two.append(scale)
        gates_own.append(gates)
        return with_gates(normed, gates)

    groups = [[None] * 4 for _ in micros]
    gather_a = Flow(gather_steps(route(0, sum_a[0]), groups[0], (3, 3, 3, 3)))
    token, up_moved = turn([flow_b, gather_a, upstream_flow], values=up_moved + [token])
    if two:
        experts.insert(1, [expert_up[0], up_moved[0]])
    token = turn([gather_a])
    token = turn([gather_a, upstream_flow, flow_b], experts[0][0], experts[2][0])
    second_payload = route(1, sum_b[0])
    gather_b = Flow(gather_steps(second_payload, groups[1], (2, 2, 3, 3)))

    shared, kept, calls = [None] * 4, None, 0
    back = [[None] * 4 for _ in micros]
    expert_index = place * 4 + line
    order = jnp.stack([expert_index, expert_index * tokens // 512, lax.axis_index("dp")])
    order = order.astype(jnp.int32)

    def expert(m, k, token, flows):
        nonlocal kept, calls
        shared[k], back[m][k], kept = expert_call(
            order, groups[m][k], upstream_groups[k], tokens, experts, kept, calls, 8, (m, shared[k]), capacity, [token]
        )
        calls += 1
        token, met = turn(flows, values=[shared[k], back[m][k], *kept])
        shared[k], back[m][k], kept = met[0], met[1], met[2:]
        return token

    token = expert(0, 0, token, [gather_a, upstream_flow, gather_b])
    token = expert(0, 1, token, [gather_a, gather_b])
    token = expert(0, 2, token, [gather_a, gather_b])
    token = expert(0, 3, token, [gather_b])
    down_a, down_b, out_sum = [], [], []
    scatter_a = Flow(scatter_steps(back[0], down_a))
    token = expert(1, 2, token, [gather_b, scatter_a])
    token = expert(1, 3, token, [scatter_a])
    scatter_b = Flow(scatter_steps(back[1], down_b))
    token = expert(1, 1, token, [scatter_a, scatter_b])
    token = expert(1, 0, token, [scatter_a, scatter_b])
    rows_in, out_grad, hidden, gate_pre_grad, up_pre_grad = kept
    out_flow = Flow(scatter_steps(shared, out_sum, True))
    down_whole = product_call(hidden, out_grad, [token])
    token, (down_whole,) = turn([scatter_a, scatter_b, out_flow], values=[down_whole])
    down_sum = sum_rows(down_whole)
    gate_whole = product_call(rows_in, gate_pre_grad, [token])
    token, (gate_whole,) = turn([scatter_a, scatter_b, out_flow], values=[gate_whole])

    gate_sum = sum_rows(gate_whole)
    residual_grads, normed_grads, logit_grads = [], [], []

    def residual_back(m, summed):
        gates = gates_own[m]
        gate_value_grad = jnp.sum(summed[tokens:], axis=0).reshape(expert_count, tokens).T
        select_grad = gates * (
            gate_value_grad - jnp.sum(gates * gate_value_grad, axis=1, keepdims=True)
        )
        logit_grad = select_grad.astype(BF16)
        normed_grad = summed[:tokens] + dot_t(logit_grad, router_all)
        residual_grad = cotangent[m, 0].astype(F32) + norm_back(
            normed_grad, unit_two[m], scale_two[m], gain_two
        )
        residual_grads.append(residual_grad)
        normed_grads.append(normed_grad)
        logit_grads.append(logit_grad)
        return residual_grad.astype(BF16)

    branch = [[], []]
    branch_a = Flow(gather_ctx_steps(residual_back(0, down_a[0]), branch[0]))
    up_whole = product_call(rows_in, up_pre_grad, [token])
    token, (up_whole,) = turn([branch_a, scatter_b, out_flow], values=[up_whole])
    up_sum = sum_rows(up_whole)
    token = turn([branch_a])

    joined_grads, normed_one_grads, pair_grads, branch_list = [], [], [], []

    def attention_back(m, token):
        branch_grad = jnp.concatenate(branch[m])
        attended_grad = dot_t(branch_grad, out_rows).astype(BF16)
        joined_grad, pair_part = attention_backward_call(
            joined_list[m], attended_grad, *tables[m], [token]
        )
        branch_list.append(branch_grad)
        joined_grads.append(joined_grad)
        pair_grads.append(pair_part)
        return pair_part

    done = attention_back(0, token)
    token = turn([scatter_b, out_flow], done, down_sum)
    branch_b = Flow(gather_ctx_steps(residual_back(1, down_b[0]), branch[1]))
    normed_one_grads.append(dot_t(joined_grads[0], projections))
    token = turn([branch_b], normed_one_grads[0])
    token = turn([branch_b])
    out_last_sum = []
    out_last = Flow(idle())
    done = attention_back(1, token)
    if heads_here:
        split = sum(dot_l(left, right) for left, right in zip(attended_list, branch_list))
        split = split.astype(BF16).reshape(2, 1, 4, rows, width)
        out_last = Flow(
            unline_steps(
                [jnp.concatenate([piece_of(split, dx, s) for dx in range(2)]) for s in range(4)],
                out_last_sum,
            )
        )
    token = turn([out_flow, out_last], done, gate_sum)
    normed_one_grads.append(dot_t(joined_grads[1], projections))
    attention_gain_grad = sum(
        jnp.sum(grad * unit, axis=0) for grad, unit in zip(normed_one_grads, units)
    )
    mixture_gain_grad = sum(
        jnp.sum(grad * unit, axis=0) for grad, unit in zip(normed_grads, unit_two)
    )
    router_grad = sum(dot_l(left, right) for left, right in zip(normed_two, logit_grads))
    pair_grad = (pair_grads[0] + pair_grads[1]).reshape(-1, few)
    pair_column = jnp.pad(pair_grad, ((0, 0), (0, rows - few))).reshape(-1)
    small_columns = jnp.concatenate(
        [attention_gain_grad[:, None], mixture_gain_grad[:, None], pair_column[:, None], router_grad], axis=1
    )
    small_columns = jnp.pad(small_columns, ((0, 0), (0, SMALL - small_columns.shape[1])))
    terms = jnp.stack(
        [grad.astype(BF16).reshape(4, tokens, width) for grad in normed_one_grads], axis=1
    )

    def gradient_rows(part, parts, deps):
        product = pair_product_call(
            part, parts, normed_one, joined_grads, small_columns.astype(BF16), [], deps
        )
        return product.reshape(dp_size // parts, 4, 4, rows, -1)

    packed_sum, back_sum = [], []
    if two:
        d = lax.axis_index("dp").astype(jnp.int32)
        there = gradient_rows(1 - d, 2, [token])
        there = [piece_of(there, 0, s) for s in range(4)]
        here = gradient_rows(d, 2, there)
        token, (here,) = turn([out_flow, out_last], values=[here])
        last = Flow(
            undp_steps([piece_of(here, 0, s) for s in range(4)], there, packed_sum)
        )
    else:
        whole = gradient_rows(jnp.zeros((), jnp.int32), 1, [token])
        whole = lax.psum_scatter(whole, "dp", scatter_dimension=0, tiled=True)
        token = turn([out_flow, out_last])
        last = Flow(unline_steps([piece_of(whole, 0, s) for s in range(4)], packed_sum))
    token = turn([last, out_last])
    back_flow = Flow(scatter_ctx_steps(terms, back_sum))
    token = turn([last, back_flow, out_last], up_sum)
    if heads_here:
        own_sum, other_sum = out_last_sum[0]
        out_moved = [swap(other_sum.astype(BF16), "dp", 1)]
    else:
        out_moved = []
    token, (gate_sum, up_sum, down_sum) = turn(
        [last, back_flow], token, values=[value.astype(F32) for value in (gate_sum, up_sum, down_sum)]
    )
    if two:
        token, out_moved = turn([last, back_flow], values=out_moved + [token])
    else:
        token = turn([back_flow], token)
    summed = packed_sum[0]
    columns = 3 * per_ctx + SMALL
    swapped = lax.all_to_all(
        summed[..., :columns].astype(BF16), "ctx", split_axis=0, concat_axis=0, tiled=True
    )
    if heads_here:
        out_rows_sum = own_sum + out_moved[0].astype(F32)
    else:
        out_grad_rows = sum(
            dot_l(left, right) for left, right in zip(attended_list, branch_list)
        ).astype(BF16)
        spread_rows = jnp.zeros((HALVES, 4, share, width), BF16)
        spread_rows = lax.dynamic_update_slice_in_dim(
            spread_rows, out_grad_rows.reshape(HALVES, 1, share, width), place, 1
        )
        out_rows_sum = lax.psum_scatter(
            spread_rows.reshape(-1, width), ("dp", "ctx", "expert"), scatter_dimension=0, tiled=True
        ).astype(F32)
    *gradients, small_sums = unpack_call(swapped)
    outputs = [(residuals[m] + out_sum[0][m]).astype(BF16) for m in micros]
    input_grads = []
    for m in micros:
        stream = inputs[m, 0].astype(F32)
        scale_one = row_scale(stream)
        input_grads.append(
            residual_grads[m] + norm_back(back_sum[0][m], stream * scale_one, scale_one, gain_one)
        )
    return (
        jnp.stack(outputs)[:, None],
        jnp.stack(input_grads)[:, None],
        gradients[0],
        gradients[1],
        gradients[2],
        out_rows_sum,
        small_sums[:, 0],
        small_sums[:, 1],
        small_sums[:few, 2],
        small_sums[:, 3 : 3 + expert_count],
        gate_sum[None],
        up_sum[None],
        down_sum[None],
    )


def solution(mesh):
    tokens_4 = P(None, ("dp", "expert"), "ctx", None)
    group = P(None, ("dp", "expert"), None)
    matrix = P(("dp", "ctx", "expert"), None)
    vector = P(("dp", "ctx", "expert"))
    experts = P(("ctx", "expert"), "dp", None)
    return jax.shard_map(
        body,
        mesh=mesh,
        in_specs=(tokens_4, tokens_4, group, group, tokens_4)
        + (matrix,) * 4
        + (vector,) * 3
        + (matrix,)
        + (experts,) * 3,
        out_specs=(tokens_4, tokens_4)
        + (matrix,) * 4
        + (vector,) * 3
        + (matrix,)
        + (experts,) * 3,
        check_vma=False,
    )
```
